32 devices in a mesh: fsdp: 4 (over y, core), ctx: 4 (over z), tp: 2 (over x).
Axes of the slice: x: 2, y: 2, z: 4, core: 2. Of those that a mesh axis runs over, the one named last changes fastest.
Arguments:
- tokens: bfloat16 [4, 2048, 2560], P('fsdp', 'ctx'), may hold values from -6 to 6
- prefix: int32 [4], P('fsdp'), may hold values from 204 to 1024
- attn_gain: float32 [2560], replicated, may hold values from 0.1 to 1.9
- w_query: bfloat16 [2560, 2560], P('fsdp', 'tp'), may hold values from -0.125 to 0.125
- w_key: bfloat16 [2560, 640], P('fsdp', 'tp'), may hold values from -0.125 to 0.125
- w_value: bfloat16 [2560, 640], P('fsdp', 'tp'), may hold values from -0.125 to 0.125
- w_out: bfloat16 [2560, 2560], P('tp', 'fsdp'), may hold values from -2 to 2
- mlp_gain: float32 [2560], replicated, may hold values from 0.1 to 1.9
- w_gate: bfloat16 [2560, 7168], P('fsdp', 'tp'), may hold values from -0.125 to 0.125
- w_up: bfloat16 [2560, 7168], P('fsdp', 'tp'), may hold values from -0.125 to 0.125
- w_down: bfloat16 [7168, 2560], P('tp', 'fsdp'), may hold values from -0.0625 to 0.0625
- cotangent: bfloat16 [4, 2048, 2560], P('fsdp', 'ctx'), may hold values from -6 to 6
Outputs:
- layer_out: bfloat16 [4, 2048, 2560], P('fsdp', 'ctx')
- input_grad: float32 [4, 2048, 2560], P('fsdp', 'ctx')
- attn_gain_grad: float32 [2560], P(('fsdp', 'ctx'))
- query_grad: float32 [2560, 2560], P(('fsdp', 'ctx'), 'tp')
- key_grad: float32 [2560, 640], P(('fsdp', 'ctx'), 'tp')
- value_grad: float32 [2560, 640], P(('fsdp', 'ctx'), 'tp')
- out_grad: float32 [2560, 2560], P('tp', ('fsdp', 'ctx'))
- mlp_gain_grad: float32 [2560], P(('fsdp', 'ctx'))
- gate_grad: float32 [2560, 7168], P(('fsdp', 'ctx'), 'tp')
- up_grad: float32 [2560, 7168], P(('fsdp', 'ctx'), 'tp')
- down_grad: float32 [7168, 2560], P('tp', ('fsdp', 'ctx'))
The draws below stay inside these ranges and needn't reach their ends.
All inputs are finite; a program needn't handle non-finite values.
Results may differ from the reference program's by a relative error of at most 0.022.
Values may be sent and summed in bfloat16 or wider, within the bound.
A program may use at most 256 MiB of HBM per device.

```python
import math
import jax
import jax.numpy as jnp
from jax import lax

D = 2560
H = 32
KVH = 8
HD = 80
FF = 7168
LEN = 2048
SEQS = 4


def set_ends(entries, own_key, least, high):
    extent = entries.shape
    spot = [jax.random.randint(jax.random.fold_in(own_key, axis), (), 0, extent[axis]) for axis in range(len(extent))]
    entries = entries.at[tuple(spot)].set(least)
    longest = extent.index(max(extent))
    spot[longest] = (spot[longest] + 1) % extent[longest]
    return entries.at[tuple(spot)].set(high)


def strengthened(values, rng, source, target, parts, factor):
    def block_of(position):
        return (jnp.arange(values.shape[position]) // (values.shape[position] // parts)).reshape((-1,) + (1,) * (values.ndim - 1 - position))

    one_side = jax.random.permutation(rng, parts)[block_of(target)]
    other_side = (block_of(target) + parts // 2) % parts
    return jnp.where((block_of(source) == one_side) | (block_of(source) == other_side), factor * values, values)


def shard_levels(key, extent, shards, smallest, high):
    factor_of, own = 1.0, jax.random.fold_in(key, 6)
    for axis_at, blocks in shards:
        draws = jnp.exp(jax.random.uniform(jax.random.fold_in(own, axis_at), (blocks,), jnp.float32, smallest / len(shards), high / len(shards)))
        factor_of = factor_of * jnp.repeat(draws, extent[axis_at] // blocks).reshape([-1 if axis == axis_at else 1 for axis in range(len(extent))])
    return factor_of


def gaussian(own_key, dims, deviation, most, cuts=(), held_as=jnp.bfloat16):
    values = jax.random.normal(own_key, dims, jnp.float32) * deviation
    if len(cuts) > 0:
        values = shard_levels(own_key, dims, cuts, -0.22, 0.18) * values
    return jnp.clip(values, min=-most, max=most).astype(held_as)


def gaussian_with(key, shape, deviation, reach, split, heavy, kind=jnp.bfloat16):
    result = deviation * jax.random.normal(key, shape, jnp.float32)
    if split:
        result = result * shard_levels(key, shape, split, -0.22, 0.18)
    return jnp.clip(strengthened(result, jax.random.fold_in(key, 3), *heavy), -reach, reach).astype(kind)


def setup_inputs(seed: int = 0) -> dict:
    arg_keys = jax.random.split(jax.random.key(seed), 13)
    return {
        "tokens": gaussian(arg_keys[0], (SEQS, LEN, D), 1.0, 6.0, ((0, 4), (1, 4))),
        "prefix": set_ends(jax.random.randint(arg_keys[1], (SEQS,), LEN // 10, LEN // 2 + 1), jax.random.fold_in(arg_keys[1], 1), LEN // 10, (LEN // 2 + 1) - 1).astype(jnp.int32),
        "attn_gain": jnp.clip(1.0 + 0.18 * jax.random.normal(arg_keys[2], (D,), jnp.float32), 0.1, 1.9),
        "w_query": gaussian(arg_keys[3], (D, H * HD), D ** -0.5, 0.125, ((0, 4), (1, 2))),
        "w_key": gaussian(arg_keys[4], (D, KVH * HD), D ** -0.5, 0.125, ((0, 4), (1, 2))),
        "w_value": gaussian(arg_keys[5], (D, KVH * HD), D ** -0.5, 0.125, ((0, 4), (1, 2))),
        "w_out": gaussian(arg_keys[6], (H * HD, D), (max(4, 8 * H * HD // LEN)) ** -0.5, 2.0, ((0, 2), (1, 4))),
        "mlp_gain": jnp.clip(1.0 + 0.18 * jax.random.normal(arg_keys[7], (D,), jnp.float32), 0.1, 1.9),
        "w_gate": gaussian(arg_keys[8], (D, FF), D ** -0.5, 0.125, ((0, 4), (1, 2))),
        "w_up": gaussian(arg_keys[9], (D, FF), D ** -0.5, 0.125, ((0, 4), (1, 2))),
        "w_down": gaussian(arg_keys[10], (FF, D), FF ** -0.5, 0.0625, ((0, 2), (1, 4))),
        "cotangent": gaussian_with(arg_keys[11], (SEQS, LEN, D), 1.0, 6.0, ((0, 4), (1, 4)), (1, 2, 4, 2.0)),
    }


EPS = 1e-05
THETA = 1000000.0
MASKED = -1e+30
HIGHEST = lax.Precision.HIGHEST

@jax.custom_vjp
def low(v):
    return lax.optimization_barrier(v.astype(jnp.bfloat16)).astype(jnp.float32)

@jax.custom_vjp
def low_back(v):
    return v

def low_keep(v):
    return (low(v), None)

def low_pass(kept, grad):
    return (grad,)

def back_keep(v):
    return (v, None)

def back_low(kept, grad):
    return (low(grad),)
low.defvjp(low_keep, low_pass)
low_back.defvjp(back_keep, back_low)

def product(left_matrix, right_matrix):
    return jnp.dot(left_matrix, right_matrix, precision=HIGHEST, preferred_element_type=jnp.float32)

def rms_scale(values, gain_vec):
    return values * lax.rsqrt(lax.optimization_barrier(jnp.mean(values * values, axis=-1, keepdims=True)) + EPS) * gain_vec

def rope_tables(positions, head_dim):
    half_dim = head_dim // 2
    frequency = THETA ** (-(jnp.arange(half_dim, dtype=jnp.float32) * 2.0) / head_dim)
    angles = positions.astype(jnp.float32)[:, None] * frequency[None, :]
    angles = jnp.concatenate([angles, angles], axis=1)
    return (jnp.cos(angles), jnp.sin(angles))

def turn_half(values):
    half_dim = values.shape[-1] // 2
    return jnp.concatenate([-values[..., half_dim:], values[..., :half_dim]], axis=-1)

def rotate(values, cos_table, sin_table):
    return values * cos_table[:, None, :] + turn_half(values) * sin_table[:, None, :]

def attend_group(pieces, allowed):
    query_part, key_part, value_part = pieces
    scores = jnp.einsum('gqrd,gkd->grqk', query_part, key_part, precision=HIGHEST, preferred_element_type=jnp.float32) * HD ** (-0.5)
    scores = jnp.where(allowed[:, None], low_back(scores), MASKED)
    top_score = lax.optimization_barrier(jnp.max(scores, axis=-1, keepdims=True))
    weights = jnp.exp(scores - top_score)
    probs = weights / lax.optimization_barrier(jnp.sum(weights, axis=-1, keepdims=True))
    return jnp.einsum('grqk,gkd->gqrd', low(probs), value_part, precision=HIGHEST, preferred_element_type=jnp.float32)

def layer(tokens, attn_gain, w_query, w_key, w_value, w_out, mlp_gain, w_gate, w_up, w_down, prefix):
    group_size = tokens.shape[0]
    length = tokens.shape[1]
    per_group = H // KVH
    positions = jnp.arange(length, dtype=jnp.int32)
    cos_table, sin_table = rope_tables(positions, HD)
    normed_one = low(rms_scale(tokens, attn_gain))
    query_proj = low_back(product(normed_one, w_query)).reshape(group_size, length, H, HD)
    key_proj = low_back(product(normed_one, w_key)).reshape(group_size, length, KVH, HD)
    value_proj = low_back(product(normed_one, w_value)).reshape(group_size, length, KVH, HD)
    queries = low(rotate(query_proj, cos_table, sin_table))
    keys = low(rotate(key_proj, cos_table, sin_table))
    values = low(value_proj)
    allowed = (positions[None, None, :] <= positions[None, :, None]) | (positions[None, None, :] < prefix[:, None, None])
    query_groups = queries.reshape(group_size, length, KVH, per_group, HD).transpose(2, 0, 1, 3, 4)
    key_groups = keys.transpose(2, 0, 1, 3)
    value_groups = values.transpose(2, 0, 1, 3)

    def one_group(pieces):
        return attend_group(pieces, allowed)
    attended = lax.map(jax.checkpoint(one_group), (query_groups, key_groups, value_groups))
    attended = attended.transpose(1, 2, 0, 3, 4).reshape(group_size, length, H * HD)
    heads_out = low_back(low(attended))
    middle = tokens + low_back(product(heads_out, w_out))
    normed_two = low(rms_scale(middle, mlp_gain))
    gate_proj = low_back(product(normed_two, w_gate))
    up_proj = low_back(product(normed_two, w_up))
    hidden = low(jax.nn.silu(gate_proj) * up_proj)
    return middle + product(hidden, w_down)

def reference(tokens, prefix, attn_gain, w_query, w_key, w_value, w_out, mlp_gain, w_gate, w_up, w_down, cotangent):
    params = tuple((weight.astype(jnp.float32) for weight in (attn_gain, w_query, w_key, w_value, w_out, mlp_gain, w_gate, w_up, w_down)))
    group_size = math.gcd(SEQS, max(1, 4096 // LEN))
    group_count = SEQS // group_size
    token_groups = tokens.astype(jnp.float32).reshape(group_count, group_size, LEN, D)
    grad_groups = cotangent.astype(jnp.float32).reshape(group_count, group_size, LEN, D)
    prefix_groups = prefix.reshape(group_count, group_size)
    empty_sums = tuple((jnp.zeros(weight.shape, jnp.float32) for weight in params))

    def one_step(totals, pieces):
        group_tokens, group_grad, group_prefix = pieces

        def forward(inputs, *weights):
            return layer(inputs, *weights, group_prefix)
        output, pullback = jax.vjp(forward, group_tokens, *params)
        gradients = pullback(group_grad)
        totals = tuple((running + grad_part for running, grad_part in zip(totals, gradients[1:])))
        return (totals, (output.astype(jnp.bfloat16), gradients[0]))
    totals, (outputs, input_grads) = lax.scan(one_step, empty_sums, (token_groups, grad_groups, prefix_groups))
    return (outputs.reshape(SEQS, LEN, D), input_grads.reshape(SEQS, LEN, D), totals[0], totals[1], totals[2], totals[3], totals[4], totals[5], totals[6], totals[7], totals[8])
```

```python
import functools
import math

import jax
import jax.numpy as jnp
from jax import lax
from jax.experimental import pallas as pl
from jax.experimental.pallas import tpu as pltpu
from jax.sharding import PartitionSpec as P

HD = 80
EPS = 1e-05
THETA = 1000000.0
MASKED = -1e30
SCALE = HD ** (-0.5)
SCALE_LOG2 = SCALE * math.log2(math.e)
BF16 = jnp.bfloat16
F32 = jnp.float32


def dot(left, right):
    return jnp.dot(left, right, preferred_element_type=F32)


def dot_tn(left, right):
    return lax.dot_general(left, right, (((0,), (0,)), ((), ())), preferred_element_type=F32)


def dot_nt(left, right):
    return lax.dot_general(left, right, (((1,), (1,)), ((), ())), preferred_element_type=F32)


def rope_tables(full_len):
    half = HD // 2
    frequency = THETA ** (-(jnp.arange(half, dtype=F32) * 2.0) / HD)
    angles = jnp.arange(full_len, dtype=jnp.int32).astype(F32)[:, None] * frequency[None, :]
    cos, sin = jnp.cos(angles), jnp.sin(angles)
    return jnp.concatenate([cos, cos], axis=1), jnp.concatenate([-sin, sin], axis=1)


def swap_halves(values):
    half = HD // 2
    return jnp.concatenate([values[:, half:], values[:, :half]], axis=1)


def rotate(values, cos, sin):
    values = values.astype(F32)
    return values * cos + swap_halves(values) * sin


def rotate_back(values, cos, sin):
    return values * cos - swap_halves(values) * sin


def stack_heads(ref, rows, heads):
    return jnp.concatenate([ref[rows, h * HD : (h + 1) * HD] for h in range(heads)], axis=0)


def stack_rotated(ref, rows, heads, cos, sin):
    return jnp.concatenate(
        [rotate(ref[rows, h * HD : (h + 1) * HD], cos, sin).astype(BF16) for h in range(heads)],
        axis=0,
    )


def load_keys(qkv, cos, sin, keys, values, heads, step):
    def body(i, carry):
        rows = pl.ds(pl.multiple_of(i * step, step), step)
        at = heads * HD
        keys[rows, :] = rotate(qkv[rows, at : at + HD], cos[rows, :], sin[rows, :]).astype(BF16)
        values[rows, :] = qkv[rows, at + HD : at + 2 * HD]
        return carry

    lax.fori_loop(0, qkv.shape[0] // step, body, 0)


def key_blocks(i, rows, block, prefix):
    start = i * rows
    clear = lax.div(jnp.maximum(start + 1, prefix), block)
    needed = lax.div(jnp.maximum(start + rows, prefix) + block - 1, block)
    return clear, needed


def attend_kernel(heads, rows, block, prefix_ref, qkv, cos, sin, out, lse, keys, values):
    i = pl.program_id(0)
    prefix = prefix_ref[0]

    @pl.when(i == 0)
    def _():
        load_keys(qkv, cos, sin, keys, values, heads, rows)

    here = pl.ds(pl.multiple_of(i * rows, rows), rows)
    queries = stack_rotated(qkv, here, heads, cos[here, :], sin[here, :])
    stacked = heads * rows
    clear, needed = key_blocks(i, rows, block, prefix)

    def step(j, carry, masked):
        top, total, acc = carry
        there = pl.ds(pl.multiple_of(j * block, block), block)
        scores = dot_nt(queries, keys[there, :])
        if masked:
            key_pos = j * block + lax.broadcasted_iota(jnp.int32, (stacked, block), 1)
            query_pos = i * rows + lax.rem(
                lax.broadcasted_iota(jnp.int32, (stacked, 1), 0), rows
            )
            scores = jnp.where(key_pos < jnp.maximum(query_pos + 1, prefix), scores, MASKED)
        new_top = jnp.maximum(top, jnp.max(scores, axis=1, keepdims=True))
        factor = jnp.exp2((top - new_top) * SCALE_LOG2)
        weights = jnp.exp2(scores * SCALE_LOG2 - new_top * SCALE_LOG2)
        total = total * factor + jnp.sum(weights, axis=1, keepdims=True)
        acc = acc * factor + dot(weights.astype(BF16), values[there, :])
        return new_top, total, acc

    carry = (
        jnp.full((stacked, 1), MASKED, F32),
        jnp.zeros((stacked, 1), F32),
        jnp.zeros((stacked, HD), F32),
    )
    carry = lax.fori_loop(0, clear, functools.partial(step, masked=False), carry)
    top, total, acc = lax.fori_loop(clear, needed, functools.partial(step, masked=True), carry)
    acc = acc / total
    for h in range(heads):
        out[:, h * HD : (h + 1) * HD] = acc[h * rows : (h + 1) * rows].astype(BF16)
    log_sum = top * SCALE_LOG2 + jnp.log2(total)
    lse[0] = jnp.transpose(jnp.broadcast_to(log_sum, (stacked, 128)))[:8]


def attend_back_kernel(
    heads, rows, block, prefix_ref, qkv, grad_out, attended, lse, cos, sin, out, keys, values, grad_keys, grad_values
):
    i = pl.program_id(0)
    prefix = prefix_ref[0]
    at = heads * HD

    @pl.when(i == 0)
    def _():
        load_keys(qkv, cos, sin, keys, values, heads, rows)
        grad_keys[...] = jnp.zeros_like(grad_keys)
        grad_values[...] = jnp.zeros_like(grad_values)

    here = pl.ds(pl.multiple_of(i * rows, rows), rows)
    cos_here, sin_here = cos[here, :], sin[here, :]
    queries = stack_rotated(qkv, here, heads, cos_here, sin_here)
    grads = stack_heads(grad_out, here, heads)
    outs = stack_heads(attended, here, heads)
    stacked = heads * rows
    row_dot = lax.dot_general(
        jnp.ones((8, HD), F32),
        grads.astype(F32) * outs.astype(F32),
        (((1,), (1,)), ((), ())),
        precision=lax.Precision.HIGHEST,
        preferred_element_type=F32,
    )[:1]
    log_sum = lse[0, :1]
    clear, needed = key_blocks(i, rows, block, prefix)

    def step(j, grad_queries, masked):
        there = pl.ds(pl.multiple_of(j * block, block), block)
        key_part = keys[there, :]
        probs = jnp.exp2(dot_nt(key_part, queries) * SCALE_LOG2 - log_sum)
        if masked:
            key_pos = j * block + lax.broadcasted_iota(jnp.int32, (block, stacked), 0)
            query_pos = i * rows + lax.rem(
                lax.broadcasted_iota(jnp.int32, (1, stacked), 1), rows
            )
            probs = jnp.where(key_pos < jnp.maximum(query_pos + 1, prefix), probs, 0.0)
        grad_probs = dot_nt(values[there, :], grads)
        grad_scores = (probs * (grad_probs - row_dot)).astype(BF16)
        grad_values[there, :] += dot(probs.astype(BF16), grads)
        grad_keys[there, :] += dot(grad_scores, queries)
        return grad_queries + dot_tn(grad_scores, key_part)

    grad_queries = jnp.zeros((stacked, HD), F32)
    grad_queries = lax.fori_loop(0, clear, functools.partial(step, masked=False), grad_queries)
    grad_queries = lax.fori_loop(clear, needed, functools.partial(step, masked=True), grad_queries)
    for h in range(heads):
        part = grad_queries[h * rows : (h + 1) * rows] * SCALE
        out[here, h * HD : (h + 1) * HD] = rotate_back(part, cos_here, sin_here).astype(BF16)

    @pl.when(i == pl.num_programs(0) - 1)
    def _():
        def body(k, carry):
            at_rows = pl.ds(pl.multiple_of(k * rows, rows), rows)
            part = grad_keys[at_rows, :] * SCALE
            out[at_rows, at : at + HD] = rotate_back(part, cos[at_rows, :], sin[at_rows, :]).astype(BF16)
            out[at_rows, at + HD : at + 2 * HD] = grad_values[at_rows, :].astype(BF16)
            return carry

        lax.fori_loop(0, qkv.shape[0] // rows, body, 0)


VMEM_LIMIT = 48 * 1024 * 1024


def attention_sizes(full_len):
    return min(256, full_len), min(512, full_len)


def attend(prefix, qkv, cos, sin):
    full_len, width = qkv.shape
    heads = width // HD - 2
    rows, block = attention_sizes(full_len)
    steps = full_len // rows
    whole = lambda shape: pl.BlockSpec(shape, lambda i: (0,) * len(shape))
    return pl.pallas_call(
        functools.partial(attend_kernel, heads, rows, block),
        grid=(steps,),
        in_specs=[
            pl.BlockSpec(memory_space=pltpu.SMEM),
            whole((full_len, width)),
            whole((full_len, HD)),
            whole((full_len, HD)),
        ],
        out_specs=[
            pl.BlockSpec((rows, heads * HD), lambda i: (i, 0)),
            pl.BlockSpec((1, 8, heads * rows), lambda i: (i, 0, 0)),
        ],
        out_shape=[
            jax.ShapeDtypeStruct((full_len, heads * HD), BF16),
            jax.ShapeDtypeStruct((steps, 8, heads * rows), F32),
        ],
        scratch_shapes=[pltpu.VMEM((full_len, HD), BF16)] * 2,
        compiler_params=pltpu.CompilerParams(vmem_limit_bytes=VMEM_LIMIT),
        cost_estimate=pl.CostEstimate(
            flops=heads * full_len * full_len * HD * 8, bytes_accessed=full_len * width * 4, transcendentals=heads * full_len * full_len // 2
        ),
        name="attend",
    )(prefix, qkv, cos, sin)


def attend_back(prefix, qkv, grad_out, attended, lse, cos, sin):
    full_len, width = qkv.shape
    heads = width // HD - 2
    rows, block = attention_sizes(full_len)
    steps = full_len // rows
    whole = lambda shape: pl.BlockSpec(shape, lambda i: (0,) * len(shape))
    return pl.pallas_call(
        functools.partial(attend_back_kernel, heads, rows, block),
        grid=(steps,),
        in_specs=[
            pl.BlockSpec(memory_space=pltpu.SMEM),
            whole((full_len, width)),
            whole((full_len, heads * HD)),
            whole((full_len, heads * HD)),
            pl.BlockSpec((1, 8, heads * rows), lambda i: (i, 0, 0)),
            whole((full_len, HD)),
            whole((full_len, HD)),
        ],
        out_specs=whole((full_len, width)),
        out_shape=jax.ShapeDtypeStruct((full_len, width), BF16),
        scratch_shapes=[pltpu.VMEM((full_len, HD), BF16)] * 2 + [pltpu.VMEM((full_len, HD), F32)] * 2,
        compiler_params=pltpu.CompilerParams(vmem_limit_bytes=VMEM_LIMIT),
        cost_estimate=pl.CostEstimate(
            flops=heads * full_len * full_len * HD * 20, bytes_accessed=full_len * width * 8, transcendentals=heads * full_len * full_len // 2
        ),
        name="attend_back",
    )(prefix, qkv, grad_out, attended, lse, cos, sin)


def normalize(values, gain):
    scale = lax.rsqrt(jnp.mean(values * values, axis=-1, keepdims=True) + EPS)
    return scale, (values * scale * gain).astype(BF16)


def normalize_back(values, scale, gain, grad_normed):
    inner = grad_normed * gain
    mixed = jnp.mean(inner * values, axis=-1, keepdims=True)
    return scale * inner - values * scale**3 * mixed


def owner_sum(partial, groups, context):
    width, columns = partial.shape
    piece = width // (groups * context)
    partial = jnp.swapaxes(partial.reshape(groups, context, piece, columns), 0, 1).reshape(width, columns)
    return lax.psum_scatter(partial, "ctx", scatter_dimension=0, tiled=True).reshape(groups, piece, columns)


def on_device(
    tokens, prefix, attn_gain, w_query, w_key, w_value, w_out, mlp_gain, w_gate, w_up, w_down, cotangent
):
    _, local_len, width = tokens.shape
    groups, context, halves = lax.axis_size("fsdp"), lax.axis_size("ctx"), lax.axis_size("tp")
    own_len = local_len // halves
    full_len = local_len * context
    query_cols = w_query.shape[1]
    kv_heads = w_key.shape[1] // HD
    copies = context // kv_heads
    heads = query_cols // HD // context
    group_cols = (heads + 2) * HD
    hidden_cols = w_gate.shape[1] // groups
    own_start = lax.axis_index("tp") * own_len
    own = lambda values: lax.dynamic_slice_in_dim(values, own_start, own_len, 0)

    parts = []
    for c in range(context):
        kv = c // copies
        parts.append(w_query[:, c * heads * HD : (c + 1) * heads * HD])
        parts.append(w_key[:, kv * HD : (kv + 1) * HD])
        parts.append(w_value[:, kv * HD : (kv + 1) * HD])
    qkv_shard = jnp.concatenate(parts, axis=1)
    qkv_full = lax.all_gather(qkv_shard, "fsdp", axis=0, tiled=True)
    mixer_full = lax.all_gather(w_out, "fsdp", axis=1, tiled=True)
    gate_cols = lax.all_to_all(w_gate, "fsdp", split_axis=1, concat_axis=0, tiled=True)
    up_cols = lax.all_to_all(w_up, "fsdp", split_axis=1, concat_axis=0, tiled=True)
    down_rows = lax.all_to_all(w_down, "fsdp", split_axis=0, concat_axis=1, tiled=True)
    grad_out = cotangent.reshape(local_len, width)
    grad_plane = lax.all_gather(grad_out, "fsdp", axis=0, tiled=True)

    cos, sin = rope_tables(full_len)
    inputs_all = tokens.reshape(local_len, width)
    _, normed_one = normalize(inputs_all.astype(F32), attn_gain)
    inputs = own(inputs_all).astype(F32)
    scale_one = lax.rsqrt(jnp.mean(inputs * inputs, axis=-1, keepdims=True) + EPS)

    proj = dot(normed_one, qkv_full).astype(BF16)
    qkv = lax.all_to_all(proj, "ctx", split_axis=1, concat_axis=0, tiled=True)
    attended, lse = attend(prefix, qkv, cos, sin)
    heads_back = lax.all_to_all(attended, "ctx", split_axis=0, concat_axis=1, tiled=True)
    branch = lax.psum_scatter(dot(heads_back, mixer_full).astype(BF16), "tp", scatter_dimension=0, tiled=True)
    middle = inputs + branch.astype(F32)
    scale_two, normed_two = normalize(middle, mlp_gain)

    normed_plane = lax.all_gather(normed_two, ("fsdp", "tp"), axis=0, tiled=True)
    gate_proj = dot(normed_plane, gate_cols)
    up_proj = dot(normed_plane, up_cols)
    sigmoid_gate = jax.nn.sigmoid(gate_proj)
    hidden = (gate_proj * sigmoid_gate * up_proj).astype(BF16)
    down_part = lax.psum_scatter(
        dot(hidden, down_rows).astype(BF16), ("fsdp", "tp"), scatter_dimension=0, tiled=True
    )
    layer_out = lax.all_gather((middle + down_part.astype(F32)).astype(BF16), "tp", axis=0, tiled=True)

    grad_hidden = dot_nt(grad_plane, down_rows)
    grad_gate = (grad_hidden * up_proj * sigmoid_gate * (1.0 + gate_proj * (1.0 - sigmoid_gate))).astype(BF16)
    grad_up = (grad_hidden * gate_proj * sigmoid_gate).astype(BF16)
    grad_normed_two = lax.psum_scatter(
        (dot_nt(grad_gate, gate_cols) + dot_nt(grad_up, up_cols)).astype(BF16),
        ("fsdp", "tp"),
        scatter_dimension=0,
        tiled=True,
    ).astype(F32)
    grad_middle = own(grad_out).astype(F32) + normalize_back(middle, scale_two, mlp_gain, grad_normed_two)
    branch_low = lax.all_gather(grad_middle.astype(BF16), "tp", axis=0, tiled=True)

    grad_heads = dot_nt(branch_low, mixer_full).astype(BF16)
    grad_attended = lax.all_to_all(grad_heads, "ctx", split_axis=1, concat_axis=0, tiled=True)
    grad_qkv = attend_back(prefix, qkv, grad_attended, attended, lse, cos, sin)
    grad_proj = lax.all_to_all(grad_qkv, "ctx", split_axis=0, concat_axis=1, tiled=True)
    grad_normed_one = lax.psum_scatter(
        dot_nt(grad_proj, qkv_full).astype(BF16), "tp", scatter_dimension=0, tiled=True
    ).astype(F32)
    own_input_grad = grad_middle + normalize_back(inputs, scale_one, attn_gain, grad_normed_one)
    input_grad = lax.all_gather(own_input_grad.astype(BF16), "tp", axis=0, tiled=True).astype(F32)

    def plane_grad(left, right):
        sums = owner_sum(dot_tn(left, right).astype(BF16), groups, context)
        return lax.all_to_all(sums, "fsdp", split_axis=0, concat_axis=0, tiled=True)

    down_grad = plane_grad(grad_plane, hidden).astype(F32)
    down_grad = jnp.transpose(down_grad, (0, 2, 1)).reshape(groups * hidden_cols, -1)
    gate_grad = jnp.transpose(plane_grad(normed_plane, grad_gate), (1, 0, 2)).reshape(-1, groups * hidden_cols)
    up_grad = jnp.transpose(plane_grad(normed_plane, grad_up), (1, 0, 2)).reshape(-1, groups * hidden_cols)
    gate_grad, up_grad = gate_grad.astype(F32), up_grad.astype(F32)

    def token_grad(left, right):
        summed = lax.psum_scatter(dot_tn(left, right).astype(BF16), "fsdp", scatter_dimension=0, tiled=True)
        return lax.psum_scatter(summed, "ctx", scatter_dimension=0, tiled=True).astype(F32)

    out_grad = jnp.transpose(token_grad(branch_low, heads_back))
    qkv_grad = token_grad(normed_one, grad_proj)

    piece = width // (groups * context)
    piece_start = lax.axis_index("ctx") * piece
    rows_of = lambda weight: lax.dynamic_slice_in_dim(weight, piece_start, piece, 0).astype(F32)
    mlp_sum = jnp.sum(rows_of(w_gate) * gate_grad + rows_of(w_up) * up_grad, axis=1)
    attn_sum = jnp.sum(rows_of(qkv_shard) * qkv_grad, axis=1)
    gain_starts = lax.axis_index("fsdp") * (piece * context) + piece_start
    gain_of = lambda gain: lax.dynamic_slice_in_dim(gain, gain_starts, piece, 0)
    sums = lax.psum(jnp.stack([mlp_sum, attn_sum]), "tp")
    mlp_gain_grad = sums[0] / gain_of(mlp_gain)
    attn_gain_grad = sums[1] / gain_of(attn_gain)

    grouped = qkv_grad.reshape(piece, context, group_cols)
    query_grad = grouped[:, :, : heads * HD].reshape(piece, query_cols)
    pairs = grouped[:, :, heads * HD :].reshape(piece, kv_heads, copies, 2 * HD).sum(axis=2)
    key_grad = pairs[:, :, :HD].reshape(piece, kv_heads * HD)
    value_grad = pairs[:, :, HD:].reshape(piece, kv_heads * HD)
    return (
        layer_out.reshape(tokens.shape),
        input_grad.reshape(tokens.shape),
        attn_gain_grad,
        query_grad,
        key_grad,
        value_grad,
        out_grad,
        mlp_gain_grad,
        gate_grad,
        up_grad,
        down_grad,
    )


def solution(mesh):
    rows = P("fsdp", "ctx", None)
    owned = P(("fsdp", "ctx"), "tp")
    owned_t = P("tp", ("fsdp", "ctx"))
    gain = P(("fsdp", "ctx"))
    down, up = P("fsdp", "tp"), P("tp", "fsdp")
    return jax.shard_map(
        on_device,
        mesh=mesh,
        in_specs=(rows, P("fsdp"), P(), down, down, down, up, P(), down, down, up, rows),
        out_specs=(rows, rows, gain, owned, owned, owned, owned_t, gain, owned, owned, owned_t),
        check_vma=False,
    )
```

```python
import functools
import math

import jax
import jax.numpy as jnp
from jax import lax
from jax.experimental import pallas as pl
from jax.experimental.pallas import tpu as pltpu
from jax.sharding import PartitionSpec as P

HD = 80
EPS = 1e-05
THETA = 1000000.0
MASKED = -1e30
SCALE = HD ** (-0.5)
SCALE_LOG2 = SCALE * math.log2(math.e)
BF16 = jnp.bfloat16
F32 = jnp.float32


def dot(left, right):
    return jnp.dot(left, right, preferred_element_type=F32)


def dot_tn(left, right):
    return lax.dot_general(left, right, (((0,), (0,)), ((), ())), preferred_element_type=F32)


def dot_nt(left, right):
    return lax.dot_general(left, right, (((1,), (1,)), ((), ())), preferred_element_type=F32)


def rope_tables(full_len):
    half = HD // 2
    frequency = THETA ** (-(jnp.arange(half, dtype=F32) * 2.0) / HD)
    angles = jnp.arange(full_len, dtype=jnp.int32).astype(F32)[:, None] * frequency[None, :]
    cos, sin = jnp.cos(angles), jnp.sin(angles)
    return jnp.concatenate([cos, cos], axis=1), jnp.concatenate([-sin, sin], axis=1)


def swap_halves(values):
    half = HD // 2
    return jnp.concatenate([values[:, half:], values[:, :half]], axis=1)


def rotate(values, cos, sin):
    values = values.astype(F32)
    return values * cos + swap_halves(values) * sin


def rotate_back(values, cos, sin):
    return values * cos - swap_halves(values) * sin


def stack_heads(ref, rows, heads):
    return jnp.concatenate([ref[rows, h * HD : (h + 1) * HD] for h in range(heads)], axis=0)


def stack_rotated(ref, rows, heads, cos, sin):
    return jnp.concatenate(
        [rotate(ref[rows, h * HD : (h + 1) * HD], cos, sin).astype(BF16) for h in range(heads)],
        axis=0,
    )


def load_keys(qkv, cos, sin, keys, values, heads, step):
    def body(i, carry):
        rows = pl.ds(pl.multiple_of(i * step, step), step)
        at = heads * HD
        keys[rows, :] = rotate(qkv[rows, at : at + HD], cos[rows, :], sin[rows, :]).astype(BF16)
        values[rows, :] = qkv[rows, at + HD : at + 2 * HD]
        return carry

    lax.fori_loop(0, qkv.shape[0] // step, body, 0)


def key_blocks(i, rows, block, prefix):
    start = i * rows
    clear = lax.div(jnp.maximum(start + 1, prefix), block)
    needed = lax.div(jnp.maximum(start + rows, prefix) + block - 1, block)
    return clear, needed


def attend_kernel(heads, rows, block, prefix_ref, qkv, cos, sin, out, lse, keys, values):
    i = pl.program_id(0)
    prefix = prefix_ref[0]

    @pl.when(i == 0)
    def _():
        load_keys(qkv, cos, sin, keys, values, heads, rows)

    here = pl.ds(pl.multiple_of(i * rows, rows), rows)
    queries = stack_rotated(qkv, here, heads, cos[here, :], sin[here, :])
    stacked = heads * rows
    clear, needed = key_blocks(i, rows, block, prefix)

    def step(j, carry, masked):
        top, total, acc = carry
        there = pl.ds(pl.multiple_of(j * block, block), block)
        scores = dot_nt(queries, keys[there, :])
        if masked:
            key_pos = j * block + lax.broadcasted_iota(jnp.int32, (stacked, block), 1)
            query_pos = i * rows + lax.rem(
                lax.broadcasted_iota(jnp.int32, (stacked, 1), 0), rows
            )
            scores = jnp.where(key_pos < jnp.maximum(query_pos + 1, prefix), scores, MASKED)
        new_top = jnp.maximum(top, jnp.max(scores, axis=1, keepdims=True))
        factor = jnp.exp2((top - new_top) * SCALE_LOG2)
        weights = jnp.exp2(scores * SCALE_LOG2 - new_top * SCALE_LOG2)
        total = total * factor + jnp.sum(weights, axis=1, keepdims=True)
        acc = acc * factor + dot(weights.astype(BF16), values[there, :])
        return new_top, total, acc

    carry = (
        jnp.full((stacked, 1), MASKED, F32),
        jnp.zeros((stacked, 1), F32),
        jnp.zeros((stacked, HD), F32),
    )
    carry = lax.fori_loop(0, clear, functools.partial(step, masked=False), carry)
    top, total, acc = lax.fori_loop(clear, needed, functools.partial(step, masked=True), carry)
    acc = acc / total
    for h in range(heads):
        out[:, h * HD : (h + 1) * HD] = acc[h * rows : (h + 1) * rows].astype(BF16)
    log_sum = top * SCALE_LOG2 + jnp.log2(total)
    lse[0] = jnp.transpose(jnp.broadcast_to(log_sum, (stacked, 128)))[:8]


def attend_back_kernel(
    heads, rows, block, prefix_ref, qkv, grad_out, attended, lse, cos, sin, out, keys, values, grad_keys, grad_values
):
    i = pl.program_id(0)
    prefix = prefix_ref[0]
    at = heads * HD

    @pl.when(i == 0)
    def _():
        load_keys(qkv, cos, sin, keys, values, heads, rows)
        grad_keys[...] = jnp.zeros_like(grad_keys)
        grad_values[...] = jnp.zeros_like(grad_values)

    here = pl.ds(pl.multiple_of(i * rows, rows), rows)
    cos_here, sin_here = cos[here, :], sin[here, :]
    queries = stack_rotated(qkv, here, heads, cos_here, sin_here)
    grads = stack_heads(grad_out, here, heads)
    outs = stack_heads(attended, here, heads)
    stacked = heads * rows
    row_dot = lax.dot_general(
        jnp.ones((8, HD), F32),
        grads.astype(F32) * outs.astype(F32),
        (((1,), (1,)), ((), ())),
        precision=lax.Precision.HIGHEST,
        preferred_element_type=F32,
    )[:1]
    log_sum = lse[0, :1]
    clear, needed = key_blocks(i, rows, block, prefix)

    def step(j, grad_queries, masked):
        there = pl.ds(pl.multiple_of(j * block, block), block)
        key_part = keys[there, :]
        probs = jnp.exp2(dot_nt(key_part, queries) * SCALE_LOG2 - log_sum)
        if masked:
            key_pos = j * block + lax.broadcasted_iota(jnp.int32, (block, stacked), 0)
            query_pos = i * rows + lax.rem(
                lax.broadcasted_iota(jnp.int32, (1, stacked), 1), rows
            )
            probs = jnp.where(key_pos < jnp.maximum(query_pos + 1, prefix), probs, 0.0)
        grad_probs = dot_nt(values[there, :], grads)
        grad_scores = (probs * (grad_probs - row_dot)).astype(BF16)
        grad_values[there, :] += dot(probs.astype(BF16), grads)
        grad_keys[there, :] += dot(grad_scores, queries)
        return grad_queries + dot_tn(grad_scores, key_part)

    grad_queries = jnp.zeros((stacked, HD), F32)
    grad_queries = lax.fori_loop(0, clear, functools.partial(step, masked=False), grad_queries)
    grad_queries = lax.fori_loop(clear, needed, functools.partial(step, masked=True), grad_queries)
    for h in range(heads):
        part = grad_queries[h * rows : (h + 1) * rows] * SCALE
        out[here, h * HD : (h + 1) * HD] = rotate_back(part, cos_here, sin_here).astype(BF16)

    @pl.when(i == pl.num_programs(0) - 1)
    def _():
        def body(k, carry):
            at_rows = pl.ds(pl.multiple_of(k * rows, rows), rows)
            part = grad_keys[at_rows, :] * SCALE
            out[at_rows, at : at + HD] = rotate_back(part, cos[at_rows, :], sin[at_rows, :]).astype(BF16)
            out[at_rows, at + HD : at + 2 * HD] = grad_values[at_rows, :].astype(BF16)
            return carry

        lax.fori_loop(0, qkv.shape[0] // rows, body, 0)


VMEM_LIMIT = 48 * 1024 * 1024


def attention_sizes(full_len):
    return min(256, full_len), min(512, full_len)


def attend(prefix, qkv, cos, sin):
    full_len, width = qkv.shape
    heads = width // HD - 2
    rows, block = attention_sizes(full_len)
    steps = full_len // rows
    whole = lambda shape: pl.BlockSpec(shape, lambda i: (0,) * len(shape))
    return pl.pallas_call(
        functools.partial(attend_kernel, heads, rows, block),
        grid=(steps,),
        in_specs=[
            pl.BlockSpec(memory_space=pltpu.SMEM),
            whole((full_len, width)),
            whole((full_len, HD)),
            whole((full_len, HD)),
        ],
        out_specs=[
            pl.BlockSpec((rows, heads * HD), lambda i: (i, 0)),
            pl.BlockSpec((1, 8, heads * rows), lambda i: (i, 0, 0)),
        ],
        out_shape=[
            jax.ShapeDtypeStruct((full_len, heads * HD), BF16),
            jax.ShapeDtypeStruct((steps, 8, heads * rows), F32),
        ],
        scratch_shapes=[pltpu.VMEM((full_len, HD), BF16)] * 2,
        compiler_params=pltpu.CompilerParams(vmem_limit_bytes=VMEM_LIMIT),
        cost_estimate=pl.CostEstimate(
            flops=heads * full_len * full_len * HD * 8, bytes_accessed=full_len * width * 4, transcendentals=heads * full_len * full_len // 2
        ),
        name="attend",
    )(prefix, qkv, cos, sin)


def attend_back(prefix, qkv, grad_out, attended, lse, cos, sin):
    full_len, width = qkv.shape
    heads = width // HD - 2
    rows, block = attention_sizes(full_len)
    steps = full_len // rows
    whole = lambda shape: pl.BlockSpec(shape, lambda i: (0,) * len(shape))
    return pl.pallas_call(
        functools.partial(attend_back_kernel, heads, rows, block),
        grid=(steps,),
        in_specs=[
            pl.BlockSpec(memory_space=pltpu.SMEM),
            whole((full_len, width)),
            whole((full_len, heads * HD)),
            whole((full_len, heads * HD)),
            pl.BlockSpec((1, 8, heads * rows), lambda i: (i, 0, 0)),
            whole((full_len, HD)),
            whole((full_len, HD)),
        ],
        out_specs=whole((full_len, width)),
        out_shape=jax.ShapeDtypeStruct((full_len, width), BF16),
        scratch_shapes=[pltpu.VMEM((full_len, HD), BF16)] * 2 + [pltpu.VMEM((full_len, HD), F32)] * 2,
        compiler_params=pltpu.CompilerParams(vmem_limit_bytes=VMEM_LIMIT),
        cost_estimate=pl.CostEstimate(
            flops=heads * full_len * full_len * HD * 20, bytes_accessed=full_len * width * 8, transcendentals=heads * full_len * full_len // 2
        ),
        name="attend_back",
    )(prefix, qkv, grad_out, attended, lse, cos, sin)


def mlp_kernel(
    groups,
    halves,
    normed,
    cotangent,
    gate_hbm,
    up_hbm,
    down_hbm,
    plane,
    hidden_out,
    grad_gate_out,
    grad_up_out,
    total_out,
    gate_w,
    up_w,
    down_w,
    rows_in,
    grad_in,
    hidden_s,
    grad_gate_s,
    grad_up_s,
    part,
    to_core,
    from_core,
    to_chip,
    from_chip,
    load_sem,
    store_sem,
    row_send,
    row_recv,
    relay_send,
    relay_recv,
    core_send,
    core_recv,
    chip_send,
    chip_recv,
):
    own_len, width = normed.shape
    chips_y = groups // 2
    chips = chips_y * halves
    f, t = lax.axis_index("fsdp"), lax.axis_index("tp")
    y, core = lax.div(f, 2), lax.rem(f, 2)

    def chip_at(step, sign):
        a, b = lax.div(step, halves), lax.rem(step, halves)
        return lax.rem(y + sign * a + chips_y, chips_y), lax.rem(t + sign * b + halves, halves)

    def device(at, at_core):
        return {"fsdp": at[0] * 2 + at_core, "tp": at[1]}

    def rows_of(at, at_core):
        slot = (at[0] * 2 + at_core) * halves + at[1]
        return pl.ds(pl.multiple_of(slot * own_len, own_len), own_len)

    here = (y, t)
    mate = device(here, 1 - core)
    mine = rows_of(here, core)

    def send_rows(step):
        return pltpu.make_async_remote_copy(
            src_ref=normed,
            dst_ref=plane.at[mine],
            send_sem=row_send.at[step],
            recv_sem=row_recv.at[step],
            device_id=device(chip_at(step, 1), core),
            device_id_type=pl.DeviceIdType.MESH,
        )

    def relay(step, source):
        rows = rows_of(chip_at(step, -1), core)
        return pltpu.make_async_remote_copy(
            src_ref=source,
            dst_ref=plane.at[rows],
            send_sem=relay_send.at[step],
            recv_sem=relay_recv.at[step],
            device_id=mate,
            device_id_type=pl.DeviceIdType.MESH,
        )

    def send_part(step):
        return pltpu.make_async_remote_copy(
            src_ref=to_core.at[step],
            dst_ref=from_core.at[step],
            send_sem=core_send.at[step],
            recv_sem=core_recv.at[step],
            device_id=mate,
            device_id_type=pl.DeviceIdType.MESH,
        )

    def send_sum(step):
        return pltpu.make_async_remote_copy(
            src_ref=to_chip.at[step],
            dst_ref=from_chip.at[step],
            send_sem=chip_send.at[step],
            recv_sem=chip_recv.at[step],
            device_id=device(chip_at(step, -1), core),
            device_id_type=pl.DeviceIdType.MESH,
        )

    barrier = pltpu.get_barrier_semaphore()
    pl.semaphore_signal(barrier, inc=1, device_id=mate, device_id_type=pl.DeviceIdType.MESH)
    for step in range(1, chips):
        pl.semaphore_signal(
            barrier, inc=1, device_id=device(chip_at(step, 1), core), device_id_type=pl.DeviceIdType.MESH
        )
    pl.semaphore_wait(barrier, chips)

    for step in range(1, chips):
        send_rows(step).start()
    relay(0, normed).start()
    own_copy = pltpu.make_async_copy(normed, plane.at[mine], load_sem.at[5])
    own_copy.start()
    weights = [
        pltpu.make_async_copy(gate_hbm, gate_w, load_sem.at[2]),
        pltpu.make_async_copy(up_hbm, up_w, load_sem.at[3]),
        pltpu.make_async_copy(down_hbm, down_w, load_sem.at[4]),
    ]
    for copy in weights:
        copy.start()
    own_copy.wait()
    for copy in weights:
        copy.wait()

    def stores(rows):
        return [
            pltpu.make_async_copy(hidden_s, hidden_out.at[rows], store_sem.at[0]),
            pltpu.make_async_copy(grad_gate_s, grad_gate_out.at[rows], store_sem.at[1]),
            pltpu.make_async_copy(grad_up_s, grad_up_out.at[rows], store_sem.at[2]),
        ]

    def block(rows, result):
        loads = [
            pltpu.make_async_copy(plane.at[rows], rows_in, load_sem.at[0]),
            pltpu.make_async_copy(cotangent.at[rows], grad_in, load_sem.at[1]),
        ]
        for copy in loads:
            copy.start()
        for copy in loads:
            copy.wait()
        gate = dot(rows_in[...], gate_w[...])
        up = dot(rows_in[...], up_w[...])
        grad_hidden = dot_nt(grad_in[...], down_w[...])
        sigmoid = 1.0 / (1.0 + jnp.exp(-gate))
        silu = gate * sigmoid
        hidden_s[...] = (silu * up).astype(BF16)
        grad_up_s[...] = (grad_hidden * silu).astype(BF16)
        grad_gate_s[...] = (grad_hidden * up * sigmoid * (1.0 + gate * (1.0 - sigmoid))).astype(BF16)
        for copy in stores(rows):
            copy.start()
        tile = 512 if width % 512 == 0 else width
        for at in range(0, width, tile):
            result[:, at : at + tile] = (
                dot_nt(grad_gate_s[...], gate_w[at : at + tile, :]) + dot_nt(grad_up_s[...], up_w[at : at + tile, :])
            ).astype(BF16)
        for copy in stores(rows):
            copy.wait()

    def pair(step, carry):
        source = chip_at(step, -1)

        @pl.when(step > 0)
        def _():
            send_rows(step).wait_recv()
            relay(step, plane.at[rows_of(source, core)]).start()

        block(rows_of(source, core), part)
        relay(step, normed).wait_recv()
        block(rows_of(source, 1 - core), to_core.at[step])
        send_part(step).start()
        send_part(step).wait_recv()

        @pl.when(step == 0)
        def _():
            total_out[...] = part[...].astype(F32) + from_core[step].astype(F32)

        @pl.when(step > 0)
        def _():
            to_chip[step] = (part[...].astype(F32) + from_core[step].astype(F32)).astype(BF16)
            send_sum(step).start()

        return carry

    lax.fori_loop(0, chips, pair, 0)

    def collect(step, carry):
        send_sum(step).wait_recv()
        total_out[...] += from_chip[step].astype(F32)
        send_sum(step).wait_send()
        send_rows(step).wait_send()
        return carry

    lax.fori_loop(1, chips, collect, 0)

    def drain(step, carry):
        relay(step, normed).wait_send()
        send_part(step).wait_send()
        return carry

    lax.fori_loop(0, chips, drain, 0)


def mlp(groups, halves, normed, cotangent, gate_cols, up_cols, down_rows):
    own_len, width = normed.shape
    hidden = gate_cols.shape[1]
    chips = groups // 2 * halves
    plane_len = own_len * groups * halves
    anywhere = pl.BlockSpec(memory_space=pl.ANY)
    dma = pltpu.SemaphoreType.DMA
    low = lambda *shape: pltpu.VMEM(shape, BF16)
    return pl.pallas_call(
        functools.partial(mlp_kernel, groups, halves),
        in_specs=[anywhere] * 5,
        out_specs=[anywhere] * 4 + [pl.BlockSpec(memory_space=pltpu.VMEM)],
        out_shape=[
            jax.ShapeDtypeStruct((plane_len, width), BF16),
            jax.ShapeDtypeStruct((plane_len, hidden), BF16),
            jax.ShapeDtypeStruct((plane_len, hidden), BF16),
            jax.ShapeDtypeStruct((plane_len, hidden), BF16),
            jax.ShapeDtypeStruct((own_len, width), F32),
        ],
        scratch_shapes=[
            low(width, hidden),
            low(width, hidden),
            low(hidden, width),
            low(own_len, width),
            low(own_len, width),
            low(own_len, hidden),
            low(own_len, hidden),
            low(own_len, hidden),
            low(own_len, width),
            low(chips, own_len, width),
            low(chips, own_len, width),
            low(chips, own_len, width),
            low(chips, own_len, width),
            dma((6,)),
            dma((3,)),
        ]
        + [dma((chips,))] * 8,
        compiler_params=pltpu.CompilerParams(
            collective_id=3, has_side_effects=True, vmem_limit_bytes=60 * 1024 * 1024
        ),
        cost_estimate=pl.CostEstimate(
            flops=plane_len * width * hidden * 10, bytes_accessed=plane_len * width * 8, transcendentals=plane_len * hidden
        ),
        name="mlp",
    )(normed, cotangent, gate_cols, up_cols, down_rows)


def normalize(values, gain):
    scale = lax.rsqrt(jnp.mean(values * values, axis=-1, keepdims=True) + EPS)
    return scale, (values * scale * gain).astype(BF16)


def normalize_back(values, scale, gain, grad_normed):
    inner = grad_normed * gain
    mixed = jnp.mean(inner * values, axis=-1, keepdims=True)
    return scale * inner - values * scale**3 * mixed


def swap(values, axis, bit):
    size = lax.axis_size(axis)
    return lax.ppermute(values, axis, [(i, i ^ bit) for i in range(size)])


def half_sum(partial):
    half = partial.shape[0] // 2
    me = lax.axis_index("tp")
    kept = lax.dynamic_slice_in_dim(partial, me * half, half, 0)
    sent = lax.dynamic_slice_in_dim(partial, (1 - me) * half, half, 0)
    return kept.astype(F32) + swap(sent, "tp", 1).astype(F32)


def halve(partial, axis, bit):
    left = lax.axis_size(axis) // bit
    rows, columns = partial.shape
    blocks = partial.reshape(left // 2, 2, rows // left, columns)
    mine = lax.rem(lax.div(lax.axis_index(axis), bit), 2)
    kept = lax.dynamic_index_in_dim(blocks, mine, 1, keepdims=False)
    sent = lax.dynamic_index_in_dim(blocks, 1 - mine, 1, keepdims=False)
    total = kept.astype(F32) + swap(sent, axis, bit).astype(F32)
    return total.astype(BF16).reshape(rows // 2, columns)


def both_halves(values):
    me = lax.axis_index("tp")
    other = swap(values, "tp", 1)
    first = jnp.where(me == 0, values, other)
    second = jnp.where(me == 0, other, values)
    return jnp.concatenate([first, second], axis=0)


def by_owner(partial, groups, context):
    width, columns = partial.shape
    piece = width // (groups * context)
    return jnp.swapaxes(partial.reshape(groups, context, piece, columns), 0, 1).reshape(width, columns)


def tie(*values):
    return lax.optimization_barrier(values)


def on_device(
    tokens, prefix, attn_gain, w_query, w_key, w_value, w_out, mlp_gain, w_gate, w_up, w_down, cotangent
):
    _, local_len, width = tokens.shape
    groups, context, halves = lax.axis_size("fsdp"), lax.axis_size("ctx"), lax.axis_size("tp")
    own_len = local_len // halves
    full_len = local_len * context
    query_cols = w_query.shape[1]
    kv_heads = w_key.shape[1] // HD
    copies = context // kv_heads
    heads = query_cols // HD // context
    group_cols = (heads + 2) * HD
    hidden_cols = w_gate.shape[1] // groups
    own_start = lax.axis_index("tp") * own_len
    own = lambda values: lax.dynamic_slice_in_dim(values, own_start, own_len, 0)

    parts = []
    for c in range(context):
        kv = c // copies
        parts.append(w_query[:, c * heads * HD : (c + 1) * heads * HD])
        parts.append(w_key[:, kv * HD : (kv + 1) * HD])
        parts.append(w_value[:, kv * HD : (kv + 1) * HD])
    qkv_shard = jnp.concatenate(parts, axis=1)
    qkv_full = lax.all_gather(qkv_shard, "fsdp", axis=0, tiled=True)
    grad_out = cotangent.reshape(local_len, width)

    cos, sin = rope_tables(full_len)
    inputs_all = tokens.reshape(local_len, width)
    _, normed_one = normalize(inputs_all.astype(F32), attn_gain)
    inputs = own(inputs_all).astype(F32)
    scale_one = lax.rsqrt(jnp.mean(inputs * inputs, axis=-1, keepdims=True) + EPS)

    qkv_full, normed_one, w_out, w_gate_now = tie(qkv_full, normed_one, w_out, w_gate)
    mixer_full = lax.all_gather(w_out, "fsdp", axis=1, tiled=True)
    gate_cols = lax.all_to_all(w_gate_now, "fsdp", split_axis=1, concat_axis=0, tiled=True)
    proj = dot(normed_one, qkv_full).astype(BF16)
    qkv = lax.all_to_all(proj, "ctx", split_axis=1, concat_axis=0, tiled=True)

    qkv, gate_cols, mixer_full, w_up_now, grad_now = tie(qkv, gate_cols, mixer_full, w_up, own(grad_out))
    up_cols = lax.all_to_all(w_up_now, "fsdp", split_axis=1, concat_axis=0, tiled=True)
    grad_plane = lax.all_gather(grad_now, ("fsdp", "tp"), axis=0, tiled=True)
    attended, lse = attend(prefix, qkv, cos, sin)

    attended, up_cols, w_down_now = tie(attended, up_cols, w_down)
    down_rows = lax.all_to_all(w_down_now, "fsdp", split_axis=0, concat_axis=1, tiled=True)
    heads_back = lax.all_to_all(attended, "ctx", split_axis=0, concat_axis=1, tiled=True)
    branch = half_sum(dot(heads_back, mixer_full).astype(BF16))
    middle = inputs + branch
    scale_two, normed_two = normalize(middle, mlp_gain)

    normed_two, down_rows, grad_plane = tie(normed_two, down_rows, grad_plane)
    normed_plane, hidden, grad_gate, grad_up, grad_normed_two = mlp(
        groups, halves, normed_two, grad_plane, gate_cols, up_cols, down_rows
    )
    piece = width // (groups * context)
    plane_part = lambda left, right: by_owner(dot_tn(left, right).astype(BF16), groups, context)
    scatter = lambda part: lax.psum_scatter(part, "ctx", scatter_dimension=0, tiled=True)

    own_middle = own(grad_out).astype(F32) + normalize_back(middle, scale_two, mlp_gain, grad_normed_two)
    branch_own, grad_plane, normed_plane = tie(own_middle.astype(BF16), grad_plane, normed_plane)
    branch_low = both_halves(branch_own)
    down_part = plane_part(grad_plane, hidden)
    branch_low, down_part, normed_plane_now = tie(branch_low, down_part, normed_plane)
    down_sum = scatter(down_part)
    gate_part = plane_part(normed_plane_now, grad_gate)
    grad_heads = dot_nt(branch_low, mixer_full).astype(BF16)
    grad_heads, gate_part, normed_plane_now, hidden_now = tie(grad_heads, gate_part, normed_plane, hidden)
    gate_sum = scatter(gate_part)
    grad_attended = lax.all_to_all(grad_heads, "ctx", split_axis=1, concat_axis=0, tiled=True)
    up_part = plane_part(normed_plane_now, grad_up)
    down_out = dot(hidden_now, down_rows).astype(BF16)
    down_out = halve(down_out, "fsdp", 1)
    grad_attended, up_part, down_out, heads_back = tie(grad_attended, up_part, down_out, heads_back)
    up_sum = scatter(up_part)
    grad_qkv = attend_back(prefix, qkv, grad_attended, attended, lse, cos, sin)
    bit = 2
    while bit < groups:
        down_out = halve(down_out, "fsdp", bit)
        bit *= 2
    out_part = dot_tn(branch_low, heads_back).astype(BF16)
    out_part = halve(out_part, "fsdp", 1)
    grad_qkv, out_part, down_out = tie(grad_qkv, out_part, down_out)
    grad_proj = lax.all_to_all(grad_qkv, "ctx", split_axis=0, concat_axis=1, tiled=True)
    bit = 2
    while bit < groups:
        out_part = halve(out_part, "fsdp", bit)
        bit *= 2
    down_half = half_sum(down_out)
    grad_proj, out_part, down_half = tie(grad_proj, out_part, down_half)
    qkv_part = halve(dot_tn(normed_one, grad_proj).astype(BF16), "fsdp", 1)
    grad_normed_one = half_sum(dot_nt(grad_proj, qkv_full).astype(BF16))
    layer_own = (middle + down_half).astype(BF16)
    own_input_grad = own_middle + normalize_back(inputs, scale_one, attn_gain, grad_normed_one)
    bit = 2
    while bit < groups:
        qkv_part = halve(qkv_part, "fsdp", bit)
        bit *= 2
    qkv_part, input_own, layer_own = tie(qkv_part, own_input_grad.astype(BF16), layer_own)
    input_grad = both_halves(input_own).astype(F32)
    layer_out = both_halves(layer_own)

    def from_groups(sums):
        sums = sums.reshape(groups, piece, hidden_cols)
        return lax.all_to_all(sums, "fsdp", split_axis=0, concat_axis=0, tiled=True)

    down_grad = jnp.transpose(from_groups(down_sum), (0, 2, 1)).reshape(groups * hidden_cols, -1).astype(F32)
    wide = lambda sums: jnp.transpose(from_groups(sums), (1, 0, 2)).reshape(-1, groups * hidden_cols).astype(F32)
    gate_grad, up_grad = wide(gate_sum), wide(up_sum)
    out_grad = jnp.transpose(scatter(out_part).astype(F32))
    qkv_grad = scatter(qkv_part).astype(F32)

    piece_start = lax.axis_index("ctx") * piece
    rows_of = lambda weight: lax.dynamic_slice_in_dim(weight, piece_start, piece, 0).astype(F32)
    mlp_sum = jnp.sum(rows_of(w_gate) * gate_grad + rows_of(w_up) * up_grad, axis=1)
    attn_sum = jnp.sum(rows_of(qkv_shard) * qkv_grad, axis=1)
    gain_starts = lax.axis_index("fsdp") * (piece * context) + piece_start
    gain_of = lambda gain: lax.dynamic_slice_in_dim(gain, gain_starts, piece, 0)
    sums = lax.psum(jnp.stack([mlp_sum, attn_sum]), "tp")
    mlp_gain_grad = sums[0] / gain_of(mlp_gain)
    attn_gain_grad = sums[1] / gain_of(attn_gain)

    grouped = qkv_grad.reshape(piece, context, group_cols)
    query_grad = grouped[:, :, : heads * HD].reshape(piece, query_cols)
    pairs = grouped[:, :, heads * HD :].reshape(piece, kv_heads, copies, 2 * HD).sum(axis=2)
    key_grad = pairs[:, :, :HD].reshape(piece, kv_heads * HD)
    value_grad = pairs[:, :, HD:].reshape(piece, kv_heads * HD)
    return (
        layer_out.reshape(tokens.shape),
        input_grad.reshape(tokens.shape),
        attn_gain_grad,
        query_grad,
        key_grad,
        value_grad,
        out_grad,
        mlp_gain_grad,
        gate_grad,
        up_grad,
        down_grad,
    )


def solution(mesh):
    rows = P("fsdp", "ctx", None)
    owned = P(("fsdp", "ctx"), "tp")
    owned_t = P("tp", ("fsdp", "ctx"))
    gain = P(("fsdp", "ctx"))
    down, up = P("fsdp", "tp"), P("tp", "fsdp")
    return jax.shard_map(
        on_device,
        mesh=mesh,
        in_specs=(rows, P("fsdp"), P(), down, down, down, up, P(), down, down, up, rows),
        out_specs=(rows, rows, gain, owned, owned, owned, owned_t, gain, owned, owned, owned_t),
        check_vma=False,
    )
```

```python
import functools
import math

import jax
import jax.numpy as jnp
from jax import lax
from jax.experimental import pallas as pl
from jax.experimental.pallas import tpu as pltpu
from jax.sharding import PartitionSpec as P

HD = 80
EPS = 1e-05
THETA = 1000000.0
MASKED = -1e30
SCALE = HD ** (-0.5)
SCALE_LOG2 = SCALE * math.log2(math.e)
BF16 = jnp.bfloat16
F32 = jnp.float32
MESH = pl.DeviceIdType.MESH


def dot(left, right):
    return jnp.dot(left, right, preferred_element_type=F32)


def dot_tn(left, right):
    return lax.dot_general(left, right, (((0,), (0,)), ((), ())), preferred_element_type=F32)


def dot_nt(left, right):
    return lax.dot_general(left, right, (((1,), (1,)), ((), ())), preferred_element_type=F32)


def rope_tables(full_len):
    half = HD // 2
    frequency = THETA ** (-(jnp.arange(half, dtype=F32) * 2.0) / HD)
    angles = jnp.arange(full_len, dtype=jnp.int32).astype(F32)[:, None] * frequency[None, :]
    cos, sin = jnp.cos(angles), jnp.sin(angles)
    return jnp.concatenate([cos, cos], axis=1), jnp.concatenate([-sin, sin], axis=1)


def swap_halves(values):
    half = HD // 2
    return jnp.concatenate([values[:, half:], values[:, :half]], axis=1)


def rotate(values, cos, sin):
    values = values.astype(F32)
    return values * cos + swap_halves(values) * sin


def rotate_back(values, cos, sin):
    return values * cos - swap_halves(values) * sin


def stack_heads(ref, rows, heads):
    return jnp.concatenate([ref[rows, h * HD : (h + 1) * HD] for h in range(heads)], axis=0)


def stack_rotated(ref, rows, heads, cos, sin):
    return jnp.concatenate(
        [rotate(ref[rows, h * HD : (h + 1) * HD], cos, sin).astype(BF16) for h in range(heads)],
        axis=0,
    )


def load_keys(pair, cos, sin, keys, values, step):
    def body(i, carry):
        rows = pl.ds(pl.multiple_of(i * step, step), step)
        keys[rows, :] = rotate(pair[rows, :HD], cos[rows, :], sin[rows, :]).astype(BF16)
        values[rows, :] = pair[rows, HD:]
        return carry

    lax.fori_loop(0, pair.shape[0] // step, body, 0)


def key_blocks(i, rows, block, full_len):
    start = i * rows
    clear = lax.div(start + 1, block)
    needed = lax.div(jnp.maximum(start + rows, full_len // 2) + block - 1, block)
    return clear, needed


def attention_sizes(full_len):
    return min(256, full_len), min(512, full_len)


def front_kernel(
    groups,
    context,
    heads,
    prefix_ref,
    tokens,
    gain_one,
    gain_two,
    cos,
    sin,
    w_query,
    w_key,
    w_value,
    w_out,
    w_gate,
    w_up,
    w_down,
    cotangent,
    normed,
    query_in,
    pair_in,
    attended,
    lse,
    heads_in,
    middle,
    normed_two,
    query_hbm,
    key_hbm,
    value_hbm,
    mixer_hbm,
    gate_hbm,
    up_hbm,
    down_hbm,
    grad_plane,
    query_w,
    key_w,
    value_w,
    mixer_w,
    query_out,
    pair_out,
    keys,
    values,
    branch_out,
    branch_in,
    own_sem,
    save_sem,
    gather_send,
    gather_recv,
    relay_send,
    relay_recv,
    query_send,
    query_recv,
    pair_send,
    pair_recv,
    heads_send,
    heads_recv,
    ff_own,
    ff_send,
    ff_recv,
    branch_sem,
    plane_sem,
):
    ff_in, ff_out = (w_gate, w_up, w_down), (gate_hbm, up_hbm, down_hbm)
    local_len, width = tokens.shape
    full_len = local_len * context
    own_len = local_len // 2
    chips = groups // 2
    f, c, t = lax.axis_index("fsdp"), lax.axis_index("ctx"), lax.axis_index("tp")
    y, core = lax.div(f, 2), lax.rem(f, 2)
    mate = {"fsdp": y * 2 + 1 - core}
    up_y = lambda a: {"fsdp": lax.rem(y + a, chips) * 2 + core}
    source_y = lambda a: lax.rem(y + chips - a, chips) * 2 + core
    next_group = lambda k: lax.rem(f + k, groups)
    next_ctx = lambda k: lax.rem(c + k, context)
    last_ctx = lambda k: lax.rem(c + context - k, context)
    other_half = {"tp": 1 - t}

    gathered = [
        (w_query, query_w, query_hbm),
        (w_key, key_w, key_hbm),
        (w_value, value_w, value_hbm),
        (w_out, mixer_w, mixer_hbm),
    ]

    def own_shard(w):
        return pltpu.make_async_copy(gathered[w][0], gathered[w][1].at[f], own_sem.at[w])

    def to_chip(w, a):
        return pltpu.make_async_remote_copy(
            src_ref=gathered[w][0],
            dst_ref=gathered[w][1].at[f],
            send_sem=gather_send.at[w, a],
            recv_sem=gather_recv.at[w, a],
            device_id=up_y(a) if a else mate,
            device_id_type=MESH,
        )

    def relay(w, a):
        at = source_y(a)
        return pltpu.make_async_remote_copy(
            src_ref=gathered[w][1].at[at],
            dst_ref=gathered[w][1].at[at],
            send_sem=relay_send.at[w, a],
            recv_sem=relay_recv.at[w, a],
            device_id=mate,
            device_id_type=MESH,
        )

    def save(w):
        return pltpu.make_async_copy(gathered[w][1], gathered[w][2], save_sem.at[w])

    def send_all(w):
        for a in range(1, chips):
            to_chip(w, a).start()
        to_chip(w, 0).start()
        own_shard(w).start()

    def arrive(w):
        for a in range(1, chips):
            to_chip(w, a).wait_recv()
            relay(w, a).start()

    def complete(w):
        own_shard(w).wait()
        to_chip(w, 0).wait_recv()
        for a in range(1, chips):
            relay(w, a).wait_recv()
        save(w).start()

    def finish(w):
        for a in range(chips):
            to_chip(w, a).wait_send()
        for a in range(1, chips):
            relay(w, a).wait_send()
        save(w).wait()

    def send_heads(kind, k):
        out, into, send, recv = [
            (query_out, query_in, query_send, query_recv),
            (pair_out, pair_in, pair_send, pair_recv),
        ][kind]
        return pltpu.make_async_remote_copy(
            src_ref=out.at[next_ctx(k)],
            dst_ref=into.at[pl.ds(pl.multiple_of(c * local_len, local_len), local_len)],
            send_sem=send.at[k],
            recv_sem=recv.at[k],
            device_id={"ctx": next_ctx(k)},
            device_id_type=MESH,
        )

    def rows_of_ctx(at):
        return pl.ds(pl.multiple_of(at * local_len, local_len), local_len)

    def send_back(at):
        return pltpu.make_async_remote_copy(
            src_ref=attended.at[rows_of_ctx(at)],
            dst_ref=heads_in.at[c],
            send_sem=heads_send.at[at],
            recv_sem=heads_recv.at[c],
            device_id={"ctx": at},
            device_id_type=MESH,
        )

    def get_back(at):
        return pltpu.make_async_remote_copy(
            src_ref=attended.at[rows_of_ctx(at)],
            dst_ref=heads_in.at[at],
            send_sem=heads_send.at[at],
            recv_sem=heads_recv.at[at],
            device_id={"ctx": at},
            device_id_type=MESH,
        )

    def ff_parts(w, g):
        units = lax.rem(g, 2) * 2 + lax.rem(c, 2)
        if w < 2:
            cols = ff_out[w].shape[1]
            shard = width // groups
            return (
                ff_in[w].at[:, pl.ds(pl.multiple_of(units * cols, cols), cols)],
                ff_out[w].at[pl.ds(pl.multiple_of(f * shard, shard), shard)],
            )
        rows = ff_out[w].shape[1]
        return ff_in[w].at[pl.ds(pl.multiple_of(units * rows, rows), rows)], ff_out[w].at[f]

    def send_ff(w, k):
        g = next_group(k)
        source, target = ff_parts(w, g)
        return pltpu.make_async_remote_copy(
            src_ref=source,
            dst_ref=target,
            send_sem=ff_send.at[w, k],
            recv_sem=ff_recv.at[w, k],
            device_id={"fsdp": g},
            device_id_type=MESH,
        )

    def own_ff(w):
        source, target = ff_parts(w, f)
        return pltpu.make_async_copy(source, target, ff_own.at[w])

    pair_rows = lambda at_core, at_pair: pl.ds(pl.multiple_of((at_core * 2 + at_pair) * local_len, local_len), local_len)
    p = lax.rem(c, 2)
    pair_mate = {"ctx": c + 1 - 2 * p}
    plane_own = pltpu.make_async_copy(cotangent, grad_plane.at[pair_rows(core, p)], plane_sem.at[0])

    def plane_copy(i, source, rows, partner):
        return pltpu.make_async_remote_copy(
            src_ref=source,
            dst_ref=grad_plane.at[rows],
            send_sem=plane_sem.at[1 + 2 * i],
            recv_sem=plane_sem.at[2 + 2 * i],
            device_id=partner,
            device_id_type=MESH,
        )

    plane_copies = [
        plane_copy(0, cotangent, pair_rows(core, p), pair_mate),
        plane_copy(1, cotangent, pair_rows(core, p), mate),
        plane_copy(2, grad_plane.at[pair_rows(core, 1 - p)], pair_rows(core, 1 - p), mate),
    ]

    barrier = pltpu.get_barrier_semaphore()
    partners = [{"fsdp": next_group(k)} for k in range(1, groups)]
    partners += [{"ctx": next_ctx(k)} for k in range(1, context)]
    partners.append(other_half)
    for partner in partners:
        pl.semaphore_signal(barrier, inc=1, device_id=partner, device_id_type=MESH)
    pl.semaphore_wait(barrier, len(partners))

    for w in range(3):
        send_all(w)
    plane_own.start()
    for copy in plane_copies[:2]:
        copy.start()

    step = min(128, local_len)

    def norm_rows(i, carry):
        rows = pl.ds(pl.multiple_of(i * step, step), step)
        part = tokens[rows, :].astype(F32)
        scale = lax.rsqrt(jnp.mean(part * part, axis=-1, keepdims=True) + EPS)
        normed[rows, :] = (part * scale * gain_one[...]).astype(BF16)
        return carry

    lax.fori_loop(0, local_len // step, norm_rows, 0)

    shard = width // groups

    def project(weight):
        total = None
        for g in range(groups):
            part = dot(normed[:, g * shard : (g + 1) * shard], weight[g])
            total = part if total is None else total + part
        return total.astype(BF16)

    query_cols = heads * HD
    arrive(0)
    complete(0)
    query = project(query_w)
    for at in range(context):
        query_out[at] = query[:, at * query_cols : (at + 1) * query_cols]
    for k in range(1, context):
        send_heads(0, k).start()
    query_in[rows_of_ctx(c), :] = query_out[c]
    for w in (1, 2):
        arrive(w)
    for w in (1, 2):
        complete(w)
    send_all(3)
    kv_heads = key_w.shape[2] // HD
    copies = context // kv_heads
    key, value = project(key_w), project(value_w)
    for at in range(context):
        head = at // copies
        pair_out[at, :, :HD] = key[:, head * HD : (head + 1) * HD]
        pair_out[at, :, HD:] = value[:, head * HD : (head + 1) * HD]
    for k in range(1, context):
        send_heads(1, k).start()
    pair_in[rows_of_ctx(c), :] = pair_out[c]

    for k in range(1, context):
        send_heads(0, k).wait_recv()
        send_heads(1, k).wait_recv()

    rows, block = attention_sizes(full_len)
    load_keys(pair_in, cos, sin, keys, values, rows)
    stacked = heads * rows
    prefix = prefix_ref[0]

    def attend_block(i, carry):
        here = pl.ds(pl.multiple_of(i * rows, rows), rows)
        queries = stack_rotated(query_in, here, heads, cos[here, :], sin[here, :])
        clear, needed = key_blocks(i, rows, block, full_len)

        def key_step(j, carry, masked):
            top, total, acc = carry
            there = pl.ds(pl.multiple_of(j * block, block), block)
            scores = dot_nt(queries, keys[there, :])
            if masked:
                key_pos = j * block + lax.broadcasted_iota(jnp.int32, (stacked, block), 1)
                query_pos = i * rows + lax.rem(lax.broadcasted_iota(jnp.int32, (stacked, 1), 0), rows)
                scores = jnp.where(key_pos < jnp.maximum(query_pos + 1, prefix), scores, MASKED)
            new_top = jnp.maximum(top, jnp.max(scores, axis=1, keepdims=True))
            factor = jnp.exp2((top - new_top) * SCALE_LOG2)
            weights = jnp.exp2(scores * SCALE_LOG2 - new_top * SCALE_LOG2)
            total = total * factor + jnp.sum(weights, axis=1, keepdims=True)
            acc = acc * factor + dot(weights.astype(BF16), values[there, :])
            return new_top, total, acc

        state = (
            jnp.full((stacked, 1), MASKED, F32),
            jnp.zeros((stacked, 1), F32),
            jnp.zeros((stacked, HD), F32),
        )
        state = lax.fori_loop(0, clear, functools.partial(key_step, masked=False), state)
        top, total, acc = lax.fori_loop(clear, needed, functools.partial(key_step, masked=True), state)
        acc = acc / total
        for h in range(heads):
            attended[here, h * HD : (h + 1) * HD] = acc[h * rows : (h + 1) * rows].astype(BF16)
        log_sum = top * SCALE_LOG2 + jnp.log2(total)
        lse[i] = jnp.transpose(jnp.broadcast_to(log_sum, (stacked, 128)))[:8]
        return carry

    per_ctx = local_len // rows
    arrive(3)
    plane_copies[0].wait_recv()
    plane_copies[2].start()
    for w in range(3):
        for k in range(1, groups):
            send_ff(w, k).start()
        own_ff(w).start()

    def attend_rows(at, carry):
        lax.fori_loop(at * per_ctx, (at + 1) * per_ctx, attend_block, 0)

        @pl.when(at != c)
        def _():
            send_back(at).start()

        @pl.when(at == c)
        def _():
            heads_in[c] = attended[rows_of_ctx(c), :]

        return carry

    lax.fori_loop(0, context, attend_rows, 0)

    def collect(at, carry):
        @pl.when(at != c)
        def _():
            get_back(at).wait_recv()
            send_back(at).wait_send()

        return carry

    lax.fori_loop(0, context, collect, 0)

    complete(3)

    def branch_rows(start, store):
        half = pl.ds(pl.multiple_of(start, own_len), own_len)
        for g in range(groups):
            total = None
            for at in range(context):
                part = dot(heads_in[at, half, :], mixer_w[g, at * query_cols : (at + 1) * query_cols, :])
                total = part if total is None else total + part
            store(g * shard, total)

    def keep_low(at, part):
        branch_out[:, at : at + shard] = part.astype(BF16)

    def keep(at, part):
        middle[:, at : at + shard] = part

    branch_rows((1 - t) * own_len, keep_low)
    branch = pltpu.make_async_remote_copy(
        src_ref=branch_out,
        dst_ref=branch_in,
        send_sem=branch_sem.at[0],
        recv_sem=branch_sem.at[1],
        device_id=other_half,
        device_id_type=MESH,
    )
    branch.start()
    branch_rows(t * own_len, keep)
    branch.wait_recv()
    part_len = min(128, own_len)

    def middle_rows(i, carry):
        at = pl.ds(pl.multiple_of(i * part_len, part_len), part_len)
        token_rows = pl.ds(pl.multiple_of(t * own_len + i * part_len, part_len), part_len)
        total = tokens[token_rows, :].astype(F32) + middle[at, :] + branch_in[at, :].astype(F32)
        middle[at, :] = total
        scale = lax.rsqrt(jnp.mean(total * total, axis=-1, keepdims=True) + EPS)
        normed_two[at, :] = (total * scale * gain_two[...]).astype(BF16)
        return carry

    lax.fori_loop(0, own_len // part_len, middle_rows, 0)
    branch.wait_send()
    for k in range(1, context):
        send_heads(0, k).wait_send()
        send_heads(1, k).wait_send()
    for w in range(4):
        finish(w)
    for w in range(3):
        for k in range(1, groups):
            send_ff(w, k).wait_recv()
            send_ff(w, k).wait_send()
        own_ff(w).wait()
    plane_own.wait()
    plane_copies[0].wait_send()
    for copy in plane_copies[1:]:
        copy.wait()


def front(groups, context, prefix, tokens, gain_one, gain_two, cos, sin, w_query, w_key, w_value, w_out, w_gate, w_up, w_down, cotangent):
    local_len, width = tokens.shape
    full_len = local_len * context
    own_len = local_len // 2
    query_cols = w_query.shape[1]
    heads = query_cols // HD // context
    rows, _ = attention_sizes(full_len)
    hidden = w_gate.shape[1] // 4
    anywhere = pl.BlockSpec(memory_space=pl.ANY)
    near = pl.BlockSpec(memory_space=pltpu.VMEM)
    dma = pltpu.SemaphoreType.DMA
    low = lambda *shape: jax.ShapeDtypeStruct(shape, BF16)
    low_v = lambda *shape: pltpu.VMEM(shape, BF16)
    shapes = [low(groups, *w.shape) for w in (w_query, w_key, w_value, w_out)]
    return pl.pallas_call(
        functools.partial(front_kernel, groups, context, heads),
        in_specs=[pl.BlockSpec(memory_space=pltpu.SMEM)] + [near] * 5 + [anywhere] * 8,
        out_specs=[near] * 8 + [anywhere] * 8,
        out_shape=[
            low(local_len, width),
            low(full_len, heads * HD),
            low(full_len, 2 * HD),
            low(full_len, heads * HD),
            jax.ShapeDtypeStruct((full_len // rows, 8, heads * rows), F32),
            low(context, local_len, heads * HD),
            jax.ShapeDtypeStruct((own_len, width), F32),
            low(own_len, width),
        ]
        + shapes
        + [low(width, hidden), low(width, hidden), low(groups, hidden, width // groups), low(4 * local_len, width)],
        scratch_shapes=[low_v(*shape.shape) for shape in shapes]
        + [
            low_v(context, local_len, heads * HD),
            low_v(context, local_len, 2 * HD),
            low_v(full_len, HD),
            low_v(full_len, HD),
            low_v(own_len, width),
            low_v(own_len, width),
            dma((4,)),
            dma((4,)),
            dma((4, groups // 2)),
            dma((4, groups // 2)),
            dma((4, groups // 2)),
            dma((4, groups // 2)),
        ]
        + [dma((context,))] * 6
        + [dma((3,)), dma((3, groups)), dma((3, groups)), dma((2,)), dma((7,))],
        compiler_params=pltpu.CompilerParams(
            collective_id=1, has_side_effects=True, vmem_limit_bytes=60 * 1024 * 1024
        ),
        cost_estimate=pl.CostEstimate(
            flops=local_len * width * query_cols * 6, bytes_accessed=local_len * width * 40, transcendentals=full_len * full_len
        ),
        name="front",
    )(
        prefix,
        tokens,
        gain_one.reshape(1, width),
        gain_two.reshape(1, width),
        cos,
        sin,
        w_query,
        w_key,
        w_value,
        w_out,
        w_gate,
        w_up,
        w_down,
        cotangent,
    )


def product(left, right, result, side, columns_in, columns_out, side_sem, columns_sem, columns_store):
    whole = pltpu.make_async_copy(right, side, side_sem)
    whole.start()
    tile = columns_in.shape[2]
    tiles = left.shape[1] // tile

    def load(i):
        at = pl.ds(pl.multiple_of(i * tile, tile), tile)
        return pltpu.make_async_copy(left.at[:, at], columns_in.at[lax.rem(i, 2)], columns_sem.at[lax.rem(i, 2)])

    def store(i):
        at = pl.ds(pl.multiple_of(i * tile, tile), tile)
        return pltpu.make_async_copy(columns_out, result.at[at], columns_store.at[0])

    load(0).start()
    whole.wait()

    def body(i, carry):
        load(i).wait()

        @pl.when(i + 1 < tiles)
        def _():
            load(i + 1).start()

        made = dot_tn(columns_in[lax.rem(i, 2)], side[...]).astype(BF16)

        @pl.when(i > 0)
        def _():
            store(i - 1).wait()

        columns_out[...] = made
        store(i).start()
        return carry

    lax.fori_loop(0, tiles, body, 0)
    store(tiles - 1).wait()


def mlp_kernel(
    groups,
    normed,
    cotangent,
    gate_hbm,
    up_hbm,
    down_hbm,
    plane,
    hidden_out,
    grad_gate_out,
    grad_up_out,
    down_part,
    out_own,
    out_core,
    total_out,
    gate_w,
    up_w,
    down_w,
    rows_in,
    grad_in,
    hidden_s,
    grad_gate_s,
    grad_up_s,
    part,
    to_core,
    from_core,
    to_chip,
    from_chip,
    columns_in,
    columns_out,
    load_sem,
    rows_sem,
    grad_sem,
    store_sem,
    columns_sem,
    columns_store,
    out_low,
    out_store,
    out_send,
    out_recv,
    row_send,
    row_recv,
    relay_send,
    relay_recv,
    core_send,
    core_recv,
    chip_send,
    chip_recv,
):
    own_len, width = normed.shape
    chips = 4
    f, c, t = lax.axis_index("fsdp"), lax.axis_index("ctx"), lax.axis_index("tp")
    core, p = lax.rem(f, 2), lax.rem(c, 2)

    def chip_at(step):
        a, b = lax.div(step, 2), lax.rem(step, 2)
        return lax.rem(p + a, 2), lax.rem(t + b, 2)

    def device(at, at_core):
        return {"fsdp": f - core + at_core, "ctx": c - p + at[0], "tp": at[1]}

    def rows_of(at, at_core):
        slot = (at_core * 2 + at[0]) * 2 + at[1]
        return pl.ds(pl.multiple_of(slot * own_len, own_len), own_len)

    here = (p, t)
    mate = {"fsdp": f + 1 - 2 * core}
    mine = rows_of(here, core)

    def remote(source, target, send, recv, partner):
        return pltpu.make_async_remote_copy(
            src_ref=source, dst_ref=target, send_sem=send, recv_sem=recv, device_id=partner, device_id_type=MESH
        )

    def send_rows(step):
        return remote(normed, plane.at[mine], row_send.at[step], row_recv.at[step], device(chip_at(step), core))

    def relay(step, source):
        rows = rows_of(chip_at(step), core)
        return remote(source, plane.at[rows], relay_send.at[step], relay_recv.at[step], mate)

    def send_part(step):
        return remote(to_core.at[step], from_core.at[step], core_send.at[step], core_recv.at[step], mate)

    def send_sum(step):
        return remote(
            to_chip.at[step], from_chip.at[step], chip_send.at[step], chip_recv.at[step], device(chip_at(step), core)
        )

    barrier = pltpu.get_barrier_semaphore()
    pl.semaphore_signal(barrier, inc=1, device_id=mate, device_id_type=MESH)
    for step in range(1, chips):
        pl.semaphore_signal(barrier, inc=1, device_id=device(chip_at(step), core), device_id_type=MESH)
    pl.semaphore_wait(barrier, chips)

    for step in (1, 2):
        send_rows(step).start()
    relay(0, normed).start()
    own_copy = pltpu.make_async_copy(normed, plane.at[mine], load_sem.at[3])
    own_copy.start()
    weights = [
        pltpu.make_async_copy(gate_hbm, gate_w, load_sem.at[0]),
        pltpu.make_async_copy(up_hbm, up_w, load_sem.at[1]),
        pltpu.make_async_copy(down_hbm, down_w, load_sem.at[2]),
    ]
    for copy in weights:
        copy.start()

    def block_rows(index):
        same = 1 - lax.rem(index, 2)
        return rows_of(chip_at(lax.div(index, 2)), lax.rem(core + 1 - same, 2))

    def load_rows(index):
        slot = lax.rem(index, 2)
        return pltpu.make_async_copy(plane.at[block_rows(index)], rows_in.at[slot], rows_sem.at[slot])

    def load_grad(index):
        slot = lax.rem(index, 2)
        return pltpu.make_async_copy(cotangent.at[block_rows(index)], grad_in.at[slot], grad_sem.at[slot])

    load_grad(0).start()
    own_copy.wait()
    load_rows(0).start()
    for copy in weights:
        copy.wait()

    def stores(index):
        rows = block_rows(index)
        return [
            pltpu.make_async_copy(hidden_s, hidden_out.at[rows], store_sem.at[0]),
            pltpu.make_async_copy(grad_gate_s, grad_gate_out.at[rows], store_sem.at[1]),
            pltpu.make_async_copy(grad_up_s, grad_up_out.at[rows], store_sem.at[2]),
        ]

    def keep_out(step):
        return pltpu.make_async_copy(out_low.at[0], out_own.at[step], out_store.at[0])

    def send_out(step):
        return remote(out_low.at[1], out_core.at[step], out_send.at[step], out_recv.at[step], mate)

    def block(index, result):
        slot = lax.rem(index, 2)
        load_grad(index).wait()

        @pl.when(index + 1 < 2 * chips)
        def _():
            load_grad(index + 1).start()

        load_rows(index).wait()
        gate = dot(rows_in[slot], gate_w[...])
        up = dot(rows_in[slot], up_w[...])
        shard = width // groups
        grad_hidden = sum(dot_nt(grad_in[slot, :, g * shard : (g + 1) * shard], down_w[g]) for g in range(groups))
        sigmoid = 1.0 / (1.0 + jnp.exp(-gate))
        silu = gate * sigmoid

        @pl.when(index > 0)
        def _():
            for copy in stores(index - 1):
                copy.wait()

        hidden_s[...] = (silu * up).astype(BF16)
        grad_up_s[...] = (grad_hidden * silu).astype(BF16)
        grad_gate_s[...] = (grad_hidden * up * sigmoid * (1.0 + gate * (1.0 - sigmoid))).astype(BF16)
        for copy in stores(index):
            copy.start()

        @pl.when((index > 1) & (slot == 0))
        def _():
            keep_out(lax.div(index, 2) - 1).wait()

        @pl.when((index > 1) & (slot == 1))
        def _():
            send_out(lax.div(index, 2) - 1).wait_send()

        for g in range(groups):
            out_low[slot, :, g * shard : (g + 1) * shard] = dot(hidden_s[...], down_w[g]).astype(BF16)

        @pl.when(slot == 0)
        def _():
            keep_out(lax.div(index, 2)).start()

        @pl.when(slot == 1)
        def _():
            send_out(lax.div(index, 2)).start()

        tile = 512 if width % 512 == 0 else width
        for at in range(0, width, tile):
            result[:, at : at + tile] = (
                dot_nt(grad_gate_s[...], gate_w[at : at + tile, :]) + dot_nt(grad_up_s[...], up_w[at : at + tile, :])
            ).astype(BF16)

    def pair(step, carry):
        @pl.when(step > 0)
        def _():
            send_rows(step).wait_recv()
            relay(step, plane.at[rows_of(chip_at(step), core)]).start()
            load_rows(2 * step).start()

        @pl.when(step == 1)
        def _():
            send_rows(3).start()

        block(2 * step, part)
        relay(step, normed).wait_recv()
        load_rows(2 * step + 1).start()
        block(2 * step + 1, to_core.at[step])
        send_part(step).start()
        send_part(step).wait_recv()

        @pl.when(step == 0)
        def _():
            total_out[...] = part[...].astype(F32) + from_core[step].astype(F32)

        @pl.when(step > 0)
        def _():
            to_chip[step] = (part[...].astype(F32) + from_core[step].astype(F32)).astype(BF16)
            send_sum(step).start()

        return carry

    lax.fori_loop(0, chips, pair, 0)
    for copy in stores(2 * chips - 1):
        copy.wait()

    side = gate_w.at[pl.ds(0, columns_in.shape[1])]
    product(cotangent, hidden_out, down_part, side, columns_in, columns_out, load_sem.at[0], columns_sem, columns_store)

    def collect(step, carry):
        send_sum(step).wait_recv()
        total_out[...] += from_chip[step].astype(F32)
        send_sum(step).wait_send()
        send_rows(step).wait_send()
        return carry

    lax.fori_loop(1, chips, collect, 0)

    keep_out(chips - 1).wait()
    send_out(chips - 1).wait_send()

    def drain(step, carry):
        relay(step, normed).wait_send()
        send_part(step).wait_send()
        send_out(step).wait_recv()
        return carry

    lax.fori_loop(0, chips, drain, 0)


def mlp(groups, normed, cotangent, gate_cols, up_cols, down_rows):
    own_len, width = normed.shape
    hidden = gate_cols.shape[1]
    chips = 4
    plane_len = own_len * 2 * chips
    tile = 512 if width % 512 == 0 else width
    anywhere = pl.BlockSpec(memory_space=pl.ANY)
    dma = pltpu.SemaphoreType.DMA
    low = lambda *shape: pltpu.VMEM(shape, BF16)
    return pl.pallas_call(
        functools.partial(mlp_kernel, groups),
        in_specs=[anywhere] * 5,
        out_specs=[anywhere] * 7 + [pl.BlockSpec(memory_space=pltpu.VMEM)],
        out_shape=[
            jax.ShapeDtypeStruct((plane_len, width), BF16),
            jax.ShapeDtypeStruct((plane_len, hidden), BF16),
            jax.ShapeDtypeStruct((plane_len, hidden), BF16),
            jax.ShapeDtypeStruct((plane_len, hidden), BF16),
            jax.ShapeDtypeStruct((width, hidden), BF16),
            jax.ShapeDtypeStruct((chips, own_len, width), BF16),
            jax.ShapeDtypeStruct((chips, own_len, width), BF16),
            jax.ShapeDtypeStruct((own_len, width), F32),
        ],
        scratch_shapes=[
            low(width, hidden),
            low(width, hidden),
            low(groups, hidden, width // groups),
            low(2, own_len, width),
            low(2, own_len, width),
            low(own_len, hidden),
            low(own_len, hidden),
            low(own_len, hidden),
            low(own_len, width),
            low(chips, own_len, width),
            low(chips, own_len, width),
            low(chips, own_len, width),
            low(chips, own_len, width),
            low(2, plane_len, tile),
            low(tile, hidden),
            dma((4,)),
            dma((2,)),
            dma((2,)),
            dma((3,)),
            dma((2,)),
            dma((1,)),
            low(2, own_len, width),
            dma((1,)),
        ]
        + [dma((chips,))] * 10,
        compiler_params=pltpu.CompilerParams(
            collective_id=3, has_side_effects=True, vmem_limit_bytes=60 * 1024 * 1024
        ),
        cost_estimate=pl.CostEstimate(
            flops=plane_len * width * hidden * 10, bytes_accessed=plane_len * width * 8, transcendentals=plane_len * hidden
        ),
        name="mlp",
    )(normed, cotangent, gate_cols, up_cols, down_rows)


def remote(source, target, send, recv, partner):
    return pltpu.make_async_remote_copy(
        src_ref=source, dst_ref=target, send_sem=send, recv_sem=recv, device_id=partner, device_id_type=MESH
    )


def greet(partners):
    barrier = pltpu.get_barrier_semaphore()
    for partner in partners:
        pl.semaphore_signal(barrier, inc=1, device_id=partner, device_id_type=MESH)
    pl.semaphore_wait(barrier, len(partners))


def half_rows(half, own_len):
    return pl.ds(pl.multiple_of(half * own_len, own_len), own_len)


def ctx_rows(at, local_len):
    return pl.ds(pl.multiple_of(at * local_len, local_len), local_len)


def chip_part(part, chip_in, send, recv, a, groups):
    f = lax.axis_index("fsdp")
    chips = groups // 2
    rows = part.shape[0] // chips
    to = lax.rem(lax.div(f, 2) + a, chips)
    return remote(
        part.at[pl.ds(pl.multiple_of(to * rows, rows), rows)],
        chip_in.at[a - 1],
        send.at[a],
        recv.at[a],
        {"fsdp": to * 2 + lax.rem(f, 2)},
    )


def add_chips(part, chip_in, sums, own, other, sem, groups, context):
    chips, pairs = groups // 2, context // 2
    rows = part.shape[0] // chips
    unit = rows // context
    y = lax.div(lax.axis_index("fsdp"), 2)

    def loads(i):
        slot = lax.rem(i, 2)
        mine = pl.ds(pl.multiple_of(y * rows + i * unit, unit), unit)
        at = pl.ds(pl.multiple_of(i * unit, unit), unit)
        copies = [pltpu.make_async_copy(part.at[mine], own.at[slot], sem.at[0, slot])]
        for a in range(1, chips):
            copies.append(pltpu.make_async_copy(chip_in.at[a - 1, at], other.at[slot, a - 1], sem.at[a, slot]))
        return copies

    for copy in loads(0):
        copy.start()

    def body(i, carry):
        slot = lax.rem(i, 2)

        @pl.when(i + 1 < context)
        def _():
            for copy in loads(i + 1):
                copy.start()

        for copy in loads(i):
            copy.wait()
        made = own[slot].astype(F32)
        for a in range(1, chips):
            made = made + other[slot, a - 1].astype(F32)
        sums[lax.rem(i, pairs), lax.div(i, pairs)] = made.astype(BF16)
        return carry

    lax.fori_loop(0, context, body, 0)


def pair_part(sums, pair_in, send, recv, b, context):
    c = lax.axis_index("ctx")
    to = lax.rem(lax.div(c, 2) + b, context // 2)
    return remote(sums.at[to], pair_in.at[b - 1], send.at[b], recv.at[b], {"ctx": to * 2 + lax.rem(c, 2)})


def turn_kernel(
    groups,
    context,
    heads,
    total,
    middle,
    cotangent,
    gain,
    mixer_hbm,
    down_part,
    plane,
    grad_gate,
    grad_up,
    out_own,
    out_core,
    own_middle,
    branch_low,
    grads_in,
    chip_in,
    gate_part,
    up_part,
    out_half,
    mixer_w,
    heads_out,
    side,
    columns_in,
    columns_out,
    out_rows,
    side_sem,
    columns_sem,
    columns_store,
    out_sem,
    mixer_sem,
    branch_send,
    branch_recv,
    heads_send,
    heads_recv,
    chip_send,
    chip_recv,
):
    own_len, width = total.shape
    local_len = own_len * 2
    shard = width // groups
    query_cols = heads * HD
    chips = groups // 2
    f, c, t = lax.axis_index("fsdp"), lax.axis_index("ctx"), lax.axis_index("tp")
    next_ctx = lambda k: lax.rem(c + k, context)
    next_chip = lambda a: {"fsdp": lax.rem(lax.div(f, 2) + a, chips) * 2 + lax.rem(f, 2)}
    greet([{"ctx": next_ctx(k)} for k in range(1, context)] + [{"tp": 1 - t}] + [next_chip(a) for a in range(1, chips)])

    send_chip = lambda a: chip_part(down_part, chip_in, chip_send, chip_recv, a, groups)
    for a in range(1, chips):
        send_chip(a).start()
    mixer = pltpu.make_async_copy(mixer_hbm, mixer_w, mixer_sem.at[0])
    mixer.start()

    step = min(128, own_len)
    steps = own_len // step

    def part_rows(half, i):
        return pl.ds(pl.multiple_of(half * own_len + i * step, step), step)

    def branch(half, i):
        rows = part_rows(half, i)
        return remote(branch_low.at[rows], branch_low.at[rows], branch_send.at[i], branch_recv.at[i], {"tp": 1 - t})

    def norm_back(i, carry):
        at = pl.ds(pl.multiple_of(i * step, step), step)
        rows = part_rows(t, i)
        part = middle[at, :]
        inner = total[at, :] * gain[...]
        mixed = jnp.mean(inner * part, axis=-1, keepdims=True)
        scale = lax.rsqrt(jnp.mean(part * part, axis=-1, keepdims=True) + EPS)
        grad = cotangent[rows, :].astype(F32) + scale * inner - part * (scale * scale * scale * mixed)
        own_middle[at, :] = grad
        branch_low[rows, :] = grad.astype(BF16)
        branch(t, i).start()
        return carry

    lax.fori_loop(0, steps, norm_back, 0)
    mixer.wait()

    def send_grads(half, k, order):
        return remote(
            heads_out.at[next_ctx(k), half_rows(half, own_len)],
            grads_in.at[pl.ds(pl.multiple_of(c * local_len + half * own_len, own_len), own_len)],
            heads_send.at[k, order],
            heads_recv.at[k, order],
            {"ctx": next_ctx(k)},
        )

    def aside(order):
        source, part = ((grad_gate, gate_part), (grad_up, up_part))[order]
        product(plane, source, part, side, columns_in, columns_out, side_sem.at[0], columns_sem, columns_store)

    def add_cores():
        p = lax.rem(c, 2)

        def body(step, carry):
            loads = [
                pltpu.make_async_copy(out_own.at[step], out_rows.at[0], out_sem.at[0]),
                pltpu.make_async_copy(out_core.at[step], out_rows.at[1], out_sem.at[1]),
            ]
            for copy in loads:
                copy.start()
            for copy in loads:
                copy.wait()
            out_rows[0] = (out_rows[0].astype(F32) + out_rows[1].astype(F32)).astype(BF16)
            slot = lax.rem(p + lax.div(step, 2), 2) * 2 + lax.rem(t + lax.rem(step, 2), 2)
            store = pltpu.make_async_copy(out_rows.at[0], out_half.at[slot], out_sem.at[2])
            store.start()
            store.wait()
            return carry

        lax.fori_loop(0, out_own.shape[0], body, 0)

    def both_parts(order, carry):
        half = jnp.where(order == 0, t, 1 - t)

        def one(i, inner):
            @pl.when(order == 1)
            def _():
                branch(1 - t, i).wait_recv()

            rows = part_rows(half, i)
            grad = sum(dot_nt(branch_low[rows, g * shard : (g + 1) * shard], mixer_w[g]) for g in range(groups))
            for at in range(context):
                heads_out[at, rows, :] = grad[:, at * query_cols : (at + 1) * query_cols].astype(BF16)
            return inner

        lax.fori_loop(0, steps, one, 0)
        for k in range(1, context):
            send_grads(half, k, order).start()
        grads_in[pl.ds(pl.multiple_of(c * local_len + half * own_len, own_len), own_len), :] = heads_out[
            c, half_rows(half, own_len), :
        ]

        @pl.when(order == 0)
        def _():
            aside(0)

        @pl.when(order == 1)
        def _():
            aside(1)
            add_cores()

        return carry

    lax.fori_loop(0, 2, both_parts, 0)
    for order, half in enumerate((t, 1 - t)):
        for k in range(1, context):
            send_grads(half, k, order).wait()
    for i in range(steps):
        branch(t, i).wait_send()
    for a in range(1, chips):
        send_chip(a).wait()


def turn(groups, context, heads, total, middle, cotangent, gain, mixer, down_part, plane, grad_gate, grad_up, out_own, out_core):
    own_len, width = total.shape
    local_len = own_len * 2
    chips = groups // 2
    steps = own_len // min(128, own_len)
    tile = 512 if width % 512 == 0 else width
    anywhere = pl.BlockSpec(memory_space=pl.ANY)
    near = pl.BlockSpec(memory_space=pltpu.VMEM)
    dma = pltpu.SemaphoreType.DMA
    low = lambda *shape: jax.ShapeDtypeStruct(shape, BF16)
    low_v = lambda *shape: pltpu.VMEM(shape, BF16)
    return pl.pallas_call(
        functools.partial(turn_kernel, groups, context, heads),
        in_specs=[near] * 4 + [anywhere] * 7,
        out_specs=[near] * 3 + [anywhere] * 4,
        out_shape=[
            jax.ShapeDtypeStruct((own_len, width), F32),
            low(local_len, width),
            low(local_len * context, heads * HD),
            low(chips - 1, width // chips, down_part.shape[1]),
            low(*down_part.shape),
            low(*down_part.shape),
            low(*out_own.shape),
        ],
        scratch_shapes=[
            low_v(*mixer.shape),
            low_v(context, local_len, heads * HD),
            low_v(*grad_gate.shape),
            low_v(2, plane.shape[0], tile),
            low_v(tile, grad_gate.shape[1]),
            low_v(2, own_len, width),
            dma((1,)),
            dma((2,)),
            dma((1,)),
            dma((3,)),
            dma((1,)),
            dma((steps,)),
            dma((steps,)),
            dma((context, 2)),
            dma((context, 2)),
            dma((chips,)),
            dma((chips,)),
        ],
        compiler_params=pltpu.CompilerParams(collective_id=4, has_side_effects=True, vmem_limit_bytes=60 * 1024 * 1024),
        cost_estimate=pl.CostEstimate(
            flops=local_len * width * heads * HD * context * 2, bytes_accessed=local_len * width * 20, transcendentals=0
        ),
        name="turn",
    )(
        total, middle, cotangent, gain.reshape(1, width), mixer, down_part, plane, grad_gate, grad_up, out_own, out_core
    )


def back_kernel(
    groups,
    context,
    heads,
    prefix_ref,
    grads_in,
    cos,
    sin,
    query_in,
    pair_in,
    attended,
    lse,
    down_part,
    gate_part,
    up_part,
    down_in,
    out_half,
    grad_proj,
    sums,
    pair_sums,
    gate_in,
    up_in,
    out_in,
    query_back,
    pair_back,
    keys,
    values,
    grad_keys,
    grad_values,
    query_out,
    pair_out,
    sum_own,
    sum_other,
    query_send,
    query_recv,
    pair_send,
    pair_recv,
    sum_sem,
    chip_send,
    chip_recv,
    pairs_send,
    pairs_recv,
    half_send,
    half_recv,
):
    full_len, query_cols = query_in.shape
    local_len = full_len // context
    chips, pairs = groups // 2, context // 2
    f, c, t = lax.axis_index("fsdp"), lax.axis_index("ctx"), lax.axis_index("tp")
    next_chip = lambda a: {"fsdp": lax.rem(lax.div(f, 2) + a, chips) * 2 + lax.rem(f, 2)}
    greet(
        [{"ctx": lax.rem(c + k, context)} for k in range(1, context)]
        + [{"tp": 1 - t}]
        + [next_chip(a) for a in range(1, chips)]
    )

    later = ((gate_part, gate_in), (up_part, up_in))

    def send_chip(w, a):
        return chip_part(*later[w], chip_send.at[w], chip_recv.at[w], a, groups)

    def send_pair(w, b):
        return pair_part(sums.at[w], pair_sums.at[w], pairs_send.at[w], pairs_recv.at[w], b, context)

    def add_part(w, part, chip_in):
        add_chips(part, chip_in, sums.at[w], sum_own, sum_other, sum_sem, groups, context)
        for b in range(1, pairs):
            send_pair(w, b).start()

    def send_half(p):
        return remote(out_half.at[p * 2 + 1 - t], out_in.at[p], half_send.at[p], half_recv.at[p], {"tp": 1 - t})

    for a in range(1, chips):
        send_chip(0, a).start()
    for p in range(2):
        send_half(p).start()

    rows, block = attention_sizes(full_len)
    load_keys(pair_in, cos, sin, keys, values, rows)
    grad_keys[...] = jnp.zeros_like(grad_keys)
    grad_values[...] = jnp.zeros_like(grad_values)
    stacked = heads * rows
    prefix = prefix_ref[0]

    def attend_block(i):
        here = pl.ds(pl.multiple_of(i * rows, rows), rows)
        cos_here, sin_here = cos[here, :], sin[here, :]
        queries = stack_rotated(query_in, here, heads, cos_here, sin_here)
        grads = stack_heads(grads_in, here, heads)
        outs = stack_heads(attended, here, heads)
        row_dot = lax.dot_general(
            jnp.ones((8, HD), F32),
            grads.astype(F32) * outs.astype(F32),
            (((1,), (1,)), ((), ())),
            precision=lax.Precision.HIGHEST,
            preferred_element_type=F32,
        )[:1]
        log_sum = lse[i][:1]
        clear, needed = key_blocks(i, rows, block, full_len)

        def key_step(j, grad_queries, masked):
            there = pl.ds(pl.multiple_of(j * block, block), block)
            key_part = keys[there, :]
            probs = jnp.exp2(dot_nt(key_part, queries) * SCALE_LOG2 - log_sum)
            if masked:
                key_pos = j * block + lax.broadcasted_iota(jnp.int32, (block, stacked), 0)
                query_pos = i * rows + lax.rem(lax.broadcasted_iota(jnp.int32, (1, stacked), 1), rows)
                probs = jnp.where(key_pos < jnp.maximum(query_pos + 1, prefix), probs, 0.0)
            grad_probs = dot_nt(values[there, :], grads)
            grad_scores = (probs * (grad_probs - row_dot)).astype(BF16)
            grad_values[there, :] += dot(probs.astype(BF16), grads)
            grad_keys[there, :] += dot(grad_scores, queries)
            return grad_queries + dot_tn(grad_scores, key_part)

        grad_queries = jnp.zeros((stacked, HD), F32)
        grad_queries = lax.fori_loop(0, clear, functools.partial(key_step, masked=False), grad_queries)
        grad_queries = lax.fori_loop(clear, needed, functools.partial(key_step, masked=True), grad_queries)
        for h in range(heads):
            part = grad_queries[h * rows : (h + 1) * rows] * SCALE
            query_out[here, h * HD : (h + 1) * HD] = rotate_back(part, cos_here, sin_here).astype(BF16)

    per_ctx = local_len // rows

    def send_query(at, source):
        return remote(
            query_out.at[ctx_rows(at, local_len)], query_back.at[source], query_send.at[at], query_recv.at[source], {"ctx": at}
        )

    def send_pair_grads(at, source):
        return remote(
            pair_out.at[ctx_rows(at, local_len)], pair_back.at[source], pair_send.at[at], pair_recv.at[source], {"ctx": at}
        )

    def finish_pair(at, carry):
        def body(i, inner):
            at_rows = pl.ds(pl.multiple_of(at * local_len + i * rows, rows), rows)
            part = grad_keys[at_rows, :] * SCALE
            pair_out[at_rows, :HD] = rotate_back(part, cos[at_rows, :], sin[at_rows, :]).astype(BF16)
            pair_out[at_rows, HD:] = grad_values[at_rows, :].astype(BF16)
            return inner

        lax.fori_loop(0, per_ctx, body, 0)

        @pl.when(at != c)
        def _():
            send_pair_grads(at, c).start()

        @pl.when(at == c)
        def _():
            pair_back[c] = pair_out[ctx_rows(c, local_len), :]

        return carry

    def attend_rows(order, carry):
        at = context - 1 - order

        def body(i, inner):
            attend_block(at * per_ctx + per_ctx - 1 - i)
            return inner

        lax.fori_loop(0, per_ctx, body, 0)

        @pl.when(at != c)
        def _():
            send_query(at, c).start()

        @pl.when(at == c)
        def _():
            query_back[c] = query_out[ctx_rows(c, local_len), :]

        @pl.when(order == 0)
        def _():
            add_part(0, down_part, down_in)

        @pl.when(order == context // 2)
        def _():
            for a in range(1, chips):
                send_chip(0, a).wait()
                send_chip(1, a).start()
            add_part(1, gate_part, gate_in)

        @pl.when(order == context // 2 - 1)
        def _():
            lax.fori_loop(context // 2, context, finish_pair, 0)

        return carry

    lax.fori_loop(0, context, attend_rows, 0)
    lax.fori_loop(0, context // 2, finish_pair, 0)

    def collect(at, carry):
        @pl.when(at != c)
        def _():
            send_query(at, at).wait()
            send_pair_grads(at, at).wait()

        return carry

    lax.fori_loop(0, context, collect, 0)

    kv_heads = (grad_proj.shape[1] // HD - heads * context) // 2
    copies = context // kv_heads
    key_at = context * query_cols
    value_at = key_at + kv_heads * HD
    for at in range(context):
        grad_proj[:, at * query_cols : (at + 1) * query_cols] = query_back[at]
    for head in range(kv_heads):
        pair = sum(pair_back[head * copies + i].astype(F32) for i in range(copies)).astype(BF16)
        grad_proj[:, key_at + head * HD : key_at + (head + 1) * HD] = pair[:, :HD]
        grad_proj[:, value_at + head * HD : value_at + (head + 1) * HD] = pair[:, HD:]

    for a in range(1, chips):
        send_chip(1, a).wait()
    for p in range(2):
        send_half(p).wait()
    for w in range(2):
        for b in range(1, pairs):
            send_pair(w, b).wait()


def back(
    groups, context, kv_heads, prefix, grads_in, cos, sin, query_in, pair_in, attended, lse, down_part, gate_part, up_part, down_in, out_half
):
    full_len, query_cols = query_in.shape
    local_len = full_len // context
    heads = query_cols // HD
    width, hidden = down_part.shape
    chips, pairs = groups // 2, context // 2
    unit = width // (chips * context)
    anywhere = pl.BlockSpec(memory_space=pl.ANY)
    near = pl.BlockSpec(memory_space=pltpu.VMEM)
    dma = pltpu.SemaphoreType.DMA
    low = lambda *shape: jax.ShapeDtypeStruct(shape, BF16)
    low_v = lambda *shape: pltpu.VMEM(shape, BF16)
    return pl.pallas_call(
        functools.partial(back_kernel, groups, context, heads),
        in_specs=[pl.BlockSpec(memory_space=pltpu.SMEM)] + [near] * 7 + [anywhere] * 5,
        out_specs=[near] * 3 + [anywhere] * 3,
        out_shape=[
            low(local_len, context * query_cols + 2 * kv_heads * HD),
            low(2, pairs, 2, unit, hidden),
            low(2, pairs - 1, 2, unit, hidden),
            low(chips - 1, width // chips, hidden),
            low(chips - 1, width // chips, hidden),
            low(2, *out_half.shape[1:]),
        ],
        scratch_shapes=[
            low_v(context, local_len, query_cols),
            low_v(context, local_len, 2 * HD),
            low_v(full_len, HD),
            low_v(full_len, HD),
            pltpu.VMEM((full_len, HD), F32),
            pltpu.VMEM((full_len, HD), F32),
            low_v(full_len, query_cols),
            low_v(full_len, 2 * HD),
            low_v(2, unit, hidden),
            low_v(2, chips - 1, unit, hidden),
        ]
        + [dma((context,))] * 4
        + [dma((chips, 2)), dma((2, chips)), dma((2, chips)), dma((2, pairs)), dma((2, pairs)), dma((2,)), dma((2,))],
        compiler_params=pltpu.CompilerParams(collective_id=5, has_side_effects=True, vmem_limit_bytes=60 * 1024 * 1024),
        cost_estimate=pl.CostEstimate(
            flops=heads * full_len * full_len * HD * 20, bytes_accessed=full_len * width * 8, transcendentals=heads * full_len * full_len // 2
        ),
        name="back",
    )(prefix, grads_in, cos, sin, query_in, pair_in, attended, lse, down_part, gate_part, up_part, down_in, out_half)


def finish_kernel(
    groups,
    context,
    grad_proj,
    inputs,
    own_middle,
    gain,
    middle,
    early_sums,
    early_pairs,
    out_half,
    out_in,
    up_part,
    up_in,
    query_hbm,
    key_hbm,
    value_hbm,
    input_low,
    layer_low,
    units,
    query_w,
    key_w,
    value_w,
    branch_out,
    branch_in,
    own_part,
    half_own,
    half_other,
    pair_out,
    pair_in,
    sums,
    pairs_in,
    sum_own,
    sum_other,
    core_out,
    slices,
    weight_sem,
    branch_send,
    branch_recv,
    input_send,
    input_recv,
    layer_send,
    layer_recv,
    half_sem,
    out_sem,
    sum_sem,
    pairs_send,
    pairs_recv,
    core_send,
    core_recv,
    unit_send,
    unit_recv,
):
    own_len, width = own_middle.shape
    shard = width // groups
    piece = units.shape[2]
    pairs = context // 2
    f, c, t = lax.axis_index("fsdp"), lax.axis_index("ctx"), lax.axis_index("tp")
    core, p, j = lax.rem(f, 2), lax.rem(c, 2), lax.div(c, 2)
    other_half, mate, next_z = {"tp": 1 - t}, {"fsdp": f + 1 - 2 * core}, {"ctx": c + 1 - 2 * p}
    greet([other_half, mate, next_z] + [{"ctx": lax.rem(j + b, pairs) * 2 + p} for b in range(1, pairs)])

    def load_weights(g):
        slot = g % 2
        return [
            pltpu.make_async_copy(hbm.at[g], near.at[slot], weight_sem.at[i, slot])
            for i, (hbm, near) in enumerate(((query_hbm, query_w), (key_hbm, key_w), (value_hbm, value_w)))
        ]

    def load_half(at):
        return [
            pltpu.make_async_copy(out_half.at[at * 2 + t], half_own, half_sem.at[0]),
            pltpu.make_async_copy(out_in.at[at], half_other, half_sem.at[1]),
        ]

    send_out = remote(pair_out, pair_in, out_sem.at[0], out_sem.at[1], next_z)
    for copy in load_weights(0) + load_half(1 - p):
        copy.start()
    for copy in load_half(1 - p):
        copy.wait()
    pair_out[...] = (half_own[...].astype(F32) + half_other[...].astype(F32)).astype(BF16)
    send_out.start()
    for copy in load_half(p):
        copy.start()

    def send_branch(g):
        return remote(branch_out.at[g], branch_in.at[g], branch_send.at[g], branch_recv.at[g], other_half)

    query_cols, key_cols = query_w.shape[2], key_w.shape[2]

    def back_rows(half, slot):
        rows = half_rows(half, own_len)
        return (
            dot_nt(grad_proj[rows, :query_cols], query_w[slot])
            + dot_nt(grad_proj[rows, query_cols : query_cols + key_cols], key_w[slot])
            + dot_nt(grad_proj[rows, query_cols + key_cols :], value_w[slot])
        )

    for g in range(groups):
        for copy in load_weights(g):
            copy.wait()
        if g + 1 < groups:
            for copy in load_weights(g + 1):
                copy.start()
        branch_out[g] = back_rows(1 - t, g % 2).astype(BF16)
        send_branch(g).start()
        own_part[:, g * shard : (g + 1) * shard] = back_rows(t, g % 2)

    def send_core(w):
        return remote(core_out.at[w], slices.at[w, core], core_send.at[w], core_recv.at[w], mate)

    def send_unit(w, s):
        return remote(slices.at[w, s, 1 - p], units.at[w, s * 2 + p], unit_send.at[w, s], unit_recv.at[w, s], next_z)

    def to_core(w, own, others):
        kept = own[j, core].astype(F32)
        given = own[j, 1 - core].astype(F32)
        for b in range(1, pairs):
            kept = kept + others[b - 1, core].astype(F32)
            given = given + others[b - 1, 1 - core].astype(F32)
        kept, given = kept.astype(BF16), given.astype(BF16)
        for at in range(2):
            slices[w, core, at] = kept[at * piece : (at + 1) * piece]
            core_out[w, at] = given[at * piece : (at + 1) * piece]
        send_core(w).start()

    def to_owner(w):
        send_core(w).wait_recv()
        for s in range(2):
            send_unit(w, s).start()
            units[w, s * 2 + p] = slices[w, s, p]

    def send_pair(b):
        return pair_part(sums, pairs_in, pairs_send, pairs_recv, b, context)

    add_chips(up_part, up_in, sums, sum_own, sum_other, sum_sem, groups, context)
    for b in range(1, pairs):
        send_pair(b).start()
    for w in range(2):
        to_core(w, early_sums.at[w], early_pairs.at[w])
    for w in range(2):
        to_owner(w)

    step = min(128, own_len)
    steps = own_len // step

    def send_low(result, send, recv, half, i):
        rows = pl.ds(pl.multiple_of(half * own_len + i * step, step), step)
        return remote(result.at[rows], result.at[rows], send.at[i], recv.at[i], other_half)

    for g in range(groups):
        send_branch(g).wait_recv()

    def norm_back(i, carry):
        at = pl.ds(pl.multiple_of(i * step, step), step)
        grad = jnp.concatenate(
            [own_part[at, g * shard : (g + 1) * shard] + branch_in[g, at, :].astype(F32) for g in range(groups)], axis=1
        )
        part = inputs[at, :].astype(F32)
        inner = grad * gain[...]
        mixed = jnp.mean(inner * part, axis=-1, keepdims=True)
        scale = lax.rsqrt(jnp.mean(part * part, axis=-1, keepdims=True) + EPS)
        made = own_middle[at, :] + scale * inner - part * (scale * scale * scale * mixed)
        input_low[pl.ds(pl.multiple_of(t * own_len + i * step, step), step), :] = made.astype(BF16)
        send_low(input_low, input_send, input_recv, t, i).start()
        return carry

    lax.fori_loop(0, steps, norm_back, 0)

    for copy in load_half(p):
        copy.wait()
    send_out.wait_recv()

    def layer_rows(i, carry):
        at = pl.ds(pl.multiple_of(i * step, step), step)
        made = middle[at, :] + (half_own[at, :].astype(F32) + half_other[at, :].astype(F32) + pair_in[at, :].astype(F32))
        layer_low[pl.ds(pl.multiple_of(t * own_len + i * step, step), step), :] = made.astype(BF16)
        send_low(layer_low, layer_send, layer_recv, t, i).start()
        return carry

    lax.fori_loop(0, steps, layer_rows, 0)

    for b in range(1, pairs):
        send_pair(b).wait_recv()
    to_core(2, sums, pairs_in)
    to_owner(2)

    for g in range(groups):
        send_branch(g).wait_send()
    send_out.wait_send()
    for b in range(1, pairs):
        send_pair(b).wait_send()
    for w in range(3):
        send_core(w).wait_send()
        for s in range(2):
            send_unit(w, s).wait()
    for i in range(steps):
        send_low(input_low, input_send, input_recv, t, i).wait_send()
        send_low(layer_low, layer_send, layer_recv, t, i).wait_send()
        send_low(input_low, input_send, input_recv, 1 - t, i).wait_recv()
        send_low(layer_low, layer_send, layer_recv, 1 - t, i).wait_recv()


def finish(groups, context, grad_proj, inputs, own_middle, gain, middle, early_sums, early_pairs, out_half, out_in, up_part, up_in, query_full, key_full, value_full):
    own_len, width = own_middle.shape
    chips, pairs = groups // 2, context // 2
    hidden = up_part.shape[1]
    unit = width // (chips * context)
    piece = unit // 2
    steps = own_len // min(128, own_len)
    anywhere = pl.BlockSpec(memory_space=pl.ANY)
    near = pl.BlockSpec(memory_space=pltpu.VMEM)
    dma = pltpu.SemaphoreType.DMA
    low = lambda *shape: jax.ShapeDtypeStruct(shape, BF16)
    low_v = lambda *shape: pltpu.VMEM(shape, BF16)
    return pl.pallas_call(
        functools.partial(finish_kernel, groups, context),
        in_specs=[near] * 7 + [anywhere] * 7,
        out_specs=[near] * 3,
        out_shape=[low(2 * own_len, width), low(2 * own_len, width), low(3, 4, piece, hidden)],
        scratch_shapes=[low_v(2, *w.shape[1:]) for w in (query_full, key_full, value_full)]
        + [
            low_v(groups, own_len, width // groups),
            low_v(groups, own_len, width // groups),
            pltpu.VMEM((own_len, width), F32),
            low_v(own_len, width),
            low_v(own_len, width),
            low_v(own_len, width),
            low_v(own_len, width),
            low_v(pairs, 2, unit, hidden),
            low_v(pairs - 1, 2, unit, hidden),
            low_v(2, unit, hidden),
            low_v(2, chips - 1, unit, hidden),
            low_v(3, 2, piece, hidden),
            low_v(3, 2, 2, piece, hidden),
            dma((3, 2)),
            dma((groups,)),
            dma((groups,)),
            dma((steps,)),
            dma((steps,)),
            dma((steps,)),
            dma((steps,)),
            dma((2,)),
            dma((2,)),
            dma((chips, 2)),
            dma((pairs,)),
            dma((pairs,)),
            dma((3,)),
            dma((3,)),
            dma((3, 2)),
            dma((3, 2)),
        ],
        compiler_params=pltpu.CompilerParams(collective_id=6, has_side_effects=True, vmem_limit_bytes=60 * 1024 * 1024),
        cost_estimate=pl.CostEstimate(
            flops=own_len * width * grad_proj.shape[1] * 4, bytes_accessed=own_len * width * 40, transcendentals=0
        ),
        name="finish",
    )(
        grad_proj,
        inputs,
        own_middle,
        gain.reshape(1, width),
        middle,
        early_sums,
        early_pairs,
        out_half,
        out_in,
        up_part,
        up_in,
        query_full,
        key_full,
        value_full,
    )


def tie(*values):
    return lax.optimization_barrier(values)


def on_device(
    tokens, prefix, attn_gain, w_query, w_key, w_value, w_out, mlp_gain, w_gate, w_up, w_down, cotangent
):
    _, local_len, width = tokens.shape
    groups, context, halves = lax.axis_size("fsdp"), lax.axis_size("ctx"), lax.axis_size("tp")
    own_len = local_len // halves
    full_len = local_len * context
    query_cols = w_query.shape[1]
    kv_heads = w_key.shape[1] // HD
    copies = context // kv_heads
    heads = query_cols // HD // context
    group_cols = (heads + 2) * HD
    hidden_cols = w_gate.shape[1] // 4
    own_start = lax.axis_index("tp") * own_len
    own = lambda values: lax.dynamic_slice_in_dim(values, own_start, own_len, 0)

    cos, sin = rope_tables(full_len)
    inputs_all = tokens.reshape(local_len, width)
    grad_out = cotangent.reshape(local_len, width)

    (
        normed_one,
        query_in,
        pair_in,
        attended,
        lse,
        heads_back,
        middle,
        normed_two,
        query_full,
        key_full,
        value_full,
        mixer_blocks,
        gate_cols,
        up_cols,
        down_blocks,
        grad_plane,
    ) = front(
        groups,
        context,
        prefix,
        inputs_all,
        attn_gain,
        mlp_gain,
        cos,
        sin,
        w_query,
        w_key,
        w_value,
        w_out,
        w_gate,
        w_up,
        w_down,
        grad_out,
    )
    heads_back = jnp.swapaxes(heads_back, 0, 1).reshape(local_len, query_cols)

    plane, _, grad_gate, grad_up, down_part, out_own, out_core, grad_normed_two = mlp(
        groups, normed_two, grad_plane, gate_cols, up_cols, down_blocks
    )
    piece = width // (groups * context)
    own_middle, branch_low, grads_in, down_in, gate_part, up_part, out_half = turn(
        groups,
        context,
        heads,
        grad_normed_two,
        middle,
        grad_out,
        mlp_gain,
        mixer_blocks,
        down_part,
        plane,
        grad_gate,
        grad_up,
        out_own,
        out_core,
    )
    out_part = dot_tn(branch_low, heads_back).astype(BF16)
    out_part, grads_in = tie(out_part, grads_in)
    scatter = lambda part: lax.psum_scatter(part, ("fsdp", "ctx"), scatter_dimension=0, tiled=True)
    out_sum = scatter(out_part)
    grad_proj, early_sums, early_pairs, _, up_in, out_in = back(
        groups,
        context,
        kv_heads,
        prefix,
        grads_in,
        cos,
        sin,
        query_in,
        pair_in,
        attended,
        lse,
        down_part,
        gate_part,
        up_part,
        down_in,
        out_half,
    )
    qkv_part = dot_tn(normed_one, grad_proj).astype(BF16)
    qkv_part, out_in, grad_proj = tie(qkv_part, out_in, grad_proj)
    qkv_sum = scatter(qkv_part)
    input_low, layer_low, units = finish(
        groups,
        context,
        grad_proj,
        own(inputs_all),
        own_middle,
        attn_gain,
        middle,
        early_sums,
        early_pairs,
        out_half,
        out_in,
        up_part,
        up_in,
        query_full,
        key_full,
        value_full,
    )
    input_grad = input_low.astype(F32)
    layer_out = layer_low
    down_grad = jnp.swapaxes(units[0], 1, 2).reshape(4 * hidden_cols, piece).astype(F32)
    wide = lambda rows: jnp.swapaxes(rows, 0, 1).reshape(piece, 4 * hidden_cols).astype(F32)
    gate_grad, up_grad = wide(units[1]), wide(units[2])
    out_grad = jnp.transpose(out_sum.astype(F32))
    qkv_grad = qkv_sum.astype(F32)

    piece_start = lax.axis_index("ctx") * piece
    rows_of = lambda weight: lax.dynamic_slice_in_dim(weight, piece_start, piece, 0).astype(F32)
    kv_cols = kv_heads * HD
    query_grad = qkv_grad[:, :query_cols]
    key_grad = qkv_grad[:, query_cols : query_cols + kv_cols]
    value_grad = qkv_grad[:, query_cols + kv_cols :]
    mlp_sum = jnp.sum(rows_of(w_gate) * gate_grad + rows_of(w_up) * up_grad, axis=1)
    attn_sum = sum(
        jnp.sum(rows_of(weight) * grad, axis=1)
        for weight, grad in ((w_query, query_grad), (w_key, key_grad), (w_value, value_grad))
    )
    gain_starts = lax.axis_index("fsdp") * (piece * context) + piece_start
    gain_of = lambda gain: lax.dynamic_slice_in_dim(gain, gain_starts, piece, 0)
    sums = lax.psum(jnp.stack([mlp_sum, attn_sum]), "tp")
    mlp_gain_grad = sums[0] / gain_of(mlp_gain)
    attn_gain_grad = sums[1] / gain_of(attn_gain)

    return (
        layer_out.reshape(tokens.shape),
        input_grad.reshape(tokens.shape),
        attn_gain_grad,
        query_grad,
        key_grad,
        value_grad,
        out_grad,
        mlp_gain_grad,
        gate_grad,
        up_grad,
        down_grad,
    )


def solution(mesh):
    rows = P("fsdp", "ctx", None)
    owned = P(("fsdp", "ctx"), "tp")
    owned_t = P("tp", ("fsdp", "ctx"))
    gain = P(("fsdp", "ctx"))
    down, up = P("fsdp", "tp"), P("tp", "fsdp")
    return jax.shard_map(
        on_device,
        mesh=mesh,
        in_specs=(rows, P("fsdp"), P(), down, down, down, up, P(), down, down, up, rows),
        out_specs=(rows, rows, gain, owned, owned, owned, owned_t, gain, owned, owned, owned_t),
        check_vma=False,
    )
```

```python
import functools
import math

import jax
import jax.numpy as jnp
from jax import lax
from jax.experimental import pallas as pl
from jax.experimental.pallas import tpu as pltpu
from jax.sharding import PartitionSpec as P

HD = 80
EPS = 1e-05
THETA = 1000000.0
MASKED = -1e30
SCALE = HD ** (-0.5)
SCALE_LOG2 = SCALE * math.log2(math.e)
BF16 = jnp.bfloat16
F32 = jnp.float32
MESH = pl.DeviceIdType.MESH


def dot(left, right):
    return jnp.dot(left, right, preferred_element_type=F32)


def dot_tn(left, right):
    return lax.dot_general(left, right, (((0,), (0,)), ((), ())), preferred_element_type=F32)


def dot_nt(left, right):
    return lax.dot_general(left, right, (((1,), (1,)), ((), ())), preferred_element_type=F32)


def rope_tables(full_len):
    half = HD // 2
    frequency = THETA ** (-(jnp.arange(half, dtype=F32) * 2.0) / HD)
    angles = jnp.arange(full_len, dtype=jnp.int32).astype(F32)[:, None] * frequency[None, :]
    cos, sin = jnp.cos(angles), jnp.sin(angles)
    return jnp.concatenate([cos, cos], axis=1), jnp.concatenate([-sin, sin], axis=1)


def swap_halves(values):
    half = HD // 2
    return jnp.concatenate([values[:, half:], values[:, :half]], axis=1)


def rotate(values, cos, sin):
    values = values.astype(F32)
    return values * cos + swap_halves(values) * sin


def rotate_back(values, cos, sin):
    return values * cos - swap_halves(values) * sin


def stack_heads(ref, rows, heads):
    return jnp.concatenate([ref[rows, h * HD : (h + 1) * HD] for h in range(heads)], axis=0)


def stack_rotated(ref, rows, heads, cos, sin):
    return jnp.concatenate(
        [rotate(ref[rows, h * HD : (h + 1) * HD], cos, sin).astype(BF16) for h in range(heads)],
        axis=0,
    )


def load_keys(pair, cos, sin, keys, values, step):
    def body(i, carry):
        rows = pl.ds(pl.multiple_of(i * step, step), step)
        keys[rows, :] = rotate(pair[rows, :HD], cos[rows, :], sin[rows, :]).astype(BF16)
        values[rows, :] = pair[rows, HD:]
        return carry

    lax.fori_loop(0, pair.shape[0] // step, body, 0)


def key_blocks(i, rows, block, full_len):
    start = i * rows
    clear = lax.div(start + 1, block)
    needed = lax.div(jnp.maximum(start + rows, full_len // 2) + block - 1, block)
    return clear, needed


def attention_sizes(full_len):
    return min(256, full_len), min(512, full_len)


def front_kernel(
    groups,
    context,
    heads,
    prefix_ref,
    tokens,
    gain_one,
    gain_two,
    cos,
    sin,
    w_query,
    w_key,
    w_value,
    w_out,
    w_gate,
    w_up,
    w_down,
    cotangent,
    normed,
    query_in,
    pair_in,
    attended,
    lse,
    heads_in,
    middle,
    normed_two,
    query_hbm,
    key_hbm,
    value_hbm,
    mixer_hbm,
    gate_hbm,
    up_hbm,
    down_hbm,
    grad_plane,
    query_w,
    key_w,
    value_w,
    mixer_w,
    query_out,
    pair_out,
    keys,
    values,
    branch_out,
    branch_in,
    gate_near,
    up_near,
    down_near,
    own_sem,
    save_sem,
    gather_send,
    gather_recv,
    relay_send,
    relay_recv,
    piece_send,
    piece_recv,
    pass_send,
    pass_recv,
    query_send,
    query_recv,
    pair_send,
    pair_recv,
    heads_send,
    heads_recv,
    ff_own,
    ff_send,
    ff_recv,
    branch_sem,
    plane_sem,
):
    ff_in, ff_out = (w_gate, w_up, w_down), (gate_hbm, up_hbm, down_hbm)
    local_len, width = tokens.shape
    full_len = local_len * context
    own_len = local_len // 2
    chips = groups // 2
    f, c, t = lax.axis_index("fsdp"), lax.axis_index("ctx"), lax.axis_index("tp")
    y, core = lax.div(f, 2), lax.rem(f, 2)
    mate = {"fsdp": y * 2 + 1 - core}
    up_y = lambda a: {"fsdp": lax.rem(y + a, chips) * 2 + core}
    source_y = lambda a: lax.rem(y + chips - a, chips) * 2 + core
    next_group = lambda k: lax.rem(f + k, groups)
    next_ctx = lambda k: lax.rem(c + k, context)
    last_ctx = lambda k: lax.rem(c + context - k, context)
    other_half = {"tp": 1 - t}

    gathered = [
        (w_query, query_w, query_hbm),
        (w_key, key_w, key_hbm),
        (w_value, value_w, value_hbm),
        (w_out, mixer_w, mixer_hbm),
    ]

    def own_shard(w):
        return pltpu.make_async_copy(gathered[w][0], gathered[w][1].at[f], own_sem.at[w])

    def piece_rows(w):
        rows = gathered[w][0].shape[0]
        piece = max(1, round(0.6 * rows / context / 16)) * 16
        return rows - piece * context, piece

    def to_chip(w, a):
        shard_rows = pl.ds(0, piece_rows(w)[0] if a else gathered[w][0].shape[0])
        return remote(
            gathered[w][0].at[shard_rows],
            gathered[w][1].at[f, shard_rows],
            gather_send.at[w, a],
            gather_recv.at[w, a],
            up_y(a) if a else mate,
        )

    def piece_of(w, at):
        straight, piece = piece_rows(w)
        return pl.ds(pl.multiple_of(straight + at * piece, 16), piece)

    def send_piece(w, a):
        rows = piece_of(w, c)
        return remote(
            gathered[w][0].at[rows], gathered[w][1].at[f, rows], piece_send.at[w, a], piece_recv.at[w, a], up_y(a)
        )

    def pass_piece(w, a, k):
        at = gathered[w][1].at[source_y(a), piece_of(w, c)]
        return remote(at, at, pass_send.at[w, a, k], pass_recv.at[w, a, k], {"ctx": next_ctx(k)})

    def relay(w, a):
        at = source_y(a)
        return pltpu.make_async_remote_copy(
            src_ref=gathered[w][1].at[at],
            dst_ref=gathered[w][1].at[at],
            send_sem=relay_send.at[w, a],
            recv_sem=relay_recv.at[w, a],
            device_id=mate,
            device_id_type=MESH,
        )

    def save(w):
        return pltpu.make_async_copy(gathered[w][1], gathered[w][2], save_sem.at[w])

    def send_all(w):
        for a in range(1, chips):
            send_piece(w, a).start()
        for a in range(1, chips):
            to_chip(w, a).start()
        to_chip(w, 0).start()
        own_shard(w).start()

    def pass_on(w):
        for a in range(1, chips):
            send_piece(w, a).wait_recv()
            for k in range(1, context):
                pass_piece(w, a, k).start()

    def arrive(w):
        for a in range(1, chips):
            to_chip(w, a).wait_recv()
            for k in range(1, context):
                pass_piece(w, a, k).wait_recv()
            relay(w, a).start()

    def complete(w):
        own_shard(w).wait()
        to_chip(w, 0).wait_recv()
        for a in range(1, chips):
            relay(w, a).wait_recv()
        save(w).start()

    def finish(w):
        for a in range(chips):
            to_chip(w, a).wait_send()
        for a in range(1, chips):
            send_piece(w, a).wait_send()
            for k in range(1, context):
                pass_piece(w, a, k).wait_send()
            relay(w, a).wait_send()
        save(w).wait()

    def send_heads(kind, k):
        out, into, send, recv = [
            (query_out, query_in, query_send, query_recv),
            (pair_out, pair_in, pair_send, pair_recv),
        ][kind]
        return pltpu.make_async_remote_copy(
            src_ref=out.at[next_ctx(k)],
            dst_ref=into.at[pl.ds(pl.multiple_of(c * local_len, local_len), local_len)],
            send_sem=send.at[k],
            recv_sem=recv.at[k],
            device_id={"ctx": next_ctx(k)},
            device_id_type=MESH,
        )

    def rows_of_ctx(at):
        return pl.ds(pl.multiple_of(at * local_len, local_len), local_len)

    def send_back(at):
        return pltpu.make_async_remote_copy(
            src_ref=attended.at[rows_of_ctx(at)],
            dst_ref=heads_in.at[c],
            send_sem=heads_send.at[at],
            recv_sem=heads_recv.at[c],
            device_id={"ctx": at},
            device_id_type=MESH,
        )

    def get_back(at):
        return pltpu.make_async_remote_copy(
            src_ref=attended.at[rows_of_ctx(at)],
            dst_ref=heads_in.at[at],
            send_sem=heads_send.at[at],
            recv_sem=heads_recv.at[at],
            device_id={"ctx": at},
            device_id_type=MESH,
        )

    def ff_parts(w, g):
        units = lax.rem(g, 2) * 2 + lax.rem(c, 2)
        if w < 2:
            cols = ff_out[w].shape[1]
            shard = width // groups
            return (
                ff_in[w].at[:, pl.ds(pl.multiple_of(units * cols, cols), cols)],
                ff_out[w].at[pl.ds(pl.multiple_of(f * shard, shard), shard)],
            )
        rows = ff_out[w].shape[1]
        return ff_in[w].at[pl.ds(pl.multiple_of(units * rows, rows), rows)], ff_out[w].at[f]

    def send_ff(w, k):
        g = next_group(k)
        source, target = ff_parts(w, g)
        return pltpu.make_async_remote_copy(
            src_ref=source,
            dst_ref=target,
            send_sem=ff_send.at[w, k],
            recv_sem=ff_recv.at[w, k],
            device_id={"fsdp": g},
            device_id_type=MESH,
        )

    def own_ff(w, out):
        source, target = ff_parts(w, f)
        near = (gate_near, up_near, down_near)[w]
        return pltpu.make_async_copy(near, target, ff_own.at[w]) if out else pltpu.make_async_copy(source, near, ff_own.at[w])

    pair_rows = lambda at_core, at_pair: pl.ds(pl.multiple_of((at_core * 2 + at_pair) * local_len, local_len), local_len)
    p = lax.rem(c, 2)
    pair_mate = {"ctx": c + 1 - 2 * p}
    plane_own = pltpu.make_async_copy(cotangent, grad_plane.at[pair_rows(core, p)], plane_sem.at[0])

    def plane_copy(i, source, rows, partner):
        return pltpu.make_async_remote_copy(
            src_ref=source,
            dst_ref=grad_plane.at[rows],
            send_sem=plane_sem.at[1 + 2 * i],
            recv_sem=plane_sem.at[2 + 2 * i],
            device_id=partner,
            device_id_type=MESH,
        )

    def plane_half(at_core, at_pair, half):
        start = ((at_core * 2 + at_pair) * 2 + half) * own_len
        return pl.ds(pl.multiple_of(start, own_len), own_len)

    got_half = grad_plane.at[plane_half(core, 1 - p, t)]
    plane_copies = [
        plane_copy(0, cotangent.at[half_rows(t, own_len)], plane_half(core, p, t), pair_mate),
        plane_copy(1, cotangent, pair_rows(core, p), mate),
        plane_copy(2, grad_plane.at[pair_rows(core, 1 - p)], pair_rows(core, 1 - p), mate),
        plane_copy(3, got_half, plane_half(core, 1 - p, t), other_half),
    ]

    barrier = pltpu.get_barrier_semaphore()
    partners = [{"fsdp": next_group(k)} for k in range(1, groups)]
    partners += [{"ctx": next_ctx(k)} for k in range(1, context)]
    partners.append(other_half)
    for partner in partners:
        pl.semaphore_signal(barrier, inc=1, device_id=partner, device_id_type=MESH)
    pl.semaphore_wait(barrier, len(partners))

    for w in range(3):
        send_all(w)
    plane_own.start()
    for copy in plane_copies[:2]:
        copy.start()
    for w in range(3):
        own_ff(w, False).start()

    step = min(128, local_len)

    def norm_rows(i, carry):
        rows = pl.ds(pl.multiple_of(i * step, step), step)
        part = tokens[rows, :].astype(F32)
        scale = lax.rsqrt(jnp.mean(part * part, axis=-1, keepdims=True) + EPS)
        normed[rows, :] = (part * scale * gain_one[...]).astype(BF16)
        return carry

    lax.fori_loop(0, local_len // step, norm_rows, 0)

    shard = width // groups

    def project(weight):
        total = None
        for g in range(groups):
            part = dot(normed[:, g * shard : (g + 1) * shard], weight[g])
            total = part if total is None else total + part
        return total.astype(BF16)

    query_cols = heads * HD
    for w in range(3):
        pass_on(w)
    arrive(0)
    complete(0)
    query = project(query_w)
    for at in range(context):
        query_out[at] = query[:, at * query_cols : (at + 1) * query_cols]
    for k in range(1, context):
        send_heads(0, k).start()
    query_in[rows_of_ctx(c), :] = query_out[c]
    for w in (1, 2):
        arrive(w)
    for w in (1, 2):
        complete(w)
    send_all(3)
    kv_heads = key_w.shape[2] // HD
    copies = context // kv_heads
    key, value = project(key_w), project(value_w)
    for at in range(context):
        head = at // copies
        pair_out[at, :, :HD] = key[:, head * HD : (head + 1) * HD]
        pair_out[at, :, HD:] = value[:, head * HD : (head + 1) * HD]
    for k in range(1, context):
        send_heads(1, k).start()
    pair_in[rows_of_ctx(c), :] = pair_out[c]

    def start_ff(w):
        for k in range(1, groups):
            send_ff(w, k).start()

    start_ff(0)
    plane_copies[0].wait_recv()
    plane_copies[3].start()

    for k in range(1, context):
        send_heads(0, k).wait_recv()
        send_heads(1, k).wait_recv()

    rows, block = attention_sizes(full_len)
    load_keys(pair_in, cos, sin, keys, values, rows)
    stacked = heads * rows
    prefix = prefix_ref[0]

    def attend_block(i, carry):
        here = pl.ds(pl.multiple_of(i * rows, rows), rows)
        queries = stack_rotated(query_in, here, heads, cos[here, :], sin[here, :])
        clear, needed = key_blocks(i, rows, block, full_len)

        def key_step(j, carry, masked):
            top, total, acc = carry
            there = pl.ds(pl.multiple_of(j * block, block), block)
            scores = dot_nt(queries, keys[there, :])
            if masked:
                key_pos = j * block + lax.broadcasted_iota(jnp.int32, (stacked, block), 1)
                query_pos = i * rows + lax.rem(lax.broadcasted_iota(jnp.int32, (stacked, 1), 0), rows)
                scores = jnp.where(key_pos < jnp.maximum(query_pos + 1, prefix), scores, MASKED)
            new_top = jnp.maximum(top, jnp.max(scores, axis=1, keepdims=True))
            factor = jnp.exp2((top - new_top) * SCALE_LOG2)
            weights = jnp.exp2(scores * SCALE_LOG2 - new_top * SCALE_LOG2)
            total = total * factor + jnp.sum(weights, axis=1, keepdims=True)
            acc = acc * factor + dot(weights.astype(BF16), values[there, :])
            return new_top, total, acc

        state = (
            jnp.full((stacked, 1), MASKED, F32),
            jnp.zeros((stacked, 1), F32),
            jnp.zeros((stacked, HD), F32),
        )
        state = lax.fori_loop(0, clear, functools.partial(key_step, masked=False), state)
        top, total, acc = lax.fori_loop(clear, needed, functools.partial(key_step, masked=True), state)
        acc = acc / total
        for h in range(heads):
            attended[here, h * HD : (h + 1) * HD] = acc[h * rows : (h + 1) * rows].astype(BF16)
        log_sum = top * SCALE_LOG2 + jnp.log2(total)
        lse[i] = jnp.transpose(jnp.broadcast_to(log_sum, (stacked, 128)))[:8]
        return carry

    per_ctx = local_len // rows
    pass_on(3)
    for w in range(3):
        own_ff(w, False).wait()
        own_ff(w, True).start()
    for w in (1, 2):
        start_ff(w)

    def attend_rows(at, carry):
        lax.fori_loop(at * per_ctx, (at + 1) * per_ctx, attend_block, 0)

        @pl.when(at != c)
        def _():
            send_back(at).start()

        @pl.when(at == c)
        def _():
            heads_in[c] = attended[rows_of_ctx(c), :]

        @pl.when(at == context // 2)
        def _():
            arrive(3)

        return carry

    lax.fori_loop(0, context, attend_rows, 0)

    def collect(at, carry):
        @pl.when(at != c)
        def _():
            get_back(at).wait_recv()
            send_back(at).wait_send()

        return carry

    lax.fori_loop(0, context, collect, 0)

    complete(3)
    plane_copies[3].wait_recv()
    plane_copies[2].start()

    def branch_rows(start, store):
        half = pl.ds(pl.multiple_of(start, own_len), own_len)
        for g in range(groups):
            total = None
            for at in range(context):
                part = dot(heads_in[at, half, :], mixer_w[g, at * query_cols : (at + 1) * query_cols, :])
                total = part if total is None else total + part
            store(g * shard, total)

    def keep_low(at, part):
        branch_out[:, at : at + shard] = part.astype(BF16)

    def keep(at, part):
        middle[:, at : at + shard] = part

    branch_rows((1 - t) * own_len, keep_low)
    branch = pltpu.make_async_remote_copy(
        src_ref=branch_out,
        dst_ref=branch_in,
        send_sem=branch_sem.at[0],
        recv_sem=branch_sem.at[1],
        device_id=other_half,
        device_id_type=MESH,
    )
    branch.start()
    branch_rows(t * own_len, keep)
    branch.wait_recv()
    part_len = min(128, own_len)

    def middle_rows(i, carry):
        at = pl.ds(pl.multiple_of(i * part_len, part_len), part_len)
        token_rows = pl.ds(pl.multiple_of(t * own_len + i * part_len, part_len), part_len)
        total = tokens[token_rows, :].astype(F32) + middle[at, :] + branch_in[at, :].astype(F32)
        middle[at, :] = total
        scale = lax.rsqrt(jnp.mean(total * total, axis=-1, keepdims=True) + EPS)
        normed_two[at, :] = (total * scale * gain_two[...]).astype(BF16)
        return carry

    lax.fori_loop(0, own_len // part_len, middle_rows, 0)
    branch.wait_send()
    for k in range(1, context):
        send_heads(0, k).wait_send()
        send_heads(1, k).wait_send()
    for w in range(4):
        finish(w)
    for w in range(3):
        for k in range(1, groups):
            send_ff(w, k).wait_recv()
            send_ff(w, k).wait_send()
        own_ff(w, True).wait()
    plane_own.wait()
    for copy in (plane_copies[0], plane_copies[3]):
        copy.wait_send()
    for copy in plane_copies[1:3]:
        copy.wait()


def front(groups, context, prefix, tokens, gain_one, gain_two, cos, sin, w_query, w_key, w_value, w_out, w_gate, w_up, w_down, cotangent):
    local_len, width = tokens.shape
    full_len = local_len * context
    own_len = local_len // 2
    query_cols = w_query.shape[1]
    heads = query_cols // HD // context
    rows, _ = attention_sizes(full_len)
    hidden = w_gate.shape[1] // 4
    anywhere = pl.BlockSpec(memory_space=pl.ANY)
    near = pl.BlockSpec(memory_space=pltpu.VMEM)
    dma = pltpu.SemaphoreType.DMA
    low = lambda *shape: jax.ShapeDtypeStruct(shape, BF16)
    low_v = lambda *shape: pltpu.VMEM(shape, BF16)
    shapes = [low(groups, *w.shape) for w in (w_query, w_key, w_value, w_out)]
    return pl.pallas_call(
        functools.partial(front_kernel, groups, context, heads),
        in_specs=[pl.BlockSpec(memory_space=pltpu.SMEM)] + [near] * 5 + [anywhere] * 7 + [near],
        out_specs=[near] * 8 + [anywhere] * 8,
        out_shape=[
            low(local_len, width),
            low(full_len, heads * HD),
            low(full_len, 2 * HD),
            low(full_len, heads * HD),
            jax.ShapeDtypeStruct((full_len // rows, 8, heads * rows), F32),
            low(context, local_len, heads * HD),
            jax.ShapeDtypeStruct((own_len, width), F32),
            low(own_len, width),
        ]
        + shapes
        + [low(width, hidden), low(width, hidden), low(groups, hidden, width // groups), low(4 * local_len, width)],
        scratch_shapes=[low_v(*shape.shape) for shape in shapes]
        + [
            low_v(context, local_len, heads * HD),
            low_v(context, local_len, 2 * HD),
            low_v(full_len, HD),
            low_v(full_len, HD),
            low_v(own_len, width),
            low_v(own_len, width),
            low_v(width // groups, hidden),
            low_v(width // groups, hidden),
            low_v(hidden, width // groups),
            dma((4,)),
            dma((4,)),
        ]
        + [dma((4, groups // 2))] * 6
        + [dma((4, groups // 2, context))] * 2
        + [dma((context,))] * 6
        + [dma((3,)), dma((3, groups)), dma((3, groups)), dma((2,)), dma((9,))],
        compiler_params=pltpu.CompilerParams(
            collective_id=1, has_side_effects=True, vmem_limit_bytes=60 * 1024 * 1024
        ),
        cost_estimate=pl.CostEstimate(
            flops=local_len * width * query_cols * 6, bytes_accessed=local_len * width * 40, transcendentals=full_len * full_len
        ),
        name="front",
    )(
        prefix,
        tokens,
        gain_one.reshape(1, width),
        gain_two.reshape(1, width),
        cos,
        sin,
        w_query,
        w_key,
        w_value,
        w_out,
        w_gate,
        w_up,
        w_down,
        cotangent,
    )


def product(left, right, result, side, columns_in, columns_out, side_sem, columns_sem, columns_store):
    whole = pltpu.make_async_copy(right, side, side_sem)
    whole.start()
    tile = columns_in.shape[2]
    tiles = left.shape[1] // tile

    def load(i):
        at = pl.ds(pl.multiple_of(i * tile, tile), tile)
        return pltpu.make_async_copy(left.at[:, at], columns_in.at[lax.rem(i, 2)], columns_sem.at[lax.rem(i, 2)])

    def store(i):
        at = pl.ds(pl.multiple_of(i * tile, tile), tile)
        return pltpu.make_async_copy(columns_out, result.at[at], columns_store.at[0])

    load(0).start()
    whole.wait()

    def body(i, carry):
        load(i).wait()

        @pl.when(i + 1 < tiles)
        def _():
            load(i + 1).start()

        made = dot_tn(columns_in[lax.rem(i, 2)], side[...]).astype(BF16)

        @pl.when(i > 0)
        def _():
            store(i - 1).wait()

        columns_out[...] = made
        store(i).start()
        return carry

    lax.fori_loop(0, tiles, body, 0)
    store(tiles - 1).wait()


def mlp_kernel(
    groups,
    normed,
    cotangent,
    gate_hbm,
    up_hbm,
    down_hbm,
    plane,
    hidden_out,
    grad_gate_out,
    grad_up_out,
    down_part,
    gate_part,
    out_own,
    out_core,
    total_out,
    gate_w,
    up_w,
    down_w,
    rows_in,
    grad_in,
    hidden_s,
    grad_gate_s,
    grad_up_s,
    part,
    to_core,
    from_core,
    to_chip,
    from_chip,
    columns_in,
    columns_out,
    load_sem,
    rows_sem,
    grad_sem,
    store_sem,
    columns_sem,
    columns_store,
    out_low,
    out_store,
    out_send,
    out_recv,
    row_send,
    row_recv,
    relay_send,
    relay_recv,
    core_send,
    core_recv,
    chip_send,
    chip_recv,
):
    own_len, width = normed.shape
    chips = 4
    f, c, t = lax.axis_index("fsdp"), lax.axis_index("ctx"), lax.axis_index("tp")
    core, p = lax.rem(f, 2), lax.rem(c, 2)

    def chip_at(step):
        a, b = lax.div(step, 2), lax.rem(step, 2)
        return lax.rem(p + a, 2), lax.rem(t + b, 2)

    def device(at, at_core):
        return {"fsdp": f - core + at_core, "ctx": c - p + at[0], "tp": at[1]}

    def rows_of(at, at_core):
        slot = (at_core * 2 + at[0]) * 2 + at[1]
        return pl.ds(pl.multiple_of(slot * own_len, own_len), own_len)

    here = (p, t)
    mate = {"fsdp": f + 1 - 2 * core}
    mine = rows_of(here, core)

    def remote(source, target, send, recv, partner):
        return pltpu.make_async_remote_copy(
            src_ref=source, dst_ref=target, send_sem=send, recv_sem=recv, device_id=partner, device_id_type=MESH
        )

    def send_rows(step):
        return remote(normed, plane.at[mine], row_send.at[step], row_recv.at[step], device(chip_at(step), core))

    def relay(step, source):
        rows = rows_of(chip_at(step), core)
        return remote(source, plane.at[rows], relay_send.at[step], relay_recv.at[step], mate)

    def send_part(step):
        return remote(to_core.at[step], from_core.at[step], core_send.at[step], core_recv.at[step], mate)

    def send_sum(step):
        return remote(
            to_chip.at[step], from_chip.at[step], chip_send.at[step], chip_recv.at[step], device(chip_at(step), core)
        )

    greet([mate] + [device(chip_at(step), core) for step in range(1, chips)])

    for step in (1, 2):
        send_rows(step).start()
    relay(0, normed).start()
    own_copy = pltpu.make_async_copy(normed, plane.at[mine], load_sem.at[3])
    own_copy.start()
    weights = [
        pltpu.make_async_copy(gate_hbm, gate_w, load_sem.at[0]),
        pltpu.make_async_copy(up_hbm, up_w, load_sem.at[1]),
        pltpu.make_async_copy(down_hbm, down_w, load_sem.at[2]),
    ]
    for copy in weights:
        copy.start()

    def block_rows(index):
        same = 1 - lax.rem(index, 2)
        return rows_of(chip_at(lax.div(index, 2)), lax.rem(core + 1 - same, 2))

    def load_rows(index):
        slot = lax.rem(index, 2)
        return pltpu.make_async_copy(plane.at[block_rows(index)], rows_in.at[slot], rows_sem.at[slot])

    def load_grad(index):
        slot = lax.rem(index, 2)
        return pltpu.make_async_copy(cotangent.at[block_rows(index)], grad_in.at[slot], grad_sem.at[slot])

    load_grad(0).start()
    own_copy.wait()
    load_rows(0).start()
    for copy in weights:
        copy.wait()

    def stores(index):
        rows = block_rows(index)
        return [
            pltpu.make_async_copy(hidden_s, hidden_out.at[rows], store_sem.at[0]),
            pltpu.make_async_copy(grad_gate_s, grad_gate_out.at[rows], store_sem.at[1]),
            pltpu.make_async_copy(grad_up_s, grad_up_out.at[rows], store_sem.at[2]),
        ]

    def keep_out(step):
        return pltpu.make_async_copy(out_low.at[0], out_own.at[step], out_store.at[0])

    def send_out(step):
        return remote(out_low.at[1], out_core.at[step], out_send.at[step], out_recv.at[step], mate)

    def block(index, result):
        slot = lax.rem(index, 2)
        load_grad(index).wait()

        @pl.when(index + 1 < 2 * chips)
        def _():
            load_grad(index + 1).start()

        load_rows(index).wait()
        gate = dot(rows_in[slot], gate_w[...])
        up = dot(rows_in[slot], up_w[...])
        shard = width // groups
        grad_hidden = sum(dot_nt(grad_in[slot, :, g * shard : (g + 1) * shard], down_w[g]) for g in range(groups))
        sigmoid = 1.0 / (1.0 + jnp.exp(-gate))
        silu = gate * sigmoid

        @pl.when(index > 0)
        def _():
            for copy in stores(index - 1):
                copy.wait()

        hidden_s[...] = (silu * up).astype(BF16)
        grad_up_s[...] = (grad_hidden * silu).astype(BF16)
        grad_gate_s[...] = (grad_hidden * up * sigmoid * (1.0 + gate * (1.0 - sigmoid))).astype(BF16)
        for copy in stores(index):
            copy.start()

        @pl.when((index > 1) & (slot == 0))
        def _():
            keep_out(lax.div(index, 2) - 1).wait()

        @pl.when((index > 1) & (slot == 1))
        def _():
            send_out(lax.div(index, 2) - 1).wait_send()

        for g in range(groups):
            out_low[slot, :, g * shard : (g + 1) * shard] = dot(hidden_s[...], down_w[g]).astype(BF16)

        @pl.when(slot == 0)
        def _():
            keep_out(lax.div(index, 2)).start()

        @pl.when(slot == 1)
        def _():
            send_out(lax.div(index, 2)).start()

        tile = 512 if width % 512 == 0 else width
        for at in range(0, width, tile):
            result[:, at : at + tile] = (
                dot_nt(grad_gate_s[...], gate_w[at : at + tile, :]) + dot_nt(grad_up_s[...], up_w[at : at + tile, :])
            ).astype(BF16)

    def pair(step, carry):
        @pl.when(step > 0)
        def _():
            send_rows(step).wait_recv()
            relay(step, plane.at[rows_of(chip_at(step), core)]).start()
            load_rows(2 * step).start()

        @pl.when(step == 1)
        def _():
            send_rows(3).start()

        block(2 * step, part)
        relay(step, normed).wait_recv()
        load_rows(2 * step + 1).start()
        block(2 * step + 1, to_core.at[step])
        send_part(step).start()
        send_part(step).wait_recv()

        @pl.when(step == 0)
        def _():
            total_out[...] = part[...].astype(F32) + from_core[step].astype(F32)

        @pl.when(step > 0)
        def _():
            to_chip[step] = (part[...].astype(F32) + from_core[step].astype(F32)).astype(BF16)
            send_sum(step).start()

        return carry

    lax.fori_loop(0, chips, pair, 0)
    for copy in stores(2 * chips - 1):
        copy.wait()

    side = gate_w.at[pl.ds(0, columns_in.shape[1])]
    product(cotangent, hidden_out, down_part, side, columns_in, columns_out, load_sem.at[0], columns_sem, columns_store)
    product(plane, grad_gate_out, gate_part, side, columns_in, columns_out, load_sem.at[0], columns_sem, columns_store)

    def collect(step, carry):
        send_sum(step).wait_recv()
        total_out[...] += from_chip[step].astype(F32)
        send_sum(step).wait_send()
        send_rows(step).wait_send()
        return carry

    lax.fori_loop(1, chips, collect, 0)

    keep_out(chips - 1).wait()
    send_out(chips - 1).wait_send()

    def drain(step, carry):
        relay(step, normed).wait_send()
        send_part(step).wait_send()
        send_out(step).wait_recv()
        return carry

    lax.fori_loop(0, chips, drain, 0)


def mlp(groups, normed, cotangent, gate_cols, up_cols, down_rows):
    own_len, width = normed.shape
    hidden = gate_cols.shape[1]
    chips = 4
    plane_len = own_len * 2 * chips
    tile = 512 if width % 512 == 0 else width
    anywhere = pl.BlockSpec(memory_space=pl.ANY)
    dma = pltpu.SemaphoreType.DMA
    low = lambda *shape: pltpu.VMEM(shape, BF16)
    return pl.pallas_call(
        functools.partial(mlp_kernel, groups),
        in_specs=[pl.BlockSpec(memory_space=pltpu.VMEM)] + [anywhere] * 4,
        out_specs=[anywhere] * 8 + [pl.BlockSpec(memory_space=pltpu.VMEM)],
        out_shape=[
            jax.ShapeDtypeStruct((plane_len, width), BF16),
            jax.ShapeDtypeStruct((plane_len, hidden), BF16),
            jax.ShapeDtypeStruct((plane_len, hidden), BF16),
            jax.ShapeDtypeStruct((plane_len, hidden), BF16),
            jax.ShapeDtypeStruct((width, hidden), BF16),
            jax.ShapeDtypeStruct((width, hidden), BF16),
            jax.ShapeDtypeStruct((chips, own_len, width), BF16),
            jax.ShapeDtypeStruct((chips, own_len, width), BF16),
            jax.ShapeDtypeStruct((own_len, width), F32),
        ],
        scratch_shapes=[
            low(width, hidden),
            low(width, hidden),
            low(groups, hidden, width // groups),
            low(2, own_len, width),
            low(2, own_len, width),
            low(own_len, hidden),
            low(own_len, hidden),
            low(own_len, hidden),
            low(own_len, width),
            low(chips, own_len, width),
            low(chips, own_len, width),
            low(chips, own_len, width),
            low(chips, own_len, width),
            low(2, plane_len, tile),
            low(tile, hidden),
            dma((4,)),
            dma((2,)),
            dma((2,)),
            dma((3,)),
            dma((2,)),
            dma((1,)),
            low(2, own_len, width),
            dma((1,)),
        ]
        + [dma((chips,))] * 10,
        compiler_params=pltpu.CompilerParams(
            collective_id=3, has_side_effects=True, vmem_limit_bytes=60 * 1024 * 1024
        ),
        cost_estimate=pl.CostEstimate(
            flops=plane_len * width * hidden * 10, bytes_accessed=plane_len * width * 8, transcendentals=plane_len * hidden
        ),
        name="mlp",
    )(normed, cotangent, gate_cols, up_cols, down_rows)


def remote(source, target, send, recv, partner):
    return pltpu.make_async_remote_copy(
        src_ref=source, dst_ref=target, send_sem=send, recv_sem=recv, device_id=partner, device_id_type=MESH
    )


def greet(partners):
    barrier = pltpu.get_barrier_semaphore()
    for partner in partners:
        pl.semaphore_signal(barrier, inc=1, device_id=partner, device_id_type=MESH)
    pl.semaphore_wait(barrier, len(partners))


def half_rows(half, own_len):
    return pl.ds(pl.multiple_of(half * own_len, own_len), own_len)


def ctx_rows(at, local_len):
    return pl.ds(pl.multiple_of(at * local_len, local_len), local_len)


def chip_part(part, chip_in, send, recv, a, groups):
    f = lax.axis_index("fsdp")
    chips = groups // 2
    rows = part.shape[0] // chips
    to = lax.rem(lax.div(f, 2) + a, chips)
    return remote(
        part.at[pl.ds(pl.multiple_of(to * rows, rows), rows)],
        chip_in.at[a - 1],
        send.at[a],
        recv.at[a],
        {"fsdp": to * 2 + lax.rem(f, 2)},
    )


def add_chips(part, chip_in, sums, own, other, sem, groups, context):
    chips, pairs = groups // 2, context // 2
    rows = part.shape[0] // chips
    unit = rows // context
    y = lax.div(lax.axis_index("fsdp"), 2)

    def loads(i):
        slot = lax.rem(i, 2)
        mine = pl.ds(pl.multiple_of(y * rows + i * unit, unit), unit)
        at = pl.ds(pl.multiple_of(i * unit, unit), unit)
        copies = [pltpu.make_async_copy(part.at[mine], own.at[slot], sem.at[0, slot])]
        for a in range(1, chips):
            copies.append(pltpu.make_async_copy(chip_in.at[a - 1, at], other.at[slot, a - 1], sem.at[a, slot]))
        return copies

    for copy in loads(0):
        copy.start()

    def body(i, carry):
        slot = lax.rem(i, 2)

        @pl.when(i + 1 < context)
        def _():
            for copy in loads(i + 1):
                copy.start()

        for copy in loads(i):
            copy.wait()
        made = own[slot].astype(F32)
        for a in range(1, chips):
            made = made + other[slot, a - 1].astype(F32)
        sums[lax.rem(i, pairs), lax.div(i, pairs)] = made.astype(BF16)
        return carry

    lax.fori_loop(0, context, body, 0)


def pair_part(sums, pair_in, send, recv, b, context):
    c = lax.axis_index("ctx")
    to = lax.rem(lax.div(c, 2) + b, context // 2)
    return remote(sums.at[to], pair_in.at[b - 1], send.at[b], recv.at[b], {"ctx": to * 2 + lax.rem(c, 2)})


def token_product(left, right, at_core, result, groups):
    shard = left.shape[1] // groups
    columns = right.shape[1]
    tile = 640 if columns % 640 == 0 else columns
    for own in range(2):

        @pl.when(at_core == own)
        def _():
            for y in range(groups // 2):
                at = (y * 2 + own) * shard
                for n in range(0, columns, tile):
                    result[y, :, n : n + tile] = dot_tn(left[:, at : at + shard], right[:, n : n + tile]).astype(BF16)


def add_rows(left, right, result):
    rows = left.shape[0]
    step = 160 if rows % 160 == 0 else rows

    def body(i, carry):
        at = pl.ds(pl.multiple_of(i * step, step), step)
        result[at, :] = (left[at, :].astype(F32) + right[at, :].astype(F32)).astype(BF16)
        return carry

    lax.fori_loop(0, rows // step, body, 0)


def turn_kernel(
    groups,
    context,
    heads,
    total,
    middle,
    cotangent,
    gain,
    mixer_hbm,
    down_part,
    plane,
    grad_up,
    out_own,
    out_core,
    heads_back,
    own_middle,
    branch_low,
    grads_in,
    mixer_sums,
    chip_in,
    up_part,
    out_half,
    mixer_w,
    heads_out,
    side,
    columns_in,
    columns_out,
    out_rows,
    heads_all,
    mixer_part,
    core_sem,
    side_sem,
    columns_sem,
    columns_store,
    out_sem,
    mixer_sem,
    branch_send,
    branch_recv,
    heads_send,
    heads_recv,
    chip_send,
    chip_recv,
):
    own_len, width = total.shape
    local_len = own_len * 2
    shard = width // groups
    query_cols = heads * HD
    chips = groups // 2
    f, c, t = lax.axis_index("fsdp"), lax.axis_index("ctx"), lax.axis_index("tp")
    next_ctx = lambda k: lax.rem(c + k, context)
    next_chip = lambda a: {"fsdp": lax.rem(lax.div(f, 2) + a, chips) * 2 + lax.rem(f, 2)}
    core = lax.rem(f, 2)
    mate = {"fsdp": f + 1 - 2 * core}
    greet(
        [{"ctx": next_ctx(k)} for k in range(1, context)]
        + [{"tp": 1 - t}, mate]
        + [next_chip(a) for a in range(1, chips)]
    )

    send_chip = lambda a: chip_part(down_part, chip_in, chip_send, chip_recv, a, groups)
    for a in range(1, chips):
        send_chip(a).start()
    mixer = pltpu.make_async_copy(mixer_hbm, mixer_w, mixer_sem.at[0])
    mixer.start()

    step = min(128, own_len)
    steps = own_len // step

    def part_rows(half, i):
        return pl.ds(pl.multiple_of(half * own_len + i * step, step), step)

    def branch(half, i):
        rows = part_rows(half, i)
        return remote(branch_low.at[rows], branch_low.at[rows], branch_send.at[i], branch_recv.at[i], {"tp": 1 - t})

    def norm_back(i, carry):
        at = pl.ds(pl.multiple_of(i * step, step), step)
        rows = part_rows(t, i)
        part = middle[at, :]
        inner = total[at, :] * gain[...]
        mixed = jnp.mean(inner * part, axis=-1, keepdims=True)
        scale = lax.rsqrt(jnp.mean(part * part, axis=-1, keepdims=True) + EPS)
        grad = cotangent[rows, :].astype(F32) + scale * inner - part * (scale * scale * scale * mixed)
        own_middle[at, :] = grad
        branch_low[rows, :] = grad.astype(BF16)
        branch(t, i).start()
        return carry

    lax.fori_loop(0, steps, norm_back, 0)
    mixer.wait()

    def send_grads(half, k, order):
        return remote(
            heads_out.at[next_ctx(k), half_rows(half, own_len)],
            grads_in.at[pl.ds(pl.multiple_of(c * local_len + half * own_len, own_len), own_len)],
            heads_send.at[k, order],
            heads_recv.at[k, order],
            {"ctx": next_ctx(k)},
        )

    for at in range(context):
        heads_all[:, at * query_cols : (at + 1) * query_cols] = heads_back[at]
    send_core = remote(mixer_part, mixer_sums, core_sem.at[0], core_sem.at[1], mate)

    def add_cores():
        p = lax.rem(c, 2)

        def body(step, carry):
            loads = [
                pltpu.make_async_copy(out_own.at[step], out_rows.at[0], out_sem.at[0]),
                pltpu.make_async_copy(out_core.at[step], out_rows.at[1], out_sem.at[1]),
            ]
            for copy in loads:
                copy.start()
            for copy in loads:
                copy.wait()
            out_rows[0] = (out_rows[0].astype(F32) + out_rows[1].astype(F32)).astype(BF16)
            slot = lax.rem(p + lax.div(step, 2), 2) * 2 + lax.rem(t + lax.rem(step, 2), 2)
            store = pltpu.make_async_copy(out_rows.at[0], out_half.at[slot], out_sem.at[2])
            store.start()
            store.wait()
            return carry

        lax.fori_loop(0, out_own.shape[0], body, 0)

    def both_parts(order, carry):
        half = jnp.where(order == 0, t, 1 - t)

        def one(i, inner):
            @pl.when(order == 1)
            def _():
                branch(1 - t, i).wait_recv()

            rows = part_rows(half, i)
            grad = sum(dot_nt(branch_low[rows, g * shard : (g + 1) * shard], mixer_w[g]) for g in range(groups))
            for at in range(context):
                heads_out[at, rows, :] = grad[:, at * query_cols : (at + 1) * query_cols].astype(BF16)
            return inner

        lax.fori_loop(0, steps, one, 0)
        for k in range(1, context):
            send_grads(half, k, order).start()
        grads_in[pl.ds(pl.multiple_of(c * local_len + half * own_len, own_len), own_len), :] = heads_out[
            c, half_rows(half, own_len), :
        ]

        @pl.when(order == 0)
        def _():
            product(plane, grad_up, up_part, side, columns_in, columns_out, side_sem.at[0], columns_sem, columns_store)

        @pl.when(order == 1)
        def _():
            token_product(branch_low, heads_all, 1 - core, mixer_part, groups)
            send_core.start()
            add_cores()
            send_core.wait()
            token_product(branch_low, heads_all, core, mixer_part, groups)
            for at in range(chips):
                add_rows(mixer_part.at[at], mixer_sums.at[at], mixer_sums.at[at])

        return carry

    lax.fori_loop(0, 2, both_parts, 0)
    for order, half in enumerate((t, 1 - t)):
        for k in range(1, context):
            send_grads(half, k, order).wait()
    for i in range(steps):
        branch(t, i).wait_send()
    for a in range(1, chips):
        send_chip(a).wait()


def turn(groups, context, heads, total, middle, cotangent, gain, mixer, down_part, plane, grad_up, out_own, out_core, heads_back):
    own_len, width = total.shape
    local_len = own_len * 2
    chips = groups // 2
    hidden = down_part.shape[1]
    steps = own_len // min(128, own_len)
    tile = 512 if width % 512 == 0 else width
    anywhere = pl.BlockSpec(memory_space=pl.ANY)
    near = pl.BlockSpec(memory_space=pltpu.VMEM)
    dma = pltpu.SemaphoreType.DMA
    low = lambda *shape: jax.ShapeDtypeStruct(shape, BF16)
    low_v = lambda *shape: pltpu.VMEM(shape, BF16)
    return pl.pallas_call(
        functools.partial(turn_kernel, groups, context, heads),
        in_specs=[near] * 4 + [anywhere] * 6 + [near],
        out_specs=[near] * 4 + [anywhere] * 3,
        out_shape=[
            jax.ShapeDtypeStruct((own_len, width), F32),
            low(local_len, width),
            low(local_len * context, heads * HD),
            low(chips, width // groups, context * heads * HD),
            low(chips - 1, width // chips, hidden),
            low(*down_part.shape),
            low(*out_own.shape),
        ],
        scratch_shapes=[
            low_v(*mixer.shape),
            low_v(context, local_len, heads * HD),
            low_v(*grad_up.shape),
            low_v(2, plane.shape[0], tile),
            low_v(tile, hidden),
            low_v(2, own_len, width),
            low_v(local_len, context * heads * HD),
            low_v(chips, width // groups, context * heads * HD),
            dma((2,)),
            dma((1,)),
            dma((2,)),
            dma((1,)),
            dma((3,)),
            dma((1,)),
            dma((steps,)),
            dma((steps,)),
            dma((context, 2)),
            dma((context, 2)),
            dma((chips,)),
            dma((chips,)),
        ],
        compiler_params=pltpu.CompilerParams(collective_id=4, has_side_effects=True, vmem_limit_bytes=60 * 1024 * 1024),
        cost_estimate=pl.CostEstimate(
            flops=local_len * width * heads * HD * context * 2, bytes_accessed=local_len * width * 20, transcendentals=0
        ),
        name="turn",
    )(
        total, middle, cotangent, gain.reshape(1, width), mixer, down_part, plane, grad_up, out_own, out_core, heads_back
    )


def back_kernel(
    groups,
    context,
    heads,
    prefix_ref,
    grads_in,
    cos,
    sin,
    query_in,
    pair_in,
    attended,
    lse,
    middle,
    down_part,
    gate_part,
    up_part,
    down_in,
    out_half,
    mixer_sums,
    grad_proj,
    sums,
    pair_sums,
    layer_low,
    gate_in,
    up_in,
    out_in,
    mixer_in,
    query_back,
    pair_back,
    keys,
    values,
    grad_keys,
    grad_values,
    query_out,
    pair_out,
    sum_own,
    sum_other,
    query_send,
    query_recv,
    pair_send,
    pair_recv,
    sum_sem,
    chip_send,
    chip_recv,
    pairs_send,
    pairs_recv,
    half_send,
    half_recv,
    mixer_send,
    mixer_recv,
    half_own,
    half_other,
    pair_rows_out,
    pair_rows_in,
    rows_sem,
    pair_rows_sem,
    layer_send,
    layer_recv,
):
    full_len, query_cols = query_in.shape
    local_len = full_len // context
    chips, pairs = groups // 2, context // 2
    f, c, t = lax.axis_index("fsdp"), lax.axis_index("ctx"), lax.axis_index("tp")
    next_chip = lambda a: {"fsdp": lax.rem(lax.div(f, 2) + a, chips) * 2 + lax.rem(f, 2)}
    greet(
        [{"ctx": lax.rem(c + k, context)} for k in range(1, context)]
        + [{"tp": 1 - t}]
        + [next_chip(a) for a in range(1, chips)]
    )

    p = lax.rem(c, 2)
    own_len, width = middle.shape

    later = ((gate_part, gate_in), (up_part, up_in))

    def send_chip(w, a):
        return chip_part(*later[w], chip_send.at[w], chip_recv.at[w], a, groups)

    def send_pair(w, b):
        return pair_part(sums.at[w], pair_sums.at[w], pairs_send.at[w], pairs_recv.at[w], b, context)

    def add_part(w, part, chip_in):
        add_chips(part, chip_in, sums.at[w], sum_own, sum_other, sum_sem, groups, context)
        for b in range(1, pairs):
            send_pair(w, b).start()

    def send_mixer(a):
        to = lax.rem(lax.div(f, 2) + a, chips)
        return remote(mixer_sums.at[to], mixer_in.at[a - 1], mixer_send.at[a], mixer_recv.at[a], next_chip(a))

    def send_half(p):
        return remote(out_half.at[p * 2 + 1 - t], out_in.at[p], half_send.at[p], half_recv.at[p], {"tp": 1 - t})

    for a in range(1, chips):
        send_chip(0, a).start()
    for at in range(2):
        send_half(at).start()
    add_part(0, down_part, down_in)

    rows, block = attention_sizes(full_len)
    load_keys(pair_in, cos, sin, keys, values, rows)
    grad_keys[...] = jnp.zeros_like(grad_keys)
    grad_values[...] = jnp.zeros_like(grad_values)
    stacked = heads * rows
    prefix = prefix_ref[0]

    def attend_block(i):
        here = pl.ds(pl.multiple_of(i * rows, rows), rows)
        cos_here, sin_here = cos[here, :], sin[here, :]
        queries = stack_rotated(query_in, here, heads, cos_here, sin_here)
        grads = stack_heads(grads_in, here, heads)
        outs = stack_heads(attended, here, heads)
        row_dot = lax.dot_general(
            jnp.ones((8, HD), F32),
            grads.astype(F32) * outs.astype(F32),
            (((1,), (1,)), ((), ())),
            precision=lax.Precision.HIGHEST,
            preferred_element_type=F32,
        )[:1]
        log_sum = lse[i][:1]
        clear, needed = key_blocks(i, rows, block, full_len)

        def key_step(j, grad_queries, masked):
            there = pl.ds(pl.multiple_of(j * block, block), block)
            key_part = keys[there, :]
            probs = jnp.exp2(dot_nt(key_part, queries) * SCALE_LOG2 - log_sum)
            if masked:
                key_pos = j * block + lax.broadcasted_iota(jnp.int32, (block, stacked), 0)
                query_pos = i * rows + lax.rem(lax.broadcasted_iota(jnp.int32, (1, stacked), 1), rows)
                probs = jnp.where(key_pos < jnp.maximum(query_pos + 1, prefix), probs, 0.0)
            grad_probs = dot_nt(values[there, :], grads)
            grad_scores = (probs * (grad_probs - row_dot)).astype(BF16)
            grad_values[there, :] += dot(probs.astype(BF16), grads)
            grad_keys[there, :] += dot(grad_scores, queries)
            return grad_queries + dot_tn(grad_scores, key_part)

        grad_queries = jnp.zeros((stacked, HD), F32)
        grad_queries = lax.fori_loop(0, clear, functools.partial(key_step, masked=False), grad_queries)
        grad_queries = lax.fori_loop(clear, needed, functools.partial(key_step, masked=True), grad_queries)
        for h in range(heads):
            part = grad_queries[h * rows : (h + 1) * rows] * SCALE
            query_out[here, h * HD : (h + 1) * HD] = rotate_back(part, cos_here, sin_here).astype(BF16)

    per_ctx = local_len // rows

    def load_half(at):
        return [
            pltpu.make_async_copy(out_half.at[at * 2 + t], half_own, rows_sem.at[0]),
            pltpu.make_async_copy(out_in.at[at], half_other, rows_sem.at[1]),
        ]

    send_rows = remote(pair_rows_out, pair_rows_in, pair_rows_sem.at[0], pair_rows_sem.at[1], {"ctx": c + 1 - 2 * p})

    def pass_half():
        for at in range(2):
            send_half(at).wait()
        for copy in load_half(1 - p):
            copy.start()
        for copy in load_half(1 - p):
            copy.wait()
        pair_rows_out[...] = (half_own[...].astype(F32) + half_other[...].astype(F32)).astype(BF16)
        send_rows.start()
        for copy in load_half(p):
            copy.start()

    part_len = min(128, own_len)
    parts_of_rows = own_len // part_len

    def send_layer(half, i):
        at = pl.ds(pl.multiple_of(half * own_len + i * part_len, part_len), part_len)
        return remote(layer_low.at[at], layer_low.at[at], layer_send.at[i], layer_recv.at[i], {"tp": 1 - t})

    def layer_rows(i, carry):
        at = pl.ds(pl.multiple_of(i * part_len, part_len), part_len)
        made = middle[at, :] + (half_own[at, :].astype(F32) + half_other[at, :].astype(F32) + pair_rows_in[at, :].astype(F32))
        layer_low[pl.ds(pl.multiple_of(t * own_len + i * part_len, part_len), part_len), :] = made.astype(BF16)
        send_layer(t, i).start()
        return carry

    def send_query(at, source):
        return remote(
            query_out.at[ctx_rows(at, local_len)], query_back.at[source], query_send.at[at], query_recv.at[source], {"ctx": at}
        )

    def send_pair_grads(at, source):
        return remote(
            pair_out.at[ctx_rows(at, local_len)], pair_back.at[source], pair_send.at[at], pair_recv.at[source], {"ctx": at}
        )

    def finish_pair(at, carry):
        def body(i, inner):
            at_rows = pl.ds(pl.multiple_of(at * local_len + i * rows, rows), rows)
            part = grad_keys[at_rows, :] * SCALE
            pair_out[at_rows, :HD] = rotate_back(part, cos[at_rows, :], sin[at_rows, :]).astype(BF16)
            pair_out[at_rows, HD:] = grad_values[at_rows, :].astype(BF16)
            return inner

        lax.fori_loop(0, per_ctx, body, 0)

        @pl.when(at != c)
        def _():
            send_pair_grads(at, c).start()

        @pl.when(at == c)
        def _():
            pair_back[c] = pair_out[ctx_rows(c, local_len), :]

        return carry

    def attend_rows(order, carry):
        at = context - 1 - order

        def body(i, inner):
            attend_block(at * per_ctx + per_ctx - 1 - i)
            return inner

        lax.fori_loop(0, per_ctx, body, 0)

        @pl.when(at != c)
        def _():
            send_query(at, c).start()

        @pl.when(at == c)
        def _():
            query_back[c] = query_out[ctx_rows(c, local_len), :]

        @pl.when(order == context // 2 - 1)
        def _():
            for a in range(1, chips):
                send_chip(0, a).wait()
                send_chip(1, a).start()
                send_mixer(a).start()
            add_part(1, gate_part, gate_in)

        @pl.when(order == context // 2)
        def _():
            pass_half()

        @pl.when(order == context // 2 - 1)
        def _():
            lax.fori_loop(context // 2, context, finish_pair, 0)

        return carry

    lax.fori_loop(0, context, attend_rows, 0)
    lax.fori_loop(0, context // 2, finish_pair, 0)
    for copy in load_half(p):
        copy.wait()
    send_rows.wait()
    lax.fori_loop(0, parts_of_rows, layer_rows, 0)

    def collect(at, carry):
        @pl.when(at != c)
        def _():
            send_query(at, at).wait()
            send_pair_grads(at, at).wait()

        return carry

    lax.fori_loop(0, context, collect, 0)

    kv_heads = (grad_proj.shape[1] // HD - heads * context) // 2
    copies = context // kv_heads
    key_at = context * query_cols
    value_at = key_at + kv_heads * HD
    for at in range(context):
        grad_proj[:, at * query_cols : (at + 1) * query_cols] = query_back[at]
    for head in range(kv_heads):
        pair = sum(pair_back[head * copies + i].astype(F32) for i in range(copies)).astype(BF16)
        grad_proj[:, key_at + head * HD : key_at + (head + 1) * HD] = pair[:, :HD]
        grad_proj[:, value_at + head * HD : value_at + (head + 1) * HD] = pair[:, HD:]

    for a in range(1, chips):
        send_mixer(a).wait()
        send_chip(1, a).wait()
    for i in range(parts_of_rows):
        send_layer(t, i).wait_send()
        send_layer(1 - t, i).wait_recv()
    for w in range(2):
        for b in range(1, pairs):
            send_pair(w, b).wait()


def back(
    groups, context, kv_heads, prefix, grads_in, cos, sin, query_in, pair_in, attended, lse, middle, down_part, gate_part, up_part, down_in, out_half, mixer_sums
):
    full_len, query_cols = query_in.shape
    local_len = full_len // context
    heads = query_cols // HD
    width, hidden = up_part.shape
    own_len = middle.shape[0]
    steps = own_len // min(128, own_len)
    chips, pairs = groups // 2, context // 2
    unit = width // (chips * context)
    anywhere = pl.BlockSpec(memory_space=pl.ANY)
    near = pl.BlockSpec(memory_space=pltpu.VMEM)
    dma = pltpu.SemaphoreType.DMA
    low = lambda *shape: jax.ShapeDtypeStruct(shape, BF16)
    low_v = lambda *shape: pltpu.VMEM(shape, BF16)
    return pl.pallas_call(
        functools.partial(back_kernel, groups, context, heads),
        in_specs=[pl.BlockSpec(memory_space=pltpu.SMEM)] + [near] * 8 + [anywhere] * 6,
        out_specs=[near] * 4 + [anywhere] * 4,
        out_shape=[
            low(local_len, context * query_cols + 2 * kv_heads * HD),
            low(2, pairs, 2, unit, hidden),
            low(2, pairs - 1, 2, unit, hidden),
            low(2 * own_len, width),
            low(chips - 1, width // chips, hidden),
            low(chips - 1, width // chips, hidden),
            low(2, *out_half.shape[1:]),
            low(chips - 1, *mixer_sums.shape[1:]),
        ],
        scratch_shapes=[
            low_v(context, local_len, query_cols),
            low_v(context, local_len, 2 * HD),
            low_v(full_len, HD),
            low_v(full_len, HD),
            pltpu.VMEM((full_len, HD), F32),
            pltpu.VMEM((full_len, HD), F32),
            low_v(full_len, query_cols),
            low_v(full_len, 2 * HD),
            low_v(2, unit, hidden),
            low_v(2, chips - 1, unit, hidden),
        ]
        + [dma((context,))] * 4
        + [
            dma((chips, 2)),
            dma((2, chips)),
            dma((2, chips)),
            dma((2, pairs)),
            dma((2, pairs)),
            dma((2,)),
            dma((2,)),
            dma((chips,)),
            dma((chips,)),
            low_v(own_len, width),
            low_v(own_len, width),
            low_v(own_len, width),
            low_v(own_len, width),
            dma((2,)),
            dma((2,)),
            dma((steps,)),
            dma((steps,)),
        ],
        compiler_params=pltpu.CompilerParams(collective_id=5, has_side_effects=True, vmem_limit_bytes=60 * 1024 * 1024),
        cost_estimate=pl.CostEstimate(
            flops=heads * full_len * full_len * HD * 20, bytes_accessed=full_len * width * 8, transcendentals=heads * full_len * full_len // 2
        ),
        name="back",
    )(prefix, grads_in, cos, sin, query_in, pair_in, attended, lse, middle, down_part, gate_part, up_part, down_in, out_half, mixer_sums)


def finish_kernel(
    groups,
    context,
    grad_proj,
    normed,
    inputs,
    own_middle,
    gain,
    ff_sums,
    ff_pairs,
    up_part,
    up_in,
    mixer_sums,
    mixer_in,
    query_hbm,
    key_hbm,
    value_hbm,
    input_low,
    proj_grad,
    mixer_grad,
    units,
    proj_in,
    query_w,
    key_w,
    value_w,
    branch_out,
    branch_in,
    own_part,
    proj_part,
    proj_sums,
    proj_own,
    proj_z,
    mixer_rows,
    mixer_own,
    mixer_z,
    up_sums,
    up_pairs,
    pairs_send,
    pairs_recv,
    unit_own,
    unit_other,
    core_out,
    slices,
    weight_sem,
    branch_send,
    branch_recv,
    input_send,
    input_recv,
    core_sem,
    proj_sem,
    proj_send,
    proj_recv,
    proj_z_send,
    proj_z_recv,
    mixer_sem,
    mixer_send,
    mixer_recv,
    unit_sem,
    core_send,
    core_recv,
    unit_send,
    unit_recv,
    keep_sem,
):
    own_len, width = own_middle.shape
    shard = width // groups
    piece = units.shape[2]
    pairs, chips = context // 2, groups // 2
    f, c, t = lax.axis_index("fsdp"), lax.axis_index("ctx"), lax.axis_index("tp")
    core, p, j, y = lax.rem(f, 2), lax.rem(c, 2), lax.div(c, 2), lax.div(f, 2)
    other_half, mate, next_z = {"tp": 1 - t}, {"fsdp": f + 1 - 2 * core}, {"ctx": c + 1 - 2 * p}
    next_ctx = lambda k: lax.rem(c + k, context)
    next_y = lambda a: lax.rem(y + a, chips)
    greet(
        [other_half, mate]
        + [{"ctx": next_ctx(k)} for k in range(1, context)]
        + [{"fsdp": next_y(a) * 2 + core} for a in range(1, chips)]
    )

    def load_weights(g):
        slot = g % 2
        return [
            pltpu.make_async_copy(hbm.at[g], near.at[slot], weight_sem.at[i, slot])
            for i, (hbm, near) in enumerate(((query_hbm, query_w), (key_hbm, key_w), (value_hbm, value_w)))
        ]

    def mixer_loads(a):
        source = mixer_sums.at[y] if a == 0 else mixer_in.at[a - 1]
        return pltpu.make_async_copy(source, mixer_rows.at[a], mixer_sem.at[a])

    for copy in load_weights(0):
        copy.start()
    for a in range(chips):
        mixer_loads(a).start()

    send_core = remote(proj_part, proj_sums, core_sem.at[0], core_sem.at[1], mate)
    token_product(normed, grad_proj, 1 - core, proj_part, groups)
    send_core.start()

    def send_mixer(k):
        return remote(mixer_own.at[next_ctx(k)], mixer_z.at[k - 1], mixer_send.at[k], mixer_recv.at[k], {"ctx": next_ctx(k)})

    for a in range(chips):
        mixer_loads(a).wait()
    for at in range(context):
        total = mixer_rows[0, at * piece : (at + 1) * piece].astype(F32)
        for a in range(1, chips):
            total = total + mixer_rows[a, at * piece : (at + 1) * piece].astype(F32)
        mixer_own[at] = total.astype(BF16)
    for k in range(1, context):
        send_mixer(k).start()

    def send_branch(g):
        return remote(branch_out.at[g], branch_in.at[g], branch_send.at[g], branch_recv.at[g], other_half)

    query_cols, key_cols = query_w.shape[2], key_w.shape[2]

    def back_rows(half, slot):
        rows = half_rows(half, own_len)
        return (
            dot_nt(grad_proj[rows, :query_cols], query_w[slot])
            + dot_nt(grad_proj[rows, query_cols : query_cols + key_cols], key_w[slot])
            + dot_nt(grad_proj[rows, query_cols + key_cols :], value_w[slot])
        )

    for g in range(groups):
        for copy in load_weights(g):
            copy.wait()
        if g + 1 < groups:
            for copy in load_weights(g + 1):
                copy.start()
        branch_out[g] = back_rows(1 - t, g % 2).astype(BF16)
        send_branch(g).start()
        own_part[:, g * shard : (g + 1) * shard] = back_rows(t, g % 2)

    def send_proj(a):
        return remote(proj_sums.at[next_y(a)], proj_in.at[a - 1], proj_send.at[a], proj_recv.at[a], {"fsdp": next_y(a) * 2 + core})

    send_core.wait()
    token_product(normed, grad_proj, core, proj_part, groups)
    for at in range(chips):
        add_rows(proj_part.at[at], proj_sums.at[at], proj_sums.at[at])
    for a in range(1, chips):
        send_proj(a).start()

    send_pair = lambda b: pair_part(up_sums, up_pairs, pairs_send, pairs_recv, b, context)
    add_chips(up_part, up_in, up_sums, unit_own, unit_other, unit_sem, groups, context)
    for b in range(1, pairs):
        send_pair(b).start()
    summed = ((ff_sums.at[0], ff_pairs.at[0]), (ff_sums.at[1], ff_pairs.at[1]), (up_sums, up_pairs))

    def send_unit_core(w):
        return remote(core_out.at[w], slices.at[w, core], core_send.at[w], core_recv.at[w], mate)

    def send_unit(w, s):
        return remote(slices.at[w, s, 1 - p], units.at[w, s * 2 + p], unit_send.at[w, s], unit_recv.at[w, s], next_z)

    def keep_unit(w, s):
        return pltpu.make_async_copy(slices.at[w, s, p], units.at[w, s * 2 + p], keep_sem.at[w, s])

    def to_core(w):
        own, others = summed[w]

        def load(kept):
            at_core = core if kept == 0 else 1 - core
            copies = [pltpu.make_async_copy(own.at[j, at_core], unit_own.at[kept], unit_sem.at[0, kept])]
            for b in range(1, pairs):
                copies.append(
                    pltpu.make_async_copy(others.at[b - 1, at_core], unit_other.at[kept, b - 1], unit_sem.at[b, kept])
                )
            return copies

        if w < 2:
            for copy in load(0) + load(1):
                copy.start()
            for copy in load(0) + load(1):
                copy.wait()
        for kept in range(2):
            at_core = core if kept == 0 else 1 - core
            total = (unit_own[kept] if w < 2 else own[j, at_core]).astype(F32)
            for b in range(1, pairs):
                total = total + (unit_other[kept, b - 1] if w < 2 else others[b - 1, at_core]).astype(F32)
            total = total.astype(BF16)
            for at in range(2):
                if kept == 0:
                    slices[w, core, at] = total[at * piece : (at + 1) * piece]
                else:
                    core_out[w, at] = total[at * piece : (at + 1) * piece]
        send_unit_core(w).start()
    def to_owner(w):
        send_unit_core(w).wait_recv()
        for s in range(2):
            send_unit(w, s).start()
            keep_unit(w, s).start()

    for w in range(2):
        to_core(w)
    for w in range(2):
        to_owner(w)

    step = min(128, own_len)
    steps = own_len // step

    def send_low(half, i):
        rows = pl.ds(pl.multiple_of(half * own_len + i * step, step), step)
        return remote(input_low.at[rows], input_low.at[rows], input_send.at[i], input_recv.at[i], other_half)

    for g in range(groups):
        send_branch(g).wait_recv()

    def norm_back(i, carry):
        at = pl.ds(pl.multiple_of(i * step, step), step)
        grad = jnp.concatenate(
            [own_part[at, g * shard : (g + 1) * shard] + branch_in[g, at, :].astype(F32) for g in range(groups)], axis=1
        )
        part = inputs[at, :].astype(F32)
        inner = grad * gain[...]
        mixed = jnp.mean(inner * part, axis=-1, keepdims=True)
        scale = lax.rsqrt(jnp.mean(part * part, axis=-1, keepdims=True) + EPS)
        made = own_middle[at, :] + scale * inner - part * (scale * scale * scale * mixed)
        input_low[pl.ds(pl.multiple_of(t * own_len + i * step, step), step), :] = made.astype(BF16)
        send_low(t, i).start()
        return carry

    lax.fori_loop(0, steps, norm_back, 0)

    def proj_load(a):
        return pltpu.make_async_copy(proj_in.at[a - 1], proj_part.at[a - 1], proj_sem.at[a])

    def send_proj_z(k):
        return remote(
            proj_own.at[next_ctx(k)], proj_z.at[k - 1], proj_z_send.at[k], proj_z_recv.at[k], {"ctx": next_ctx(k)}
        )

    for a in range(1, chips):
        send_proj(a).wait_recv()
        proj_load(a).start()
    for a in range(1, chips):
        proj_load(a).wait()
    for at in range(context):
        total = proj_sums[y, at * piece : (at + 1) * piece].astype(F32)
        for a in range(1, chips):
            total = total + proj_part[a - 1, at * piece : (at + 1) * piece].astype(F32)
        proj_own[at] = total.astype(BF16)
    for k in range(1, context):
        send_proj_z(k).start()

    for b in range(1, pairs):
        send_pair(b).wait()
    to_core(2)
    to_owner(2)
    total = mixer_own[c].astype(F32)
    for k in range(1, context):
        send_mixer(k).wait()
        total = total + mixer_z[k - 1].astype(F32)
    mixer_grad[...] = total
    total = proj_own[c].astype(F32)
    for k in range(1, context):
        send_proj_z(k).wait()
        total = total + proj_z[k - 1].astype(F32)
    proj_grad[...] = total

    for g in range(groups):
        send_branch(g).wait_send()
    for a in range(1, chips):
        send_proj(a).wait_send()
    for w in range(3):
        send_unit_core(w).wait_send()
        for s in range(2):
            send_unit(w, s).wait()
            keep_unit(w, s).wait()
    for i in range(steps):
        send_low(t, i).wait_send()
        send_low(1 - t, i).wait_recv()


def finish(
    groups,
    context,
    grad_proj,
    normed,
    inputs,
    own_middle,
    gain,
    ff_sums,
    ff_pairs,
    up_part,
    up_in,
    mixer_sums,
    mixer_in,
    query_full,
    key_full,
    value_full,
):
    own_len, width = own_middle.shape
    chips, pairs = groups // 2, context // 2
    unit, hidden = ff_sums.shape[3:]
    piece = unit // 2
    steps = own_len // min(128, own_len)
    proj_cols, mixer_cols = grad_proj.shape[1], mixer_sums.shape[2]
    core_rows = width // groups
    anywhere = pl.BlockSpec(memory_space=pl.ANY)
    near = pl.BlockSpec(memory_space=pltpu.VMEM)
    dma = pltpu.SemaphoreType.DMA
    low = lambda *shape: jax.ShapeDtypeStruct(shape, BF16)
    low_v = lambda *shape: pltpu.VMEM(shape, BF16)
    return pl.pallas_call(
        functools.partial(finish_kernel, groups, context),
        in_specs=[near] * 5 + [anywhere] * 9,
        out_specs=[near] * 3 + [anywhere] * 2,
        out_shape=[
            low(2 * own_len, width),
            jax.ShapeDtypeStruct((piece, proj_cols), F32),
            jax.ShapeDtypeStruct((piece, mixer_cols), F32),
            low(3, 4, piece, hidden),
            low(chips - 1, core_rows, proj_cols),
        ],
        scratch_shapes=[low_v(2, *w.shape[1:]) for w in (query_full, key_full, value_full)]
        + [
            low_v(groups, own_len, width // groups),
            low_v(groups, own_len, width // groups),
            pltpu.VMEM((own_len, width), F32),
            low_v(chips, core_rows, proj_cols),
            low_v(chips, core_rows, proj_cols),
            low_v(context, piece, proj_cols),
            low_v(context - 1, piece, proj_cols),
            low_v(chips, core_rows, mixer_cols),
            low_v(context, piece, mixer_cols),
            low_v(context - 1, piece, mixer_cols),
            low_v(pairs, 2, unit, hidden),
            low_v(pairs - 1, 2, unit, hidden),
            dma((pairs,)),
            dma((pairs,)),
            low_v(2, unit, hidden),
            low_v(2, max(pairs, chips) - 1, unit, hidden),
            low_v(3, 2, piece, hidden),
            low_v(3, 2, 2, piece, hidden),
            dma((3, 2)),
            dma((groups,)),
            dma((groups,)),
            dma((steps,)),
            dma((steps,)),
            dma((2,)),
            dma((chips,)),
            dma((chips,)),
            dma((chips,)),
            dma((context,)),
            dma((context,)),
            dma((chips,)),
            dma((context,)),
            dma((context,)),
            dma((max(pairs, chips), 2)),
            dma((3,)),
            dma((3,)),
            dma((3, 2)),
            dma((3, 2)),
            dma((3, 2)),
        ],
        compiler_params=pltpu.CompilerParams(collective_id=6, has_side_effects=True, vmem_limit_bytes=62 * 1024 * 1024),
        cost_estimate=pl.CostEstimate(
            flops=own_len * width * grad_proj.shape[1] * 8, bytes_accessed=own_len * width * 40, transcendentals=0
        ),
        name="finish",
    )(
        grad_proj,
        normed,
        inputs,
        own_middle,
        gain.reshape(1, width),
        ff_sums,
        ff_pairs,
        up_part,
        up_in,
        mixer_sums,
        mixer_in,
        query_full,
        key_full,
        value_full,
    )


def tie(*values):
    return lax.optimization_barrier(values)


def on_device(
    tokens, prefix, attn_gain, w_query, w_key, w_value, w_out, mlp_gain, w_gate, w_up, w_down, cotangent
):
    _, local_len, width = tokens.shape
    groups, context, halves = lax.axis_size("fsdp"), lax.axis_size("ctx"), lax.axis_size("tp")
    own_len = local_len // halves
    full_len = local_len * context
    query_cols = w_query.shape[1]
    kv_heads = w_key.shape[1] // HD
    copies = context // kv_heads
    heads = query_cols // HD // context
    group_cols = (heads + 2) * HD
    hidden_cols = w_gate.shape[1] // 4
    own_start = lax.axis_index("tp") * own_len
    own = lambda values: lax.dynamic_slice_in_dim(values, own_start, own_len, 0)

    cos, sin = rope_tables(full_len)
    inputs_all = tokens.reshape(local_len, width)
    grad_out = cotangent.reshape(local_len, width)

    (
        normed_one,
        query_in,
        pair_in,
        attended,
        lse,
        heads_back,
        middle,
        normed_two,
        query_full,
        key_full,
        value_full,
        mixer_blocks,
        gate_cols,
        up_cols,
        down_blocks,
        grad_plane,
    ) = front(
        groups,
        context,
        prefix,
        inputs_all,
        attn_gain,
        mlp_gain,
        cos,
        sin,
        w_query,
        w_key,
        w_value,
        w_out,
        w_gate,
        w_up,
        w_down,
        grad_out,
    )

    plane, _, _, grad_up, down_part, gate_part, out_own, out_core, grad_normed_two = mlp(
        groups, normed_two, grad_plane, gate_cols, up_cols, down_blocks
    )
    piece = width // (groups * context)
    own_middle, _, grads_in, mixer_sums, down_in, up_part, out_half = turn(
        groups,
        context,
        heads,
        grad_normed_two,
        middle,
        grad_out,
        mlp_gain,
        mixer_blocks,
        down_part,
        plane,
        grad_up,
        out_own,
        out_core,
        heads_back,
    )
    grad_proj, sums, pair_sums, layer_low, _, up_in, _, mixer_in = back(
        groups,
        context,
        kv_heads,
        prefix,
        grads_in,
        cos,
        sin,
        query_in,
        pair_in,
        attended,
        lse,
        middle,
        down_part,
        gate_part,
        up_part,
        down_in,
        out_half,
        mixer_sums,
    )
    input_low, qkv_grad, mixer_rows, units, _ = finish(
        groups,
        context,
        grad_proj,
        normed_one,
        own(inputs_all),
        own_middle,
        attn_gain,
        sums,
        pair_sums,
        up_part,
        up_in,
        mixer_sums,
        mixer_in,
        query_full,
        key_full,
        value_full,
    )
    input_grad = input_low.astype(F32)
    layer_out = layer_low
    down_grad = jnp.swapaxes(units[0], 1, 2).reshape(4 * hidden_cols, piece).astype(F32)
    wide = lambda rows: jnp.swapaxes(rows, 0, 1).reshape(piece, 4 * hidden_cols).astype(F32)
    gate_grad, up_grad = wide(units[1]), wide(units[2])
    out_grad = jnp.transpose(mixer_rows)

    piece_start = lax.axis_index("ctx") * piece
    rows_of = lambda weight: lax.dynamic_slice_in_dim(weight, piece_start, piece, 0).astype(F32)
    kv_cols = kv_heads * HD
    query_grad = qkv_grad[:, :query_cols]
    key_grad = qkv_grad[:, query_cols : query_cols + kv_cols]
    value_grad = qkv_grad[:, query_cols + kv_cols :]
    mlp_sum = jnp.sum(rows_of(w_gate) * gate_grad + rows_of(w_up) * up_grad, axis=1)
    attn_sum = sum(
        jnp.sum(rows_of(weight) * grad, axis=1)
        for weight, grad in ((w_query, query_grad), (w_key, key_grad), (w_value, value_grad))
    )
    gain_starts = lax.axis_index("fsdp") * (piece * context) + piece_start
    gain_of = lambda gain: lax.dynamic_slice_in_dim(gain, gain_starts, piece, 0)
    sums = lax.psum(jnp.stack([mlp_sum, attn_sum]), "tp")
    mlp_gain_grad = sums[0] / gain_of(mlp_gain)
    attn_gain_grad = sums[1] / gain_of(attn_gain)

    return (
        layer_out.reshape(tokens.shape),
        input_grad.reshape(tokens.shape),
        attn_gain_grad,
        query_grad,
        key_grad,
        value_grad,
        out_grad,
        mlp_gain_grad,
        gate_grad,
        up_grad,
        down_grad,
    )


def solution(mesh):
    rows = P("fsdp", "ctx", None)
    owned = P(("fsdp", "ctx"), "tp")
    owned_t = P("tp", ("fsdp", "ctx"))
    gain = P(("fsdp", "ctx"))
    down, up = P("fsdp", "tp"), P("tp", "fsdp")
    return jax.shard_map(
        on_device,
        mesh=mesh,
        in_specs=(rows, P("fsdp"), P(), down, down, down, up, P(), down, down, up, rows),
        out_specs=(rows, rows, gain, owned, owned, owned, owned_t, gain, owned, owned, owned_t),
        check_vma=False,
    )
```

```python
import functools
import math

import jax
import jax.numpy as jnp
from jax import lax
from jax.experimental import pallas as pl
from jax.experimental.pallas import tpu as pltpu
from jax.sharding import PartitionSpec as P

HD = 80
EPS = 1e-05
THETA = 1000000.0
MASKED = -1e30
SCALE = HD ** (-0.5)
SCALE_LOG2 = SCALE * math.log2(math.e)
BF16 = jnp.bfloat16
F32 = jnp.float32
MESH = pl.DeviceIdType.MESH


def dot(left, right):
    return jnp.dot(left, right, preferred_element_type=F32)


def dot_tn(left, right):
    return lax.dot_general(left, right, (((0,), (0,)), ((), ())), preferred_element_type=F32)


def dot_nt(left, right):
    return lax.dot_general(left, right, (((1,), (1,)), ((), ())), preferred_element_type=F32)


def rope_tables(full_len):
    half = HD // 2
    frequency = THETA ** (-(jnp.arange(half, dtype=F32) * 2.0) / HD)
    angles = jnp.arange(full_len, dtype=jnp.int32).astype(F32)[:, None] * frequency[None, :]
    cos, sin = jnp.cos(angles), jnp.sin(angles)
    return jnp.concatenate([cos, cos], axis=1), jnp.concatenate([-sin, sin], axis=1)


def swap_halves(values):
    half = HD // 2
    return jnp.concatenate([values[:, half:], values[:, :half]], axis=1)


def rotate(values, cos, sin):
    values = values.astype(F32)
    return values * cos + swap_halves(values) * sin


def rotate_back(values, cos, sin):
    return values * cos - swap_halves(values) * sin


def stack_heads(ref, rows, heads):
    return jnp.concatenate([ref[rows, h * HD : (h + 1) * HD] for h in range(heads)], axis=0)


def stack_rotated(ref, rows, heads, cos, sin):
    return jnp.concatenate(
        [rotate(ref[rows, h * HD : (h + 1) * HD], cos, sin).astype(BF16) for h in range(heads)],
        axis=0,
    )


def load_keys(qkv, at, cos, sin, keys, values, step):
    def body(i, carry):
        rows = pl.ds(pl.multiple_of(i * step, step), step)
        keys[rows, :] = rotate(qkv[rows, at : at + HD], cos[rows, :], sin[rows, :]).astype(BF16)
        values[rows, :] = qkv[rows, at + HD :]
        return carry

    lax.fori_loop(0, qkv.shape[0] // step, body, 0)


def key_blocks(i, rows, block, full_len):
    start = i * rows
    clear = lax.div(start + 1, block)
    needed = lax.div(jnp.maximum(start + rows, full_len // 2) + block - 1, block)
    return clear, needed


def attention_sizes(full_len):
    return min(256, full_len), min(512, full_len)


def front_kernel(
    groups,
    context,
    heads,
    prefix_ref,
    tokens,
    gain_one,
    gain_two,
    cos,
    sin,
    w_query,
    w_key,
    w_value,
    w_out,
    w_gate,
    w_up,
    w_down,
    cotangent,
    normed,
    qkv_in,
    attended,
    lse,
    heads_in,
    middle,
    normed_two,
    query_hbm,
    key_hbm,
    value_hbm,
    mixer_hbm,
    gate_hbm,
    up_hbm,
    down_hbm,
    grad_plane,
    query_w,
    key_w,
    value_w,
    mixer_w,
    qkv_out,
    keys,
    values,
    branch_out,
    branch_in,
    gate_near,
    up_near,
    down_near,
    own_sem,
    save_sem,
    gather_send,
    gather_recv,
    relay_send,
    relay_recv,
    piece_send,
    piece_recv,
    pass_send,
    pass_recv,
    qkv_send,
    qkv_recv,
    heads_send,
    heads_recv,
    ff_own,
    ff_send,
    ff_recv,
    branch_sem,
    plane_sem,
):
    ff_in, ff_out = (w_gate, w_up, w_down), (gate_hbm, up_hbm, down_hbm)
    local_len, width = tokens.shape
    full_len = local_len * context
    own_len = local_len // 2
    chips = groups // 2
    f, c, t = lax.axis_index("fsdp"), lax.axis_index("ctx"), lax.axis_index("tp")
    y, core = lax.div(f, 2), lax.rem(f, 2)
    mate = {"fsdp": y * 2 + 1 - core}
    up_y = lambda a: {"fsdp": lax.rem(y + a, chips) * 2 + core}
    source_y = lambda a: lax.rem(y + chips - a, chips) * 2 + core
    next_group = lambda k: lax.rem(f + k, groups)
    next_ctx = lambda k: lax.rem(c + k, context)
    last_ctx = lambda k: lax.rem(c + context - k, context)
    other_half = {"tp": 1 - t}

    gathered = [
        (w_query, query_w, query_hbm),
        (w_key, key_w, key_hbm),
        (w_value, value_w, value_hbm),
        (w_out, mixer_w, mixer_hbm),
    ]

    def own_shard(w):
        return pltpu.make_async_copy(gathered[w][0], gathered[w][1].at[f], own_sem.at[w])

    def piece_rows(w):
        rows = gathered[w][0].shape[0]
        piece = max(1, round(0.6 * rows / context / 16)) * 16
        return rows - piece * context, piece

    def to_chip(w, a):
        shard_rows = pl.ds(0, piece_rows(w)[0] if a else gathered[w][0].shape[0])
        return remote(
            gathered[w][0].at[shard_rows],
            gathered[w][1].at[f, shard_rows],
            gather_send.at[w, a],
            gather_recv.at[w, a],
            up_y(a) if a else mate,
        )

    def piece_of(w, at):
        straight, piece = piece_rows(w)
        return pl.ds(pl.multiple_of(straight + at * piece, 16), piece)

    def send_piece(w, a):
        rows = piece_of(w, c)
        return remote(
            gathered[w][0].at[rows], gathered[w][1].at[f, rows], piece_send.at[w, a], piece_recv.at[w, a], up_y(a)
        )

    def pass_piece(w, a, k):
        at = gathered[w][1].at[source_y(a), piece_of(w, c)]
        return remote(at, at, pass_send.at[w, a, k], pass_recv.at[w, a, k], {"ctx": next_ctx(k)})

    def relay(w, a):
        at = source_y(a)
        return pltpu.make_async_remote_copy(
            src_ref=gathered[w][1].at[at],
            dst_ref=gathered[w][1].at[at],
            send_sem=relay_send.at[w, a],
            recv_sem=relay_recv.at[w, a],
            device_id=mate,
            device_id_type=MESH,
        )

    def save(w):
        return pltpu.make_async_copy(gathered[w][1], gathered[w][2], save_sem.at[w])

    def send_all(w):
        for a in range(1, chips):
            send_piece(w, a).start()
        for a in range(1, chips):
            to_chip(w, a).start()
        to_chip(w, 0).start()
        own_shard(w).start()

    def pass_on(w):
        for a in range(1, chips):
            send_piece(w, a).wait_recv()
            for k in range(1, context):
                pass_piece(w, a, k).start()

    def arrive(w):
        for a in range(1, chips):
            to_chip(w, a).wait_recv()
            for k in range(1, context):
                pass_piece(w, a, k).wait_recv()
            relay(w, a).start()

    def complete(w):
        own_shard(w).wait()
        to_chip(w, 0).wait_recv()
        for a in range(1, chips):
            relay(w, a).wait_recv()
        save(w).start()

    def finish(w):
        for a in range(chips):
            to_chip(w, a).wait_send()
        for a in range(1, chips):
            send_piece(w, a).wait_send()
            for k in range(1, context):
                pass_piece(w, a, k).wait_send()
            relay(w, a).wait_send()
        save(w).wait()

    def send_heads(k):
        rows = pl.ds(pl.multiple_of(c * local_len, local_len), local_len)
        return remote(
            qkv_out.at[next_ctx(k)], qkv_in.at[rows], qkv_send.at[k], qkv_recv.at[k], {"ctx": next_ctx(k)}
        )

    def rows_of_ctx(at):
        return pl.ds(pl.multiple_of(at * local_len, local_len), local_len)

    def send_back(at):
        return pltpu.make_async_remote_copy(
            src_ref=attended.at[rows_of_ctx(at)],
            dst_ref=heads_in.at[c],
            send_sem=heads_send.at[at],
            recv_sem=heads_recv.at[c],
            device_id={"ctx": at},
            device_id_type=MESH,
        )

    def get_back(at):
        return pltpu.make_async_remote_copy(
            src_ref=attended.at[rows_of_ctx(at)],
            dst_ref=heads_in.at[at],
            send_sem=heads_send.at[at],
            recv_sem=heads_recv.at[at],
            device_id={"ctx": at},
            device_id_type=MESH,
        )

    def ff_parts(w, g):
        units = lax.rem(g, 2) * 2 + lax.rem(c, 2)
        if w < 2:
            cols = ff_out[w].shape[1]
            shard = width // groups
            return (
                ff_in[w].at[:, pl.ds(pl.multiple_of(units * cols, cols), cols)],
                ff_out[w].at[pl.ds(pl.multiple_of(f * shard, shard), shard)],
            )
        rows = ff_out[w].shape[1]
        return ff_in[w].at[pl.ds(pl.multiple_of(units * rows, rows), rows)], ff_out[w].at[f]

    def send_ff(w, k):
        g = next_group(k)
        source, target = ff_parts(w, g)
        return pltpu.make_async_remote_copy(
            src_ref=source,
            dst_ref=target,
            send_sem=ff_send.at[w, k],
            recv_sem=ff_recv.at[w, k],
            device_id={"fsdp": g},
            device_id_type=MESH,
        )

    def own_ff(w, out):
        source, target = ff_parts(w, f)
        near = (gate_near, up_near, down_near)[w]
        return pltpu.make_async_copy(near, target, ff_own.at[w]) if out else pltpu.make_async_copy(source, near, ff_own.at[w])

    pair_rows = lambda at_core, at_pair: pl.ds(pl.multiple_of((at_core * 2 + at_pair) * local_len, local_len), local_len)
    p = lax.rem(c, 2)
    pair_mate = {"ctx": c + 1 - 2 * p}
    plane_own = pltpu.make_async_copy(cotangent, grad_plane.at[pair_rows(core, p)], plane_sem.at[0])

    def plane_copy(i, source, rows, partner):
        return pltpu.make_async_remote_copy(
            src_ref=source,
            dst_ref=grad_plane.at[rows],
            send_sem=plane_sem.at[1 + 2 * i],
            recv_sem=plane_sem.at[2 + 2 * i],
            device_id=partner,
            device_id_type=MESH,
        )

    def plane_half(at_core, at_pair, half):
        start = ((at_core * 2 + at_pair) * 2 + half) * own_len
        return pl.ds(pl.multiple_of(start, own_len), own_len)

    got_half = grad_plane.at[plane_half(core, 1 - p, t)]
    plane_copies = [
        plane_copy(0, cotangent.at[half_rows(t, own_len)], plane_half(core, p, t), pair_mate),
        plane_copy(1, cotangent, pair_rows(core, p), mate),
        plane_copy(2, grad_plane.at[pair_rows(core, 1 - p)], pair_rows(core, 1 - p), mate),
        plane_copy(3, got_half, plane_half(core, 1 - p, t), other_half),
    ]

    barrier = pltpu.get_barrier_semaphore()
    partners = [{"fsdp": next_group(k)} for k in range(1, groups)]
    partners += [{"ctx": next_ctx(k)} for k in range(1, context)]
    partners.append(other_half)
    for partner in partners:
        pl.semaphore_signal(barrier, inc=1, device_id=partner, device_id_type=MESH)
    pl.semaphore_wait(barrier, len(partners))

    for w in range(3):
        send_all(w)
    plane_own.start()
    for copy in plane_copies[:2]:
        copy.start()
    for w in range(3):
        own_ff(w, False).start()

    step = min(128, local_len)

    def norm_rows(i, carry):
        rows = pl.ds(pl.multiple_of(i * step, step), step)
        part = tokens[rows, :].astype(F32)
        scale = lax.rsqrt(jnp.mean(part * part, axis=-1, keepdims=True) + EPS)
        normed[rows, :] = (part * scale * gain_one[...]).astype(BF16)
        return carry

    lax.fori_loop(0, local_len // step, norm_rows, 0)

    shard = width // groups

    def project(weight):
        total = None
        for g in range(groups):
            part = dot(normed[:, g * shard : (g + 1) * shard], weight[g])
            total = part if total is None else total + part
        return total.astype(BF16)

    query_cols = heads * HD
    for w in range(3):
        pass_on(w)
    arrive(0)
    complete(0)
    query = project(query_w)
    for at in range(context):
        qkv_out[at, :, :query_cols] = query[:, at * query_cols : (at + 1) * query_cols]
    for w in (1, 2):
        arrive(w)
    for w in (1, 2):
        complete(w)
    send_all(3)
    kv_heads = key_w.shape[2] // HD
    copies = context // kv_heads
    key, value = project(key_w), project(value_w)
    for at in range(context):
        head = at // copies
        qkv_out[at, :, query_cols : query_cols + HD] = key[:, head * HD : (head + 1) * HD]
        qkv_out[at, :, query_cols + HD :] = value[:, head * HD : (head + 1) * HD]
    for k in range(1, context):
        send_heads(k).start()
    qkv_in[rows_of_ctx(c), :] = qkv_out[c]

    def start_ff(w):
        for k in range(1, groups):
            send_ff(w, k).start()

    start_ff(0)
    plane_copies[0].wait_recv()
    plane_copies[3].start()

    for k in range(1, context):
        send_heads(k).wait_recv()

    rows, block = attention_sizes(full_len)
    load_keys(qkv_in, query_cols, cos, sin, keys, values, rows)
    stacked = heads * rows
    prefix = prefix_ref[0]

    def attend_block(i, carry):
        here = pl.ds(pl.multiple_of(i * rows, rows), rows)
        queries = stack_rotated(qkv_in, here, heads, cos[here, :], sin[here, :])
        clear, needed = key_blocks(i, rows, block, full_len)

        def key_step(j, carry, masked):
            top, total, acc = carry
            there = pl.ds(pl.multiple_of(j * block, block), block)
            scores = dot_nt(queries, keys[there, :])
            if masked:
                key_pos = j * block + lax.broadcasted_iota(jnp.int32, (stacked, block), 1)
                query_pos = i * rows + lax.rem(lax.broadcasted_iota(jnp.int32, (stacked, 1), 0), rows)
                scores = jnp.where(key_pos < jnp.maximum(query_pos + 1, prefix), scores, MASKED)
            new_top = jnp.maximum(top, jnp.max(scores, axis=1, keepdims=True))
            factor = jnp.exp2((top - new_top) * SCALE_LOG2)
            weights = jnp.exp2(scores * SCALE_LOG2 - new_top * SCALE_LOG2)
            total = total * factor + jnp.sum(weights, axis=1, keepdims=True)
            acc = acc * factor + dot(weights.astype(BF16), values[there, :])
            return new_top, total, acc

        state = (
            jnp.full((stacked, 1), MASKED, F32),
            jnp.zeros((stacked, 1), F32),
            jnp.zeros((stacked, HD), F32),
        )
        state = lax.fori_loop(0, clear, functools.partial(key_step, masked=False), state)
        top, total, acc = lax.fori_loop(clear, needed, functools.partial(key_step, masked=True), state)
        acc = acc / total
        for h in range(heads):
            attended[here, h * HD : (h + 1) * HD] = acc[h * rows : (h + 1) * rows].astype(BF16)
        log_sum = top * SCALE_LOG2 + jnp.log2(total)
        lse[i] = jnp.transpose(jnp.broadcast_to(log_sum, (stacked, 128)))[:8]
        return carry

    per_ctx = local_len // rows
    pass_on(3)
    for w in range(3):
        own_ff(w, False).wait()
        own_ff(w, True).start()
    for w in (1, 2):
        start_ff(w)

    def attend_rows(at, carry):
        lax.fori_loop(at * per_ctx, (at + 1) * per_ctx, attend_block, 0)

        @pl.when(at != c)
        def _():
            send_back(at).start()

        @pl.when(at == c)
        def _():
            heads_in[c] = attended[rows_of_ctx(c), :]

        @pl.when(at == context // 2)
        def _():
            arrive(3)

        return carry

    lax.fori_loop(0, context, attend_rows, 0)

    def collect(at, carry):
        @pl.when(at != c)
        def _():
            get_back(at).wait_recv()
            send_back(at).wait_send()

        return carry

    lax.fori_loop(0, context, collect, 0)

    complete(3)
    plane_copies[3].wait_recv()
    plane_copies[2].start()

    def branch_rows(start, store):
        half = pl.ds(pl.multiple_of(start, own_len), own_len)
        for g in range(groups):
            total = None
            for at in range(context):
                part = dot(heads_in[at, half, :], mixer_w[g, at * query_cols : (at + 1) * query_cols, :])
                total = part if total is None else total + part
            store(g * shard, total)

    def keep_low(at, part):
        branch_out[:, at : at + shard] = part.astype(BF16)

    def keep(at, part):
        middle[:, at : at + shard] = part

    branch_rows((1 - t) * own_len, keep_low)
    branch = pltpu.make_async_remote_copy(
        src_ref=branch_out,
        dst_ref=branch_in,
        send_sem=branch_sem.at[0],
        recv_sem=branch_sem.at[1],
        device_id=other_half,
        device_id_type=MESH,
    )
    branch.start()
    branch_rows(t * own_len, keep)
    branch.wait_recv()
    part_len = min(128, own_len)

    def middle_rows(i, carry):
        at = pl.ds(pl.multiple_of(i * part_len, part_len), part_len)
        token_rows = pl.ds(pl.multiple_of(t * own_len + i * part_len, part_len), part_len)
        total = tokens[token_rows, :].astype(F32) + middle[at, :] + branch_in[at, :].astype(F32)
        middle[at, :] = total
        scale = lax.rsqrt(jnp.mean(total * total, axis=-1, keepdims=True) + EPS)
        normed_two[at, :] = (total * scale * gain_two[...]).astype(BF16)
        return carry

    lax.fori_loop(0, own_len // part_len, middle_rows, 0)
    branch.wait_send()
    for k in range(1, context):
        send_heads(k).wait_send()
    for w in range(4):
        finish(w)
    for w in range(3):
        for k in range(1, groups):
            send_ff(w, k).wait_recv()
            send_ff(w, k).wait_send()
        own_ff(w, True).wait()
    plane_own.wait()
    for copy in (plane_copies[0], plane_copies[3]):
        copy.wait_send()
    for copy in plane_copies[1:3]:
        copy.wait()


def front(groups, context, prefix, tokens, gain_one, gain_two, cos, sin, w_query, w_key, w_value, w_out, w_gate, w_up, w_down, cotangent):
    local_len, width = tokens.shape
    full_len = local_len * context
    own_len = local_len // 2
    query_cols = w_query.shape[1]
    heads = query_cols // HD // context
    rows, _ = attention_sizes(full_len)
    hidden = w_gate.shape[1] // 4
    anywhere = pl.BlockSpec(memory_space=pl.ANY)
    near = pl.BlockSpec(memory_space=pltpu.VMEM)
    dma = pltpu.SemaphoreType.DMA
    low = lambda *shape: jax.ShapeDtypeStruct(shape, BF16)
    low_v = lambda *shape: pltpu.VMEM(shape, BF16)
    shapes = [low(groups, *w.shape) for w in (w_query, w_key, w_value, w_out)]
    return pl.pallas_call(
        functools.partial(front_kernel, groups, context, heads),
        in_specs=[pl.BlockSpec(memory_space=pltpu.SMEM)] + [near] * 5 + [anywhere] * 7 + [near],
        out_specs=[near] * 7 + [anywhere] * 8,
        out_shape=[
            low(local_len, width),
            low(full_len, (heads + 2) * HD),
            low(full_len, heads * HD),
            jax.ShapeDtypeStruct((full_len // rows, 8, heads * rows), F32),
            low(context, local_len, heads * HD),
            jax.ShapeDtypeStruct((own_len, width), F32),
            low(own_len, width),
        ]
        + shapes
        + [low(width, hidden), low(width, hidden), low(groups, hidden, width // groups), low(4 * local_len, width)],
        scratch_shapes=[low_v(*shape.shape) for shape in shapes]
        + [
            low_v(context, local_len, (heads + 2) * HD),
            low_v(full_len, HD),
            low_v(full_len, HD),
            low_v(own_len, width),
            low_v(own_len, width),
            low_v(width // groups, hidden),
            low_v(width // groups, hidden),
            low_v(hidden, width // groups),
            dma((4,)),
            dma((4,)),
        ]
        + [dma((4, groups // 2))] * 6
        + [dma((4, groups // 2, context))] * 2
        + [dma((context,))] * 4
        + [dma((3,)), dma((3, groups)), dma((3, groups)), dma((2,)), dma((9,))],
        compiler_params=pltpu.CompilerParams(
            collective_id=1, has_side_effects=True, vmem_limit_bytes=60 * 1024 * 1024
        ),
        cost_estimate=pl.CostEstimate(
            flops=local_len * width * query_cols * 6, bytes_accessed=local_len * width * 40, transcendentals=full_len * full_len
        ),
        name="front",
    )(
        prefix,
        tokens,
        gain_one.reshape(1, width),
        gain_two.reshape(1, width),
        cos,
        sin,
        w_query,
        w_key,
        w_value,
        w_out,
        w_gate,
        w_up,
        w_down,
        cotangent,
    )


def product(left, right, result, side, columns_in, columns_out, side_sem, columns_sem, columns_store):
    whole = pltpu.make_async_copy(right, side, side_sem)
    whole.start()
    tile = columns_in.shape[2]
    tiles = left.shape[1] // tile

    def load(i):
        at = pl.ds(pl.multiple_of(i * tile, tile), tile)
        return pltpu.make_async_copy(left.at[:, at], columns_in.at[lax.rem(i, 2)], columns_sem.at[lax.rem(i, 2)])

    def store(i):
        at = pl.ds(pl.multiple_of(i * tile, tile), tile)
        return pltpu.make_async_copy(columns_out, result.at[at], columns_store.at[0])

    load(0).start()
    whole.wait()

    def body(i, carry):
        load(i).wait()

        @pl.when(i + 1 < tiles)
        def _():
            load(i + 1).start()

        made = dot_tn(columns_in[lax.rem(i, 2)], side[...]).astype(BF16)

        @pl.when(i > 0)
        def _():
            store(i - 1).wait()

        columns_out[...] = made
        store(i).start()
        return carry

    lax.fori_loop(0, tiles, body, 0)
    store(tiles - 1).wait()


def mlp_kernel(
    groups,
    normed,
    cotangent,
    gate_hbm,
    up_hbm,
    down_hbm,
    plane,
    hidden_out,
    grad_gate_out,
    grad_up_out,
    down_part,
    gate_part,
    out_own,
    out_core,
    total_out,
    gate_w,
    up_w,
    down_w,
    rows_in,
    grad_in,
    hidden_s,
    grad_gate_s,
    grad_up_s,
    part,
    to_core,
    from_core,
    to_chip,
    from_chip,
    columns_in,
    columns_out,
    load_sem,
    rows_sem,
    grad_sem,
    store_sem,
    columns_sem,
    columns_store,
    out_low,
    out_store,
    out_send,
    out_recv,
    row_send,
    row_recv,
    relay_send,
    relay_recv,
    core_send,
    core_recv,
    chip_send,
    chip_recv,
):
    own_len, width = normed.shape
    chips = 4
    f, c, t = lax.axis_index("fsdp"), lax.axis_index("ctx"), lax.axis_index("tp")
    core, p = lax.rem(f, 2), lax.rem(c, 2)

    def chip_at(step):
        a, b = lax.div(step, 2), lax.rem(step, 2)
        return lax.rem(p + a, 2), lax.rem(t + b, 2)

    def device(at, at_core):
        return {"fsdp": f - core + at_core, "ctx": c - p + at[0], "tp": at[1]}

    def rows_of(at, at_core):
        slot = (at_core * 2 + at[0]) * 2 + at[1]
        return pl.ds(pl.multiple_of(slot * own_len, own_len), own_len)

    here = (p, t)
    mate = {"fsdp": f + 1 - 2 * core}
    mine = rows_of(here, core)

    def remote(source, target, send, recv, partner):
        return pltpu.make_async_remote_copy(
            src_ref=source, dst_ref=target, send_sem=send, recv_sem=recv, device_id=partner, device_id_type=MESH
        )

    def send_rows(step):
        return remote(normed, plane.at[mine], row_send.at[step], row_recv.at[step], device(chip_at(step), core))

    def relay(step, source):
        rows = rows_of(chip_at(step), core)
        return remote(source, plane.at[rows], relay_send.at[step], relay_recv.at[step], mate)

    def send_part(step):
        return remote(to_core.at[step], from_core.at[step], core_send.at[step], core_recv.at[step], mate)

    def send_sum(step):
        return remote(
            to_chip.at[step], from_chip.at[step], chip_send.at[step], chip_recv.at[step], device(chip_at(step), core)
        )

    greet([mate] + [device(chip_at(step), core) for step in range(1, chips)])

    for step in (1, 2):
        send_rows(step).start()
    relay(0, normed).start()
    own_copy = pltpu.make_async_copy(normed, plane.at[mine], load_sem.at[3])
    own_copy.start()
    weights = [
        pltpu.make_async_copy(gate_hbm, gate_w, load_sem.at[0]),
        pltpu.make_async_copy(up_hbm, up_w, load_sem.at[1]),
        pltpu.make_async_copy(down_hbm, down_w, load_sem.at[2]),
    ]
    for copy in weights:
        copy.start()

    def block_rows(index):
        same = 1 - lax.rem(index, 2)
        return rows_of(chip_at(lax.div(index, 2)), lax.rem(core + 1 - same, 2))

    def load_rows(index):
        slot = lax.rem(index, 2)
        return pltpu.make_async_copy(plane.at[block_rows(index)], rows_in.at[slot], rows_sem.at[slot])

    def load_grad(index):
        slot = lax.rem(index, 2)
        return pltpu.make_async_copy(cotangent.at[block_rows(index)], grad_in.at[slot], grad_sem.at[slot])

    load_grad(0).start()
    own_copy.wait()
    load_rows(0).start()
    for copy in weights:
        copy.wait()

    def stores(index):
        rows = block_rows(index)
        return [
            pltpu.make_async_copy(hidden_s, hidden_out.at[rows], store_sem.at[0]),
            pltpu.make_async_copy(grad_gate_s, grad_gate_out.at[rows], store_sem.at[1]),
            pltpu.make_async_copy(grad_up_s, grad_up_out.at[rows], store_sem.at[2]),
        ]

    def keep_out(step):
        return pltpu.make_async_copy(out_low.at[0], out_own.at[step], out_store.at[0])

    def send_out(step):
        return remote(out_low.at[1], out_core.at[step], out_send.at[step], out_recv.at[step], mate)

    def block(index, result):
        slot = lax.rem(index, 2)
        load_grad(index).wait()

        @pl.when(index + 1 < 2 * chips)
        def _():
            load_grad(index + 1).start()

        load_rows(index).wait()
        gate = dot(rows_in[slot], gate_w[...])
        up = dot(rows_in[slot], up_w[...])
        shard = width // groups
        grad_hidden = sum(dot_nt(grad_in[slot, :, g * shard : (g + 1) * shard], down_w[g]) for g in range(groups))
        sigmoid = 1.0 / (1.0 + jnp.exp(-gate))
        silu = gate * sigmoid

        @pl.when(index > 0)
        def _():
            for copy in stores(index - 1):
                copy.wait()

        hidden_s[...] = (silu * up).astype(BF16)
        grad_up_s[...] = (grad_hidden * silu).astype(BF16)
        grad_gate_s[...] = (grad_hidden * up * sigmoid * (1.0 + gate * (1.0 - sigmoid))).astype(BF16)
        for copy in stores(index):
            copy.start()

        @pl.when((index > 1) & (slot == 0))
        def _():
            keep_out(lax.div(index, 2) - 1).wait()

        @pl.when((index > 1) & (slot == 1))
        def _():
            send_out(lax.div(index, 2) - 1).wait_send()

        for g in range(groups):
            out_low[slot, :, g * shard : (g + 1) * shard] = dot(hidden_s[...], down_w[g]).astype(BF16)

        @pl.when(slot == 0)
        def _():
            keep_out(lax.div(index, 2)).start()

        @pl.when(slot == 1)
        def _():
            send_out(lax.div(index, 2)).start()

        tile = 512 if width % 512 == 0 else width
        for at in range(0, width, tile):
            result[:, at : at + tile] = (
                dot_nt(grad_gate_s[...], gate_w[at : at + tile, :]) + dot_nt(grad_up_s[...], up_w[at : at + tile, :])
            ).astype(BF16)

    def pair(step, carry):
        @pl.when(step > 0)
        def _():
            send_rows(step).wait_recv()
            relay(step, plane.at[rows_of(chip_at(step), core)]).start()
            load_rows(2 * step).start()

        @pl.when(step == 1)
        def _():
            send_rows(3).start()

        block(2 * step, part)
        relay(step, normed).wait_recv()
        load_rows(2 * step + 1).start()
        block(2 * step + 1, to_core.at[step])
        send_part(step).start()
        send_part(step).wait_recv()

        @pl.when(step == 0)
        def _():
            total_out[...] = part[...].astype(F32) + from_core[step].astype(F32)

        @pl.when(step > 0)
        def _():
            to_chip[step] = (part[...].astype(F32) + from_core[step].astype(F32)).astype(BF16)
            send_sum(step).start()

        return carry

    lax.fori_loop(0, chips, pair, 0)
    for copy in stores(2 * chips - 1):
        copy.wait()

    side = gate_w.at[pl.ds(0, columns_in.shape[1])]
    product(cotangent, hidden_out, down_part, side, columns_in, columns_out, load_sem.at[0], columns_sem, columns_store)
    product(plane, grad_gate_out, gate_part, side, columns_in, columns_out, load_sem.at[0], columns_sem, columns_store)

    def collect(step, carry):
        send_sum(step).wait_recv()
        total_out[...] += from_chip[step].astype(F32)
        send_sum(step).wait_send()
        send_rows(step).wait_send()
        return carry

    lax.fori_loop(1, chips, collect, 0)

    keep_out(chips - 1).wait()
    send_out(chips - 1).wait_send()

    def drain(step, carry):
        relay(step, normed).wait_send()
        send_part(step).wait_send()
        send_out(step).wait_recv()
        return carry

    lax.fori_loop(0, chips, drain, 0)


def mlp(groups, normed, cotangent, gate_cols, up_cols, down_rows):
    own_len, width = normed.shape
    hidden = gate_cols.shape[1]
    chips = 4
    plane_len = own_len * 2 * chips
    tile = 512 if width % 512 == 0 else width
    anywhere = pl.BlockSpec(memory_space=pl.ANY)
    dma = pltpu.SemaphoreType.DMA
    low = lambda *shape: pltpu.VMEM(shape, BF16)
    return pl.pallas_call(
        functools.partial(mlp_kernel, groups),
        in_specs=[pl.BlockSpec(memory_space=pltpu.VMEM)] + [anywhere] * 4,
        out_specs=[anywhere] * 8 + [pl.BlockSpec(memory_space=pltpu.VMEM)],
        out_shape=[
            jax.ShapeDtypeStruct((plane_len, width), BF16),
            jax.ShapeDtypeStruct((plane_len, hidden), BF16),
            jax.ShapeDtypeStruct((plane_len, hidden), BF16),
            jax.ShapeDtypeStruct((plane_len, hidden), BF16),
            jax.ShapeDtypeStruct((width, hidden), BF16),
            jax.ShapeDtypeStruct((width, hidden), BF16),
            jax.ShapeDtypeStruct((chips, own_len, width), BF16),
            jax.ShapeDtypeStruct((chips, own_len, width), BF16),
            jax.ShapeDtypeStruct((own_len, width), F32),
        ],
        scratch_shapes=[
            low(width, hidden),
            low(width, hidden),
            low(groups, hidden, width // groups),
            low(2, own_len, width),
            low(2, own_len, width),
            low(own_len, hidden),
            low(own_len, hidden),
            low(own_len, hidden),
            low(own_len, width),
            low(chips, own_len, width),
            low(chips, own_len, width),
            low(chips, own_len, width),
            low(chips, own_len, width),
            low(2, plane_len, tile),
            low(tile, hidden),
            dma((4,)),
            dma((2,)),
            dma((2,)),
            dma((3,)),
            dma((2,)),
            dma((1,)),
            low(2, own_len, width),
            dma((1,)),
        ]
        + [dma((chips,))] * 10,
        compiler_params=pltpu.CompilerParams(
            collective_id=3, has_side_effects=True, vmem_limit_bytes=60 * 1024 * 1024
        ),
        cost_estimate=pl.CostEstimate(
            flops=plane_len * width * hidden * 10, bytes_accessed=plane_len * width * 8, transcendentals=plane_len * hidden
        ),
        name="mlp",
    )(normed, cotangent, gate_cols, up_cols, down_rows)


def remote(source, target, send, recv, partner):
    return pltpu.make_async_remote_copy(
        src_ref=source, dst_ref=target, send_sem=send, recv_sem=recv, device_id=partner, device_id_type=MESH
    )


def greet(partners):
    barrier = pltpu.get_barrier_semaphore()
    for partner in partners:
        pl.semaphore_signal(barrier, inc=1, device_id=partner, device_id_type=MESH)
    pl.semaphore_wait(barrier, len(partners))


def half_rows(half, own_len):
    return pl.ds(pl.multiple_of(half * own_len, own_len), own_len)


def ctx_rows(at, local_len):
    return pl.ds(pl.multiple_of(at * local_len, local_len), local_len)


def chip_part(part, chip_in, send, recv, a, groups):
    f = lax.axis_index("fsdp")
    chips = groups // 2
    rows = part.shape[0] // chips
    to = lax.rem(lax.div(f, 2) + a, chips)
    return remote(
        part.at[pl.ds(pl.multiple_of(to * rows, rows), rows)],
        chip_in.at[a - 1],
        send.at[a],
        recv.at[a],
        {"fsdp": to * 2 + lax.rem(f, 2)},
    )


def add_chips(part, chip_in, sums, own, other, sem, groups, context):
    chips, pairs = groups // 2, context // 2
    rows = part.shape[0] // chips
    unit = rows // context
    y = lax.div(lax.axis_index("fsdp"), 2)

    def loads(i):
        slot = lax.rem(i, 2)
        mine = pl.ds(pl.multiple_of(y * rows + i * unit, unit), unit)
        at = pl.ds(pl.multiple_of(i * unit, unit), unit)
        copies = [pltpu.make_async_copy(part.at[mine], own.at[slot], sem.at[0, slot])]
        for a in range(1, chips):
            copies.append(pltpu.make_async_copy(chip_in.at[a - 1, at], other.at[slot, a - 1], sem.at[a, slot]))
        return copies

    for copy in loads(0):
        copy.start()

    def body(i, carry):
        slot = lax.rem(i, 2)

        @pl.when(i + 1 < context)
        def _():
            for copy in loads(i + 1):
                copy.start()

        for copy in loads(i):
            copy.wait()
        made = own[slot].astype(F32)
        for a in range(1, chips):
            made = made + other[slot, a - 1].astype(F32)
        sums[lax.rem(i, pairs), lax.div(i, pairs)] = made.astype(BF16)
        return carry

    lax.fori_loop(0, context, body, 0)


def pair_part(sums, pair_in, send, recv, b, context):
    c = lax.axis_index("ctx")
    to = lax.rem(lax.div(c, 2) + b, context // 2)
    return remote(sums.at[to], pair_in.at[b - 1], send.at[b], recv.at[b], {"ctx": to * 2 + lax.rem(c, 2)})


def token_product(left, right, at_core, result, groups):
    shard = left.shape[1] // groups
    columns = right.shape[1]
    tile = 640 if columns % 640 == 0 else columns
    for own in range(2):

        @pl.when(at_core == own)
        def _():
            for y in range(groups // 2):
                at = (y * 2 + own) * shard
                for n in range(0, columns, tile):
                    result[y, :, n : n + tile] = dot_tn(left[:, at : at + shard], right[:, n : n + tile]).astype(BF16)


def add_rows(left, right, result):
    rows = left.shape[0]
    step = 160 if rows % 160 == 0 else rows

    def body(i, carry):
        at = pl.ds(pl.multiple_of(i * step, step), step)
        result[at, :] = (left[at, :].astype(F32) + right[at, :].astype(F32)).astype(BF16)
        return carry

    lax.fori_loop(0, rows // step, body, 0)


def turn_kernel(
    groups,
    context,
    heads,
    total,
    middle,
    cotangent,
    gain,
    mixer_hbm,
    down_part,
    plane,
    grad_up,
    out_own,
    out_core,
    heads_back,
    own_middle,
    branch_low,
    grads_in,
    mixer_sums,
    chip_in,
    up_part,
    out_half,
    mixer_w,
    heads_out,
    side,
    columns_in,
    columns_out,
    out_rows,
    heads_all,
    mixer_part,
    core_sem,
    side_sem,
    columns_sem,
    columns_store,
    out_sem,
    mixer_sem,
    branch_send,
    branch_recv,
    heads_send,
    heads_recv,
    chip_send,
    chip_recv,
):
    own_len, width = total.shape
    local_len = own_len * 2
    shard = width // groups
    query_cols = heads * HD
    chips = groups // 2
    f, c, t = lax.axis_index("fsdp"), lax.axis_index("ctx"), lax.axis_index("tp")
    next_ctx = lambda k: lax.rem(c + k, context)
    next_chip = lambda a: {"fsdp": lax.rem(lax.div(f, 2) + a, chips) * 2 + lax.rem(f, 2)}
    core = lax.rem(f, 2)
    mate = {"fsdp": f + 1 - 2 * core}
    greet(
        [{"ctx": next_ctx(k)} for k in range(1, context)]
        + [{"tp": 1 - t}, mate]
        + [next_chip(a) for a in range(1, chips)]
    )

    send_chip = lambda a: chip_part(down_part, chip_in, chip_send, chip_recv, a, groups)
    for a in range(1, chips):
        send_chip(a).start()
    mixer = pltpu.make_async_copy(mixer_hbm, mixer_w, mixer_sem.at[0])
    mixer.start()

    step = min(128, own_len)
    steps = own_len // step

    def part_rows(half, i):
        return pl.ds(pl.multiple_of(half * own_len + i * step, step), step)

    def branch(half, i):
        rows = part_rows(half, i)
        return remote(branch_low.at[rows], branch_low.at[rows], branch_send.at[i], branch_recv.at[i], {"tp": 1 - t})

    def norm_back(i, carry):
        at = pl.ds(pl.multiple_of(i * step, step), step)
        rows = part_rows(t, i)
        part = middle[at, :]
        inner = total[at, :] * gain[...]
        mixed = jnp.mean(inner * part, axis=-1, keepdims=True)
        scale = lax.rsqrt(jnp.mean(part * part, axis=-1, keepdims=True) + EPS)
        grad = cotangent[rows, :].astype(F32) + scale * inner - part * (scale * scale * scale * mixed)
        own_middle[at, :] = grad
        branch_low[rows, :] = grad.astype(BF16)
        branch(t, i).start()
        return carry

    lax.fori_loop(0, steps, norm_back, 0)
    mixer.wait()

    def send_grads(half, i, k, order):
        return remote(
            heads_out.at[next_ctx(k), part_rows(half, i)],
            grads_in.at[pl.ds(pl.multiple_of(c * local_len + half * own_len + i * step, step), step)],
            heads_send.at[k, order, i],
            heads_recv.at[k, order, i],
            {"ctx": next_ctx(k)},
        )

    for at in range(context):
        heads_all[:, at * query_cols : (at + 1) * query_cols] = heads_back[at]
    send_core = remote(mixer_part, mixer_sums, core_sem.at[0], core_sem.at[1], mate)

    def add_cores():
        p = lax.rem(c, 2)

        def body(step, carry):
            loads = [
                pltpu.make_async_copy(out_own.at[step], out_rows.at[0], out_sem.at[0]),
                pltpu.make_async_copy(out_core.at[step], out_rows.at[1], out_sem.at[1]),
            ]
            for copy in loads:
                copy.start()
            for copy in loads:
                copy.wait()
            out_rows[0] = (out_rows[0].astype(F32) + out_rows[1].astype(F32)).astype(BF16)
            slot = lax.rem(p + lax.div(step, 2), 2) * 2 + lax.rem(t + lax.rem(step, 2), 2)
            store = pltpu.make_async_copy(out_rows.at[0], out_half.at[slot], out_sem.at[2])
            store.start()
            store.wait()
            return carry

        lax.fori_loop(0, out_own.shape[0], body, 0)

    def both_parts(order, carry):
        half = jnp.where(order == 0, t, 1 - t)

        def one(i, inner):
            @pl.when(order == 1)
            def _():
                branch(1 - t, i).wait_recv()

            rows = part_rows(half, i)
            grad = sum(dot_nt(branch_low[rows, g * shard : (g + 1) * shard], mixer_w[g]) for g in range(groups))
            for at in range(context):
                heads_out[at, rows, :] = grad[:, at * query_cols : (at + 1) * query_cols].astype(BF16)
            for k in range(1, context):
                send_grads(half, i, k, order).start()
            return inner

        lax.fori_loop(0, steps, one, 0)
        grads_in[pl.ds(pl.multiple_of(c * local_len + half * own_len, own_len), own_len), :] = heads_out[
            c, half_rows(half, own_len), :
        ]

        @pl.when(order == 0)
        def _():
            product(plane, grad_up, up_part, side, columns_in, columns_out, side_sem.at[0], columns_sem, columns_store)

        @pl.when(order == 1)
        def _():
            token_product(branch_low, heads_all, 1 - core, mixer_part, groups)
            send_core.start()
            add_cores()
            send_core.wait()
            token_product(branch_low, heads_all, core, mixer_part, groups)
            for at in range(chips):
                add_rows(mixer_part.at[at], mixer_sums.at[at], mixer_sums.at[at])

        return carry

    lax.fori_loop(0, 2, both_parts, 0)
    for order, half in enumerate((t, 1 - t)):
        for k in range(1, context):
            for i in range(steps):
                send_grads(half, i, k, order).wait()
    for i in range(steps):
        branch(t, i).wait_send()
    for a in range(1, chips):
        send_chip(a).wait()


def turn(groups, context, heads, total, middle, cotangent, gain, mixer, down_part, plane, grad_up, out_own, out_core, heads_back):
    own_len, width = total.shape
    local_len = own_len * 2
    chips = groups // 2
    hidden = down_part.shape[1]
    steps = own_len // min(128, own_len)
    tile = 512 if width % 512 == 0 else width
    anywhere = pl.BlockSpec(memory_space=pl.ANY)
    near = pl.BlockSpec(memory_space=pltpu.VMEM)
    dma = pltpu.SemaphoreType.DMA
    low = lambda *shape: jax.ShapeDtypeStruct(shape, BF16)
    low_v = lambda *shape: pltpu.VMEM(shape, BF16)
    return pl.pallas_call(
        functools.partial(turn_kernel, groups, context, heads),
        in_specs=[near] * 4 + [anywhere] * 6 + [near],
        out_specs=[near] * 4 + [anywhere] * 3,
        out_shape=[
            jax.ShapeDtypeStruct((own_len, width), F32),
            low(local_len, width),
            low(local_len * context, heads * HD),
            low(chips, width // groups, context * heads * HD),
            low(chips - 1, width // chips, hidden),
            low(*down_part.shape),
            low(*out_own.shape),
        ],
        scratch_shapes=[
            low_v(*mixer.shape),
            low_v(context, local_len, heads * HD),
            low_v(*grad_up.shape),
            low_v(2, plane.shape[0], tile),
            low_v(tile, hidden),
            low_v(2, own_len, width),
            low_v(local_len, context * heads * HD),
            low_v(chips, width // groups, context * heads * HD),
            dma((2,)),
            dma((1,)),
            dma((2,)),
            dma((1,)),
            dma((3,)),
            dma((1,)),
            dma((steps,)),
            dma((steps,)),
            dma((context, 2, steps)),
            dma((context, 2, steps)),
            dma((chips,)),
            dma((chips,)),
        ],
        compiler_params=pltpu.CompilerParams(collective_id=4, has_side_effects=True, vmem_limit_bytes=60 * 1024 * 1024),
        cost_estimate=pl.CostEstimate(
            flops=local_len * width * heads * HD * context * 2, bytes_accessed=local_len * width * 20, transcendentals=0
        ),
        name="turn",
    )(
        total, middle, cotangent, gain.reshape(1, width), mixer, down_part, plane, grad_up, out_own, out_core, heads_back
    )


def back_kernel(
    groups,
    context,
    heads,
    prefix_ref,
    grads_in,
    cos,
    sin,
    qkv_in,
    attended,
    lse,
    middle,
    down_part,
    gate_part,
    up_part,
    down_in,
    out_half,
    mixer_sums,
    grad_proj,
    sums,
    pair_sums,
    layer_low,
    gate_in,
    up_in,
    out_in,
    mixer_in,
    query_back,
    pair_back,
    keys,
    values,
    grad_keys,
    grad_values,
    query_out,
    pair_out,
    sum_own,
    sum_other,
    query_send,
    query_recv,
    pair_send,
    pair_recv,
    sum_sem,
    chip_send,
    chip_recv,
    pairs_send,
    pairs_recv,
    half_send,
    half_recv,
    mixer_send,
    mixer_recv,
    half_own,
    half_other,
    pair_rows_out,
    pair_rows_in,
    rows_sem,
    pair_rows_sem,
    layer_send,
    layer_recv,
):
    full_len, query_cols = attended.shape
    local_len = full_len // context
    chips, pairs = groups // 2, context // 2
    f, c, t = lax.axis_index("fsdp"), lax.axis_index("ctx"), lax.axis_index("tp")
    next_chip = lambda a: {"fsdp": lax.rem(lax.div(f, 2) + a, chips) * 2 + lax.rem(f, 2)}
    greet(
        [{"ctx": lax.rem(c + k, context)} for k in range(1, context)]
        + [{"tp": 1 - t}]
        + [next_chip(a) for a in range(1, chips)]
    )

    p = lax.rem(c, 2)
    own_len, width = middle.shape

    later = ((gate_part, gate_in), (up_part, up_in))

    def send_chip(w, a):
        return chip_part(*later[w], chip_send.at[w], chip_recv.at[w], a, groups)

    def send_pair(w, b):
        return pair_part(sums.at[w], pair_sums.at[w], pairs_send.at[w], pairs_recv.at[w], b, context)

    def add_part(w, part, chip_in):
        add_chips(part, chip_in, sums.at[w], sum_own, sum_other, sum_sem, groups, context)
        for b in range(1, pairs):
            send_pair(w, b).start()

    def send_mixer(a):
        to = lax.rem(lax.div(f, 2) + a, chips)
        return remote(mixer_sums.at[to], mixer_in.at[a - 1], mixer_send.at[a], mixer_recv.at[a], next_chip(a))

    def send_half(p):
        return remote(out_half.at[p * 2 + 1 - t], out_in.at[p], half_send.at[p], half_recv.at[p], {"tp": 1 - t})

    for a in range(1, chips):
        send_chip(0, a).start()
    for at in range(2):
        send_half(at).start()
    add_part(0, down_part, down_in)

    rows, block = attention_sizes(full_len)
    load_keys(qkv_in, query_cols, cos, sin, keys, values, rows)
    grad_keys[...] = jnp.zeros_like(grad_keys)
    grad_values[...] = jnp.zeros_like(grad_values)
    stacked = heads * rows
    prefix = prefix_ref[0]

    def attend_block(i):
        here = pl.ds(pl.multiple_of(i * rows, rows), rows)
        cos_here, sin_here = cos[here, :], sin[here, :]
        queries = stack_rotated(qkv_in, here, heads, cos_here, sin_here)
        grads = stack_heads(grads_in, here, heads)
        outs = stack_heads(attended, here, heads)
        row_dot = lax.dot_general(
            jnp.ones((8, HD), F32),
            grads.astype(F32) * outs.astype(F32),
            (((1,), (1,)), ((), ())),
            precision=lax.Precision.HIGHEST,
            preferred_element_type=F32,
        )[:1]
        log_sum = lse[i][:1]
        clear, needed = key_blocks(i, rows, block, full_len)

        def key_step(j, grad_queries, masked):
            there = pl.ds(pl.multiple_of(j * block, block), block)
            key_part = keys[there, :]
            probs = jnp.exp2(dot_nt(key_part, queries) * SCALE_LOG2 - log_sum)
            if masked:
                key_pos = j * block + lax.broadcasted_iota(jnp.int32, (block, stacked), 0)
                query_pos = i * rows + lax.rem(lax.broadcasted_iota(jnp.int32, (1, stacked), 1), rows)
                probs = jnp.where(key_pos < jnp.maximum(query_pos + 1, prefix), probs, 0.0)
            grad_probs = dot_nt(values[there, :], grads)
            grad_scores = (probs * (grad_probs - row_dot)).astype(BF16)
            grad_values[there, :] += dot(probs.astype(BF16), grads)
            grad_keys[there, :] += dot(grad_scores, queries)
            return grad_queries + dot_tn(grad_scores, key_part)

        grad_queries = jnp.zeros((stacked, HD), F32)
        grad_queries = lax.fori_loop(0, clear, functools.partial(key_step, masked=False), grad_queries)
        grad_queries = lax.fori_loop(clear, needed, functools.partial(key_step, masked=True), grad_queries)
        for h in range(heads):
            part = grad_queries[h * rows : (h + 1) * rows] * SCALE
            query_out[here, h * HD : (h + 1) * HD] = rotate_back(part, cos_here, sin_here).astype(BF16)

    per_ctx = local_len // rows

    def load_half(at):
        return [
            pltpu.make_async_copy(out_half.at[at * 2 + t], half_own, rows_sem.at[0]),
            pltpu.make_async_copy(out_in.at[at], half_other, rows_sem.at[1]),
        ]

    send_rows = remote(pair_rows_out, pair_rows_in, pair_rows_sem.at[0], pair_rows_sem.at[1], {"ctx": c + 1 - 2 * p})

    def pass_half():
        for at in range(2):
            send_half(at).wait()
        for copy in load_half(1 - p):
            copy.start()
        for copy in load_half(1 - p):
            copy.wait()
        pair_rows_out[...] = (half_own[...].astype(F32) + half_other[...].astype(F32)).astype(BF16)
        send_rows.start()
        for copy in load_half(p):
            copy.start()

    part_len = min(128, own_len)
    parts_of_rows = own_len // part_len

    def send_layer(half, i):
        at = pl.ds(pl.multiple_of(half * own_len + i * part_len, part_len), part_len)
        return remote(layer_low.at[at], layer_low.at[at], layer_send.at[i], layer_recv.at[i], {"tp": 1 - t})

    def layer_rows(i, carry):
        at = pl.ds(pl.multiple_of(i * part_len, part_len), part_len)
        made = middle[at, :] + (half_own[at, :].astype(F32) + half_other[at, :].astype(F32) + pair_rows_in[at, :].astype(F32))
        layer_low[pl.ds(pl.multiple_of(t * own_len + i * part_len, part_len), part_len), :] = made.astype(BF16)
        send_layer(t, i).start()
        return carry

    def send_query(at, source):
        return remote(
            query_out.at[ctx_rows(at, local_len)], query_back.at[source], query_send.at[at], query_recv.at[source], {"ctx": at}
        )

    def send_pair_grads(at, source):
        return remote(
            pair_out.at[ctx_rows(at, local_len)], pair_back.at[source], pair_send.at[at], pair_recv.at[source], {"ctx": at}
        )

    def finish_pair(at, carry):
        def body(i, inner):
            at_rows = pl.ds(pl.multiple_of(at * local_len + i * rows, rows), rows)
            part = grad_keys[at_rows, :] * SCALE
            pair_out[at_rows, :HD] = rotate_back(part, cos[at_rows, :], sin[at_rows, :]).astype(BF16)
            pair_out[at_rows, HD:] = grad_values[at_rows, :].astype(BF16)
            return inner

        lax.fori_loop(0, per_ctx, body, 0)

        @pl.when(at != c)
        def _():
            send_pair_grads(at, c).start()

        @pl.when(at == c)
        def _():
            pair_back[c] = pair_out[ctx_rows(c, local_len), :]

        return carry

    def attend_rows(order, carry):
        at = context - 1 - order

        def body(i, inner):
            attend_block(at * per_ctx + per_ctx - 1 - i)
            return inner

        lax.fori_loop(0, per_ctx, body, 0)

        @pl.when(at != c)
        def _():
            send_query(at, c).start()

        @pl.when(at == c)
        def _():
            query_back[c] = query_out[ctx_rows(c, local_len), :]

        @pl.when(order == context // 2 - 1)
        def _():
            for a in range(1, chips):
                send_chip(0, a).wait()
                send_chip(1, a).start()
                send_mixer(a).start()
            add_part(1, gate_part, gate_in)

        @pl.when(order == context // 2)
        def _():
            pass_half()

        @pl.when(order == context // 2 - 1)
        def _():
            lax.fori_loop(context // 2, context, finish_pair, 0)

        return carry

    lax.fori_loop(0, context, attend_rows, 0)
    lax.fori_loop(0, context // 2, finish_pair, 0)
    for copy in load_half(p):
        copy.wait()
    send_rows.wait()
    lax.fori_loop(0, parts_of_rows, layer_rows, 0)

    def collect(at, carry):
        @pl.when(at != c)
        def _():
            send_query(at, at).wait()
            send_pair_grads(at, at).wait()

        return carry

    lax.fori_loop(0, context, collect, 0)

    kv_heads = (grad_proj.shape[1] // HD - heads * context) // 2
    copies = context // kv_heads
    key_at = context * query_cols
    value_at = key_at + kv_heads * HD
    for at in range(context):
        grad_proj[:, at * query_cols : (at + 1) * query_cols] = query_back[at]
    for head in range(kv_heads):
        pair = sum(pair_back[head * copies + i].astype(F32) for i in range(copies)).astype(BF16)
        grad_proj[:, key_at + head * HD : key_at + (head + 1) * HD] = pair[:, :HD]
        grad_proj[:, value_at + head * HD : value_at + (head + 1) * HD] = pair[:, HD:]

    for a in range(1, chips):
        send_mixer(a).wait()
        send_chip(1, a).wait()
    for i in range(parts_of_rows):
        send_layer(t, i).wait_send()
        send_layer(1 - t, i).wait_recv()
    for w in range(2):
        for b in range(1, pairs):
            send_pair(w, b).wait()


def back(
    groups, context, kv_heads, prefix, grads_in, cos, sin, qkv_in, attended, lse, middle, down_part, gate_part, up_part, down_in, out_half, mixer_sums
):
    full_len, query_cols = attended.shape
    local_len = full_len // context
    heads = query_cols // HD
    width, hidden = up_part.shape
    own_len = middle.shape[0]
    steps = own_len // min(128, own_len)
    chips, pairs = groups // 2, context // 2
    unit = width // (chips * context)
    anywhere = pl.BlockSpec(memory_space=pl.ANY)
    near = pl.BlockSpec(memory_space=pltpu.VMEM)
    dma = pltpu.SemaphoreType.DMA
    low = lambda *shape: jax.ShapeDtypeStruct(shape, BF16)
    low_v = lambda *shape: pltpu.VMEM(shape, BF16)
    return pl.pallas_call(
        functools.partial(back_kernel, groups, context, heads),
        in_specs=[pl.BlockSpec(memory_space=pltpu.SMEM)] + [near] * 7 + [anywhere] * 6,
        out_specs=[near] * 4 + [anywhere] * 4,
        out_shape=[
            low(local_len, context * query_cols + 2 * kv_heads * HD),
            low(2, pairs, 2, unit, hidden),
            low(2, pairs - 1, 2, unit, hidden),
            low(2 * own_len, width),
            low(chips - 1, width // chips, hidden),
            low(chips - 1, width // chips, hidden),
            low(2, *out_half.shape[1:]),
            low(chips - 1, *mixer_sums.shape[1:]),
        ],
        scratch_shapes=[
            low_v(context, local_len, query_cols),
            low_v(context, local_len, 2 * HD),
            low_v(full_len, HD),
            low_v(full_len, HD),
            pltpu.VMEM((full_len, HD), F32),
            pltpu.VMEM((full_len, HD), F32),
            low_v(full_len, query_cols),
            low_v(full_len, 2 * HD),
            low_v(2, unit, hidden),
            low_v(2, chips - 1, unit, hidden),
        ]
        + [dma((context,))] * 4
        + [
            dma((chips, 2)),
            dma((2, chips)),
            dma((2, chips)),
            dma((2, pairs)),
            dma((2, pairs)),
            dma((2,)),
            dma((2,)),
            dma((chips,)),
            dma((chips,)),
            low_v(own_len, width),
            low_v(own_len, width),
            low_v(own_len, width),
            low_v(own_len, width),
            dma((2,)),
            dma((2,)),
            dma((steps,)),
            dma((steps,)),
        ],
        compiler_params=pltpu.CompilerParams(collective_id=5, has_side_effects=True, vmem_limit_bytes=60 * 1024 * 1024),
        cost_estimate=pl.CostEstimate(
            flops=heads * full_len * full_len * HD * 20, bytes_accessed=full_len * width * 8, transcendentals=heads * full_len * full_len // 2
        ),
        name="back",
    )(prefix, grads_in, cos, sin, qkv_in, attended, lse, middle, down_part, gate_part, up_part, down_in, out_half, mixer_sums)


def finish_kernel(
    groups,
    context,
    grad_proj,
    normed,
    inputs,
    own_middle,
    gain,
    ff_sums,
    ff_pairs,
    up_part,
    up_in,
    mixer_sums,
    mixer_in,
    query_hbm,
    key_hbm,
    value_hbm,
    input_low,
    proj_grad,
    mixer_grad,
    units,
    query_in,
    kv_in,
    query_w,
    key_w,
    value_w,
    branch_out,
    branch_in,
    own_part,
    query_part,
    kv_part,
    query_sums,
    kv_sums,
    query_own,
    kv_own,
    query_next,
    kv_next,
    query_z,
    kv_z,
    mixer_rows,
    mixer_own,
    mixer_next,
    mixer_z,
    up_sums,
    up_pairs,
    pairs_send,
    pairs_recv,
    unit_own,
    unit_other,
    core_out,
    slices,
    weight_sem,
    branch_send,
    branch_recv,
    input_send,
    input_recv,
    core_sem,
    proj_sem,
    proj_send,
    proj_recv,
    next_send,
    next_recv,
    z_send,
    z_recv,
    mixer_sem,
    unit_sem,
    core_send,
    core_recv,
    unit_send,
    unit_recv,
    keep_sem,
):
    own_len, width = own_middle.shape
    shard = width // groups
    piece = units.shape[2]
    pairs, chips = context // 2, groups // 2
    f, c, t = lax.axis_index("fsdp"), lax.axis_index("ctx"), lax.axis_index("tp")
    core, p, j, y = lax.rem(f, 2), lax.rem(c, 2), lax.div(c, 2), lax.div(f, 2)
    other_half, mate, next_z = {"tp": 1 - t}, {"fsdp": f + 1 - 2 * core}, {"ctx": c + 1 - 2 * p}
    next_ctx = lambda k: lax.rem(c + k, context)
    next_y = lambda a: lax.rem(y + a, chips)
    greet(
        [other_half, mate]
        + [{"ctx": next_ctx(k)} for k in range(1, context)]
        + [{"fsdp": next_y(a) * 2 + core} for a in range(1, chips)]
    )

    def load_weights(g):
        slot = g % 2
        return [
            pltpu.make_async_copy(hbm.at[g], near.at[slot], weight_sem.at[i, slot])
            for i, (hbm, near) in enumerate(((query_hbm, query_w), (key_hbm, key_w), (value_hbm, value_w)))
        ]

    def mixer_loads(a):
        source = mixer_sums.at[y] if a == 0 else mixer_in.at[a - 1]
        return pltpu.make_async_copy(source, mixer_rows.at[a], mixer_sem.at[a])

    for copy in load_weights(0):
        copy.start()
    for a in range(chips):
        mixer_loads(a).start()

    query_cols, key_cols = query_w.shape[2], key_w.shape[2]
    columns = (grad_proj.at[:, :query_cols], grad_proj.at[:, query_cols:])
    parts, proj_sums, proj_in = (query_part, kv_part), (query_sums, kv_sums), (query_in, kv_in)

    def send_core(n):
        return remote(parts[n], proj_sums[n], core_sem.at[n, 0], core_sem.at[n, 1], mate)

    for n in range(2):
        token_product(normed, columns[n], 1 - core, parts[n], groups)
        send_core(n).start()

    own_rows = (query_own, kv_own, mixer_own)
    next_rows = (query_next, kv_next, mixer_next)
    z_rows = (query_z, kv_z, mixer_z)

    def send_next(n):
        return remote(own_rows[n].at[1 - p], next_rows[n], next_send.at[n], next_recv.at[n], next_z)

    def send_z(n, b):
        to = lax.rem(j + b, pairs)
        return remote(own_rows[n].at[p, to], z_rows[n].at[b - 1], z_send.at[n, b], z_recv.at[n, b], {"ctx": to * 2 + p})

    def add_y(n, first, others):
        for at in range(context):
            total = first[at * piece : (at + 1) * piece].astype(F32)
            for other in others:
                total = total + other[at * piece : (at + 1) * piece].astype(F32)
            own_rows[n][at % 2, at // 2] = total.astype(BF16)
        send_next(n).start()

    def add_next(n):
        send_next(n).wait()
        for at in range(pairs):
            own_rows[n][p, at] = (own_rows[n][p, at].astype(F32) + next_rows[n][at].astype(F32)).astype(BF16)
        for b in range(1, pairs):
            send_z(n, b).start()

    def whole(n):
        total = own_rows[n][p, j].astype(F32)
        for b in range(1, pairs):
            send_z(n, b).wait()
            total = total + z_rows[n][b - 1].astype(F32)
        return total

    for a in range(chips):
        mixer_loads(a).wait()
    add_y(2, mixer_rows.at[0], [mixer_rows.at[a] for a in range(1, chips)])

    def send_branch(g):
        return remote(branch_out.at[g], branch_in.at[g], branch_send.at[g], branch_recv.at[g], other_half)

    def back_rows(half, slot):
        rows = half_rows(half, own_len)
        return (
            dot_nt(grad_proj[rows, :query_cols], query_w[slot])
            + dot_nt(grad_proj[rows, query_cols : query_cols + key_cols], key_w[slot])
            + dot_nt(grad_proj[rows, query_cols + key_cols :], value_w[slot])
        )

    for g in range(groups):
        for copy in load_weights(g):
            copy.wait()
        if g + 1 < groups:
            for copy in load_weights(g + 1):
                copy.start()
        branch_out[g] = back_rows(1 - t, g % 2).astype(BF16)
        send_branch(g).start()
        own_part[:, g * shard : (g + 1) * shard] = back_rows(t, g % 2)

    def send_proj(n, a):
        return remote(
            proj_sums[n].at[next_y(a)],
            proj_in[n].at[a - 1],
            proj_send.at[n, a],
            proj_recv.at[n, a],
            {"fsdp": next_y(a) * 2 + core},
        )

    for n in range(2):
        send_core(n).wait()
        token_product(normed, columns[n], core, parts[n], groups)
        for at in range(chips):
            add_rows(parts[n].at[at], proj_sums[n].at[at], proj_sums[n].at[at])
        for a in range(1, chips):
            send_proj(n, a).start()
    add_next(2)

    send_pair = lambda b: pair_part(up_sums, up_pairs, pairs_send, pairs_recv, b, context)
    add_chips(up_part, up_in, up_sums, unit_own, unit_other, unit_sem, groups, context)
    for b in range(1, pairs):
        send_pair(b).start()
    summed = ((ff_sums.at[0], ff_pairs.at[0]), (ff_sums.at[1], ff_pairs.at[1]), (up_sums, up_pairs))

    def send_unit_core(w):
        return remote(core_out.at[w], slices.at[w, core], core_send.at[w], core_recv.at[w], mate)

    def send_unit(w, s):
        return remote(slices.at[w, s, 1 - p], units.at[w, s * 2 + p], unit_send.at[w, s], unit_recv.at[w, s], next_z)

    def keep_unit(w, s):
        return pltpu.make_async_copy(slices.at[w, s, p], units.at[w, s * 2 + p], keep_sem.at[w, s])

    def to_core(w):
        own, others = summed[w]

        def load(kept):
            at_core = core if kept == 0 else 1 - core
            copies = [pltpu.make_async_copy(own.at[j, at_core], unit_own.at[kept], unit_sem.at[0, kept])]
            for b in range(1, pairs):
                copies.append(
                    pltpu.make_async_copy(others.at[b - 1, at_core], unit_other.at[kept, b - 1], unit_sem.at[b, kept])
                )
            return copies

        if w < 2:
            for copy in load(0) + load(1):
                copy.start()
            for copy in load(0) + load(1):
                copy.wait()
        for kept in range(2):
            at_core = core if kept == 0 else 1 - core
            total = (unit_own[kept] if w < 2 else own[j, at_core]).astype(F32)
            for b in range(1, pairs):
                total = total + (unit_other[kept, b - 1] if w < 2 else others[b - 1, at_core]).astype(F32)
            total = total.astype(BF16)
            for at in range(2):
                if kept == 0:
                    slices[w, core, at] = total[at * piece : (at + 1) * piece]
                else:
                    core_out[w, at] = total[at * piece : (at + 1) * piece]
        send_unit_core(w).start()
    def to_owner(w):
        send_unit_core(w).wait_recv()
        for s in range(2):
            send_unit(w, s).start()
            keep_unit(w, s).start()

    for w in range(2):
        to_core(w)
    for w in range(2):
        to_owner(w)

    def proj_load(n, a):
        return pltpu.make_async_copy(proj_in[n].at[a - 1], parts[n].at[a - 1], proj_sem.at[n, a])

    def from_y(n):
        for a in range(1, chips):
            send_proj(n, a).wait_recv()
            proj_load(n, a).start()
        for a in range(1, chips):
            proj_load(n, a).wait()
        add_y(n, proj_sums[n].at[y], [parts[n].at[a - 1] for a in range(1, chips)])

    step = min(128, own_len)
    steps = own_len // step

    def send_low(half, i):
        rows = pl.ds(pl.multiple_of(half * own_len + i * step, step), step)
        return remote(input_low.at[rows], input_low.at[rows], input_send.at[i], input_recv.at[i], other_half)

    for g in range(groups):
        send_branch(g).wait_recv()

    def norm_back(i, carry):
        at = pl.ds(pl.multiple_of(i * step, step), step)
        grad = jnp.concatenate(
            [own_part[at, g * shard : (g + 1) * shard] + branch_in[g, at, :].astype(F32) for g in range(groups)], axis=1
        )
        part = inputs[at, :].astype(F32)
        inner = grad * gain[...]
        mixed = jnp.mean(inner * part, axis=-1, keepdims=True)
        scale = lax.rsqrt(jnp.mean(part * part, axis=-1, keepdims=True) + EPS)
        made = own_middle[at, :] + scale * inner - part * (scale * scale * scale * mixed)
        input_low[pl.ds(pl.multiple_of(t * own_len + i * step, step), step), :] = made.astype(BF16)
        send_low(t, i).start()
        return carry

    lax.fori_loop(0, steps, norm_back, 0)

    from_y(0)
    for b in range(1, pairs):
        send_pair(b).wait()
    to_core(2)
    add_next(0)
    to_owner(2)
    mixer_grad[...] = whole(2)
    from_y(1)
    add_next(1)
    proj_grad[:, :query_cols] = whole(0)
    proj_grad[:, query_cols:] = whole(1)

    for g in range(groups):
        send_branch(g).wait_send()
    for n in range(2):
        for a in range(1, chips):
            send_proj(n, a).wait_send()
    for w in range(3):
        send_unit_core(w).wait_send()
        for s in range(2):
            send_unit(w, s).wait()
            keep_unit(w, s).wait()
    for i in range(steps):
        send_low(t, i).wait_send()
        send_low(1 - t, i).wait_recv()


def finish(
    groups,
    context,
    grad_proj,
    normed,
    inputs,
    own_middle,
    gain,
    ff_sums,
    ff_pairs,
    up_part,
    up_in,
    mixer_sums,
    mixer_in,
    query_full,
    key_full,
    value_full,
):
    own_len, width = own_middle.shape
    chips, pairs = groups // 2, context // 2
    unit, hidden = ff_sums.shape[3:]
    piece = unit // 2
    steps = own_len // min(128, own_len)
    proj_cols, mixer_cols, query_cols = grad_proj.shape[1], mixer_sums.shape[2], query_full.shape[2]
    column_counts = (query_cols, proj_cols - query_cols)
    core_rows = width // groups
    anywhere = pl.BlockSpec(memory_space=pl.ANY)
    near = pl.BlockSpec(memory_space=pltpu.VMEM)
    dma = pltpu.SemaphoreType.DMA
    low = lambda *shape: jax.ShapeDtypeStruct(shape, BF16)
    low_v = lambda *shape: pltpu.VMEM(shape, BF16)
    return pl.pallas_call(
        functools.partial(finish_kernel, groups, context),
        in_specs=[near] * 5 + [anywhere] * 9,
        out_specs=[near] * 3 + [anywhere] * 3,
        out_shape=[
            low(2 * own_len, width),
            jax.ShapeDtypeStruct((piece, proj_cols), F32),
            jax.ShapeDtypeStruct((piece, mixer_cols), F32),
            low(3, 4, piece, hidden),
        ]
        + [low(chips - 1, core_rows, columns) for columns in column_counts],
        scratch_shapes=[low_v(2, *w.shape[1:]) for w in (query_full, key_full, value_full)]
        + [
            low_v(groups, own_len, width // groups),
            low_v(groups, own_len, width // groups),
            pltpu.VMEM((own_len, width), F32),
        ]
        + [low_v(chips, core_rows, columns) for columns in column_counts] * 2
        + [low_v(2, pairs, piece, columns) for columns in column_counts]
        + [low_v(pairs, piece, columns) for columns in column_counts]
        + [low_v(pairs - 1, piece, columns) for columns in column_counts]
        + [
            low_v(chips, core_rows, mixer_cols),
            low_v(2, pairs, piece, mixer_cols),
            low_v(pairs, piece, mixer_cols),
            low_v(pairs - 1, piece, mixer_cols),
            low_v(pairs, 2, unit, hidden),
            low_v(pairs - 1, 2, unit, hidden),
            dma((pairs,)),
            dma((pairs,)),
            low_v(2, unit, hidden),
            low_v(2, max(pairs, chips) - 1, unit, hidden),
            low_v(3, 2, piece, hidden),
            low_v(3, 2, 2, piece, hidden),
            dma((3, 2)),
            dma((groups,)),
            dma((groups,)),
            dma((steps,)),
            dma((steps,)),
            dma((2, 2)),
            dma((2, chips)),
            dma((2, chips)),
            dma((2, chips)),
            dma((3,)),
            dma((3,)),
            dma((3, pairs)),
            dma((3, pairs)),
            dma((chips,)),
            dma((max(pairs, chips), 2)),
            dma((3,)),
            dma((3,)),
            dma((3, 2)),
            dma((3, 2)),
            dma((3, 2)),
        ],
        compiler_params=pltpu.CompilerParams(collective_id=6, has_side_effects=True, vmem_limit_bytes=62 * 1024 * 1024),
        cost_estimate=pl.CostEstimate(
            flops=own_len * width * grad_proj.shape[1] * 8, bytes_accessed=own_len * width * 40, transcendentals=0
        ),
        name="finish",
    )(
        grad_proj,
        normed,
        inputs,
        own_middle,
        gain.reshape(1, width),
        ff_sums,
        ff_pairs,
        up_part,
        up_in,
        mixer_sums,
        mixer_in,
        query_full,
        key_full,
        value_full,
    )


def tie(*values):
    return lax.optimization_barrier(values)


def on_device(
    tokens, prefix, attn_gain, w_query, w_key, w_value, w_out, mlp_gain, w_gate, w_up, w_down, cotangent
):
    _, local_len, width = tokens.shape
    groups, context, halves = lax.axis_size("fsdp"), lax.axis_size("ctx"), lax.axis_size("tp")
    own_len = local_len // halves
    full_len = local_len * context
    query_cols = w_query.shape[1]
    kv_heads = w_key.shape[1] // HD
    copies = context // kv_heads
    heads = query_cols // HD // context
    group_cols = (heads + 2) * HD
    hidden_cols = w_gate.shape[1] // 4
    own_start = lax.axis_index("tp") * own_len
    own = lambda values: lax.dynamic_slice_in_dim(values, own_start, own_len, 0)

    cos, sin = rope_tables(full_len)
    inputs_all = tokens.reshape(local_len, width)
    grad_out = cotangent.reshape(local_len, width)

    (
        normed_one,
        qkv_in,
        attended,
        lse,
        heads_back,
        middle,
        normed_two,
        query_full,
        key_full,
        value_full,
        mixer_blocks,
        gate_cols,
        up_cols,
        down_blocks,
        grad_plane,
    ) = front(
        groups,
        context,
        prefix,
        inputs_all,
        attn_gain,
        mlp_gain,
        cos,
        sin,
        w_query,
        w_key,
        w_value,
        w_out,
        w_gate,
        w_up,
        w_down,
        grad_out,
    )

    plane, _, _, grad_up, down_part, gate_part, out_own, out_core, grad_normed_two = mlp(
        groups, normed_two, grad_plane, gate_cols, up_cols, down_blocks
    )
    piece = width // (groups * context)
    own_middle, _, grads_in, mixer_sums, down_in, up_part, out_half = turn(
        groups,
        context,
        heads,
        grad_normed_two,
        middle,
        grad_out,
        mlp_gain,
        mixer_blocks,
        down_part,
        plane,
        grad_up,
        out_own,
        out_core,
        heads_back,
    )
    grad_proj, sums, pair_sums, layer_low, _, up_in, _, mixer_in = back(
        groups,
        context,
        kv_heads,
        prefix,
        grads_in,
        cos,
        sin,
        qkv_in,
        attended,
        lse,
        middle,
        down_part,
        gate_part,
        up_part,
        down_in,
        out_half,
        mixer_sums,
    )
    input_low, qkv_grad, mixer_rows, units, _, _ = finish(
        groups,
        context,
        grad_proj,
        normed_one,
        own(inputs_all),
        own_middle,
        attn_gain,
        sums,
        pair_sums,
        up_part,
        up_in,
        mixer_sums,
        mixer_in,
        query_full,
        key_full,
        value_full,
    )
    input_grad = input_low.astype(F32)
    layer_out = layer_low
    down_grad = jnp.swapaxes(units[0], 1, 2).reshape(4 * hidden_cols, piece).astype(F32)
    wide = lambda rows: jnp.swapaxes(rows, 0, 1).reshape(piece, 4 * hidden_cols).astype(F32)
    gate_grad, up_grad = wide(units[1]), wide(units[2])
    out_grad = jnp.transpose(mixer_rows)

    piece_start = lax.axis_index("ctx") * piece
    rows_of = lambda weight: lax.dynamic_slice_in_dim(weight, piece_start, piece, 0).astype(F32)
    kv_cols = kv_heads * HD
    query_grad = qkv_grad[:, :query_cols]
    key_grad = qkv_grad[:, query_cols : query_cols + kv_cols]
    value_grad = qkv_grad[:, query_cols + kv_cols :]
    mlp_sum = jnp.sum(rows_of(w_gate) * gate_grad + rows_of(w_up) * up_grad, axis=1)
    attn_sum = sum(
        jnp.sum(rows_of(weight) * grad, axis=1)
        for weight, grad in ((w_query, query_grad), (w_key, key_grad), (w_value, value_grad))
    )
    gain_starts = lax.axis_index("fsdp") * (piece * context) + piece_start
    gain_of = lambda gain: lax.dynamic_slice_in_dim(gain, gain_starts, piece, 0)
    sums = lax.psum(jnp.stack([mlp_sum, attn_sum]), "tp")
    mlp_gain_grad = sums[0] / gain_of(mlp_gain)
    attn_gain_grad = sums[1] / gain_of(attn_gain)

    return (
        layer_out.reshape(tokens.shape),
        input_grad.reshape(tokens.shape),
        attn_gain_grad,
        query_grad,
        key_grad,
        value_grad,
        out_grad,
        mlp_gain_grad,
        gate_grad,
        up_grad,
        down_grad,
    )


def solution(mesh):
    rows = P("fsdp", "ctx", None)
    owned = P(("fsdp", "ctx"), "tp")
    owned_t = P("tp", ("fsdp", "ctx"))
    gain = P(("fsdp", "ctx"))
    down, up = P("fsdp", "tp"), P("tp", "fsdp")
    return jax.shard_map(
        on_device,
        mesh=mesh,
        in_specs=(rows, P("fsdp"), P(), down, down, down, up, P(), down, down, up, rows),
        out_specs=(rows, rows, gain, owned, owned, owned, owned_t, gain, owned, owned, owned_t),
        check_vma=False,
    )
```
